32 devices in a mesh: member: 4 (over y, x), lat: 8 (over z, core).
Axes of the slice: x: 2, y: 2, z: 4, core: 2. Of those that a mesh axis runs over, the one named last changes fastest.
Arguments:
- fields: bfloat16 [4, 641, 16, 720], P('member', None, 'lat'), as said below
- noise_fields: bfloat16 [4, 8, 16, 720], P('member', None, 'lat'), may hold values from -5 to 5
- target_fields: bfloat16 [641, 16, 720], P(None, 'lat'), as said below
- band_heights: int32 [8], replicated, may hold values from 1 to 2
- tap_offsets: int32 [9, 16], P(None, 'lat'), may hold values from -8 to 8
- expand_weight: float32 [641, 1282], replicated, may hold values from -0.25 to 0.25
- expand_bias: float32 [1282], replicated, may hold values from -1.75 to 1.75
- reduce_weight: float32 [1282, 641], replicated, may hold values from -0.15625 to 0.15625
- channel_vectors: float32 [2, 641], replicated, as said below
- disco_filter: float32 [9, 641], replicated, may hold values from -2 to 2
- noise_mixing: float32 [8, 641], replicated, may hold values from -2 to 2
- first_expand: float32 [641, 1282], replicated, may hold values from -0.5 to 0.5
- second_expand: float32 [641, 1282], replicated, may hold values from 0.029994337 to 0.11997735
- first_bias: float32 [1282], replicated, may hold values from -0.5 to 0.5
- second_bias: float32 [1282], replicated, may hold values from 0.029994337 to 0.11997735
- first_reduce: float32 [1282, 641], replicated, may hold values from -0.5 to 0.5
- second_reduce: float32 [1282, 641], replicated, may hold values from 0.029994337 to 0.11997735
- first_vectors: float32 [2, 641], replicated, may hold values from -0.5 to 0.5
- second_vectors: float32 [2, 641], replicated, may hold values from 0.029994337 to 0.11997735
- first_filter: float32 [9, 641], replicated, may hold values from -0.5 to 0.5
- second_filter: float32 [9, 641], replicated, may hold values from 0.029994337 to 0.11997735
- first_mixing: float32 [8, 641], replicated, may hold values from -0.5 to 0.5
- second_mixing: float32 [8, 641], replicated, may hold values from 0.029994337 to 0.11997735
Outputs:
- mean_loss: float32 [], replicated
- input_gradient: bfloat16 [4, 641, 16, 720], P('member', None, 'lat')
- gradient_norm: float32 [], replicated
- expand_out: float32 [641, 1282], replicated
- expand_first: float32 [641, 1282], replicated
- expand_second: float32 [641, 1282], replicated
- bias_out: float32 [1282], replicated
- bias_first: float32 [1282], replicated
- bias_second: float32 [1282], replicated
- reduce_out: float32 [1282, 641], replicated
- reduce_first: float32 [1282, 641], replicated
- reduce_second: float32 [1282, 641], replicated
- vectors_out: float32 [2, 641], replicated
- vectors_first: float32 [2, 641], replicated
- vectors_second: float32 [2, 641], replicated
- filter_out: float32 [9, 641], replicated
- filter_first: float32 [9, 641], replicated
- filter_second: float32 [9, 641], replicated
- mixing_out: float32 [8, 641], replicated
- mixing_first: float32 [8, 641], replicated
- mixing_second: float32 [8, 641], replicated
- expand_copy: bfloat16 [641, 1282], replicated
- reduce_copy: bfloat16 [1282, 641], replicated
The draws below stay inside these ranges and needn't reach their ends.
Inputs may be any that keep to these rules, and one draw needn't show every extreme that they name: `band_heights`: each band has 1 or 2 live rows. `fields`: finite values. `target_fields`: finite values. `channel_vectors`: gains positive, biases of either sign.
All inputs are finite; a program needn't handle non-finite values.
Results may differ from the reference program's by a relative error of at most 0.0085.
Values may be sent and summed in bfloat16 or wider, within the bound.
No kernel may reach another device: no remote copies, remote signals or barrier semaphores. Data moves between devices by JAX's collectives and lax.ppermute only.
A program may use at most 384 MiB of HBM per device.

```python
import math
import jax
import jax.numpy as jnp
from jax import lax

C = 641
HID = 1282
NOISE = 8
LON = 720
ROWCAP = 2
MAXOFF = 8
STEP = 10
ENS = 4
RT = 16
N_LAT = 8


def rising(entries, highest):
    return 1.0 + (highest - 1.0) * jnp.arange(entries, dtype=jnp.float32) / (entries - 1)


def draw_fields(key, part):
    key = jax.random.fold_in(key, 7)
    array_shape = (ENS, C, ROWCAP * N_LAT, LON)
    base_values = jax.random.truncated_normal(key, -4.0, 4.0, array_shape, jnp.float32)
    member_scale = rising(ENS, 3.0)
    row_scale = rising(ROWCAP * N_LAT, 3.0)
    values = base_values * member_scale[:, None, None, None] * row_scale[None, None, :, None]
    return values.astype(jnp.bfloat16)


def draw_target_fields(key, part):
    key = jax.random.fold_in(key, 13)
    array_shape = (C, ROWCAP * N_LAT, LON)
    base_values = 0.5 * jax.random.truncated_normal(key, -4.0, 4.0, array_shape, jnp.float32)
    row_scale = rising(ROWCAP * N_LAT, 3.0)
    values = base_values * row_scale[None, :, None]
    return values.astype(jnp.bfloat16)


def draw_channel_vectors(key, part):
    key = jax.random.fold_in(key, 19)
    gain_key = jax.random.fold_in(key, 1)
    bias_key = jax.random.fold_in(key, 2)
    gains = 1.0 + 0.15 * jax.random.truncated_normal(gain_key, -3.0, 3.0, (C,), jnp.float32)
    biases = 0.3 * jax.random.truncated_normal(bias_key, -3.0, 3.0, (C,), jnp.float32)
    return jnp.stack([gains, biases]).astype(jnp.float32)


def with_ends(values, rng, smallest, largest):
    dims = values.shape
    spot = [jax.random.randint(jax.random.fold_in(rng, axis), (), 0, dims[axis]) for axis in range(len(dims))]
    values = values.at[tuple(spot)].set(smallest)
    longest = dims.index(max(dims))
    spot[longest] = (spot[longest] + 1) % dims[longest]
    return values.at[tuple(spot)].set(largest)


def block_levels(stream_key, dims, split, smallest, largest):
    factor_of = 1.0
    for position, parts in split:
        steps = jax.random.uniform(jax.random.fold_in(jax.random.fold_in(stream_key, 6), position), (parts,), jnp.float32, smallest / len(split), largest / len(split))
        factor_of = factor_of * jnp.repeat(jnp.exp(steps), dims[position] // parts).reshape((-1,) + (1,) * (len(dims) - 1 - position))
    return factor_of


def normal_values(rng, extent, scale, most, pieces=(), kind=jnp.bfloat16):
    array = jax.random.normal(rng, extent, jnp.float32) * scale
    if len(pieces) > 0:
        array = block_levels(rng, extent, pieces, -0.22, 0.18) * array
    return jnp.clip(array, min=-most, max=most).astype(kind)


def setup_inputs(seed: int = 0) -> dict:
    splits = jax.random.split(jax.random.key(seed), 24)
    fields = draw_fields(jax.random.fold_in(splits[23], 71), 0)
    noise_fields = normal_values(splits[1], (ENS, NOISE, RT, LON), 1.0, 5.0, ((0, 4), (2, 8)))
    target_fields = draw_target_fields(jax.random.fold_in(splits[23], 71), 0)
    band_heights = with_ends(jax.random.randint(splits[3], (N_LAT,), ROWCAP - 1, ROWCAP + 1), jax.random.fold_in(splits[3], 1), ROWCAP - 1, ROWCAP).astype(jnp.int32)
    tap_offsets = with_ends(jax.random.randint(splits[4], (9, RT), 0 - MAXOFF, MAXOFF + 1), jax.random.fold_in(splits[4], 1), 0 - MAXOFF, MAXOFF).astype(jnp.int32)
    expand_weight = normal_values(splits[5], (C, HID), C ** -0.5, 0.25, (), jnp.float32)
    expand_bias = normal_values(splits[6], (HID,), 0.3, 1.75, (), jnp.float32)
    reduce_weight = normal_values(splits[7], (HID, C), HID ** -0.5, 0.15625, (), jnp.float32)
    channel_vectors = draw_channel_vectors(jax.random.fold_in(splits[23], 71), 0)
    disco_filter = normal_values(splits[9], (9, C), 0.33, 2.0, (), jnp.float32)
    noise_mixing = normal_values(splits[10], (NOISE, C), NOISE ** -0.5, 2.0, (), jnp.float32)
    first_expand = normal_values(splits[11], (C, HID), (0.00222 * (HID * C * N_LAT * ROWCAP * LON) ** 0.5 * ENS ** -0.5 * (2 * C * HID + HID + 19 * C) ** -0.5), 0.5, (), jnp.float32)
    second_expand = jnp.clip(jnp.exp(jax.random.uniform(splits[12], (C, HID), jnp.float32, math.log(0.029994337), math.log(0.11997735))), 0.029994337, 0.11997735)
    first_bias = normal_values(splits[13], (HID,), (0.00222 * (HID * C * N_LAT * ROWCAP * LON) ** 0.5 * ENS ** -0.5 * (2 * C * HID + HID + 19 * C) ** -0.5), 0.5, (), jnp.float32)
    second_bias = jnp.clip(jnp.exp(jax.random.uniform(splits[14], (HID,), jnp.float32, math.log(0.029994337), math.log(0.11997735))), 0.029994337, 0.11997735)
    first_reduce = normal_values(splits[15], (HID, C), (0.00222 * (HID * C * N_LAT * ROWCAP * LON) ** 0.5 * ENS ** -0.5 * (2 * C * HID + HID + 19 * C) ** -0.5), 0.5, (), jnp.float32)
    second_reduce = jnp.clip(jnp.exp(jax.random.uniform(splits[16], (HID, C), jnp.float32, math.log(0.029994337), math.log(0.11997735))), 0.029994337, 0.11997735)
    first_vectors = normal_values(splits[17], (2, C), (0.00222 * (HID * C * N_LAT * ROWCAP * LON) ** 0.5 * ENS ** -0.5 * (2 * C * HID + HID + 19 * C) ** -0.5), 0.5, (), jnp.float32)
    second_vectors = jnp.clip(jnp.exp(jax.random.uniform(splits[18], (2, C), jnp.float32, math.log(0.029994337), math.log(0.11997735))), 0.029994337, 0.11997735)
    first_filter = normal_values(splits[19], (9, C), (0.00222 * (HID * C * N_LAT * ROWCAP * LON) ** 0.5 * ENS ** -0.5 * (2 * C * HID + HID + 19 * C) ** -0.5), 0.5, (), jnp.float32)
    second_filter = jnp.clip(jnp.exp(jax.random.uniform(splits[20], (9, C), jnp.float32, math.log(0.029994337), math.log(0.11997735))), 0.029994337, 0.11997735)
    first_mixing = normal_values(splits[21], (NOISE, C), (0.00222 * (HID * C * N_LAT * ROWCAP * LON) ** 0.5 * ENS ** -0.5 * (2 * C * HID + HID + 19 * C) ** -0.5), 0.5, (), jnp.float32)
    second_mixing = jnp.clip(jnp.exp(jax.random.uniform(splits[22], (NOISE, C), jnp.float32, math.log(0.029994337), math.log(0.11997735))), 0.029994337, 0.11997735)
    return {"fields": fields, "noise_fields": noise_fields, "target_fields": target_fields, "band_heights": band_heights, "tap_offsets": tap_offsets, "expand_weight": expand_weight, "expand_bias": expand_bias, "reduce_weight": reduce_weight, "channel_vectors": channel_vectors, "disco_filter": disco_filter, "noise_mixing": noise_mixing, "first_expand": first_expand, "second_expand": second_expand, "first_bias": first_bias, "second_bias": second_bias, "first_reduce": first_reduce, "second_reduce": second_reduce, "first_vectors": first_vectors, "second_vectors": second_vectors, "first_filter": first_filter, "second_filter": second_filter, "first_mixing": first_mixing, "second_mixing": second_mixing}


@jax.custom_vjp
def low(v):
    return lax.optimization_barrier(v.astype(jnp.bfloat16)).astype(jnp.float32)

@jax.custom_vjp
def low_back(v):
    return v

def low_keep(v):
    return (low(v), None)

def low_pass(kept, grad):
    return (grad,)

def back_keep(v):
    return (v, None)

def back_low(kept, grad):
    return (low(grad),)
low.defvjp(low_keep, low_pass)
low_back.defvjp(back_keep, back_low)
BETA_ONE = 0.9
BETA_TWO = 0.95
ADAM_EPS = 1e-08
DECAY_RATE = 0.1
NORM_EPS = 1e-05
SMALL_RATE = 0.3
HIGHEST = lax.Precision.HIGHEST

def smooth_abs(values):
    return jnp.sqrt(values * values + 1.0)

def layer_norm(values, norm_gain):
    gain_shape = (1, -1) + (1,) * (values.ndim - 2)
    centre = lax.optimization_barrier(jnp.mean(values, axis=1, keepdims=True))
    centred = values - centre
    spread = lax.optimization_barrier(jnp.mean(centred * centred, axis=1, keepdims=True))
    return centred * lax.rsqrt(spread + NORM_EPS) * norm_gain.reshape(gain_shape)

def disco(source, prev_row, next_row, heights, offsets, weights):
    row_count = source.shape[3]
    lon_count = source.shape[4]
    row_ids = jnp.arange(row_count, dtype=jnp.int32)
    live_rows = (row_ids[None, :] < heights[:, None]).astype(jnp.float32)[None, None, :, :, None]
    last_row = (row_ids[None, :] == heights[:, None] - 1)[None, None, :, :, None]
    upper_rows = jnp.concatenate([prev_row[:, :, :, None, :], source[:, :, :, :-1, :]], axis=3) * live_rows
    shifted = jnp.concatenate([source[:, :, :, 1:, :], jnp.zeros_like(source[:, :, :, :1, :])], axis=3)
    lower_rows = jnp.where(last_row, next_row[:, :, :, None, :], shifted) * live_rows
    lon_ids = jnp.arange(lon_count, dtype=jnp.int32)
    result = jnp.zeros_like(source)
    for lat_tap, anchor in enumerate((upper_rows, source, lower_rows)):
        for lon_tap in range(3):
            tap_index = 3 * lat_tap + lon_tap
            where_from = (lon_ids[None, None, :] + offsets[tap_index][:, :, None]) % lon_count
            where_from = jnp.broadcast_to(where_from[None, None], anchor.shape)
            gathered = jnp.take_along_axis(anchor, where_from, axis=4)
            result = result + weights[tap_index][None, :, None, None, None] * gathered
    return result

def block_total(block_items, low_expand, expand_bias, low_reduce, channel_vectors, disco_filter, noise_mixing):
    block_fields, prev_rows, next_rows, block_heights, block_offsets, block_noise, block_target = block_items
    normed = low(layer_norm(block_fields, channel_vectors[0]))
    filtered = disco(normed, prev_rows, next_rows, block_heights, block_offsets, disco_filter)
    mixed_low = low(filtered + jnp.einsum('kc,ekgrl->ecgrl', noise_mixing, block_noise, precision=HIGHEST))
    column = (1, -1, 1, 1, 1)
    pre_act = low_back(jnp.einsum('ch,ecgrl->ehgrl', low_expand, mixed_low, precision=HIGHEST) + expand_bias.reshape(column))
    activation = low(jax.nn.gelu(pre_act, approximate=False))
    branch = low_back(jnp.einsum('hc,ehgrl->ecgrl', low_reduce, activation, precision=HIGHEST) + channel_vectors[1].reshape(column))
    predicted = block_fields + branch
    ensemble = predicted.shape[0]
    row_ids = jnp.arange(predicted.shape[3], dtype=jnp.int32)
    live_rows = (row_ids[None, :] < block_heights[:, None]).astype(jnp.float32)[None, :, :, None]
    own_term = lax.optimization_barrier(jnp.sum(smooth_abs(predicted - block_target[None]), axis=0))
    pair_term = jnp.zeros_like(own_term)
    for member in range(ensemble):
        pair_term = pair_term + lax.optimization_barrier(jnp.sum(smooth_abs(predicted - predicted[member:member + 1]), axis=0))
    crps_terms = own_term / ensemble - pair_term / (2.0 * ensemble * ensemble)
    return jnp.sum(crps_terms * live_rows)

def objective(fields_in, expand_in, bias_in, reduce_in, vectors_in, filter_in, mixing_in, band_heights, tap_offsets, noise32, target32):
    ensemble, channels, total_rows, lon_count = fields_in.shape
    band_count = band_heights.shape[0]
    row_cap = total_rows // band_count
    group_size = 4
    groups = band_count // group_size
    banded = fields_in.reshape(ensemble, channels, band_count, row_cap, lon_count)
    top_rows = banded[:, :, :, 0, :]
    last_index = jnp.broadcast_to((band_heights - 1).reshape(1, 1, band_count, 1, 1), (ensemble, channels, band_count, 1, lon_count))
    bottom_rows = jnp.take_along_axis(banded, last_index, axis=3)[:, :, :, 0, :]
    top_normed = low(layer_norm(top_rows, vectors_in[0]))
    bottom_normed = low(layer_norm(bottom_rows, vectors_in[0]))
    zero_rows = jnp.zeros_like(top_normed[:, :, :1])
    prev_rows = jnp.concatenate([zero_rows, bottom_normed[:, :, :-1]], axis=2)
    next_rows = jnp.concatenate([top_normed[:, :, 1:], zero_rows], axis=2)
    block_items = (banded.reshape(ensemble, channels, groups, group_size, row_cap, lon_count).transpose(2, 0, 1, 3, 4, 5), prev_rows.reshape(ensemble, channels, groups, group_size, lon_count).transpose(2, 0, 1, 3, 4), next_rows.reshape(ensemble, channels, groups, group_size, lon_count).transpose(2, 0, 1, 3, 4), band_heights.reshape(groups, group_size), tap_offsets.reshape(9, groups, group_size, row_cap).transpose(1, 0, 2, 3), noise32.reshape(ensemble, -1, groups, group_size, row_cap, lon_count).transpose(2, 0, 1, 3, 4, 5), target32.reshape(channels, groups, group_size, row_cap, lon_count).transpose(1, 0, 2, 3, 4))
    low_expand = low(expand_in)
    low_reduce = low(reduce_in)

    def one_block(item):
        return block_total(item, low_expand, bias_in, low_reduce, vectors_in, filter_in, mixing_in)
    return jnp.sum(lax.map(jax.checkpoint(one_block), block_items))

def adam_step(weight, gradient, first, second, rate):
    first_new = BETA_ONE * first + (1.0 - BETA_ONE) * gradient
    second_new = BETA_TWO * second + (1.0 - BETA_TWO) * gradient * gradient
    first_hat = first_new / (1.0 - BETA_ONE ** STEP)
    second_hat = second_new / (1.0 - BETA_TWO ** STEP)
    weight_new = weight - rate * (first_hat / (jnp.sqrt(second_hat) + ADAM_EPS) + DECAY_RATE * weight)
    return (weight_new, first_new, second_new)

def reference(fields, noise_fields, target_fields, band_heights, tap_offsets, expand_weight, expand_bias, reduce_weight, channel_vectors, disco_filter, noise_mixing, first_expand, second_expand, first_bias, second_bias, first_reduce, second_reduce, first_vectors, second_vectors, first_filter, second_filter, first_mixing, second_mixing):
    fields32 = fields.astype(jnp.float32)
    noise32 = noise_fields.astype(jnp.float32)
    target32 = target_fields.astype(jnp.float32)

    def loss_of(fields_in, expand_in, bias_in, reduce_in, vectors_in, filter_in, mixing_in):
        return objective(fields_in, expand_in, bias_in, reduce_in, vectors_in, filter_in, mixing_in, band_heights, tap_offsets, noise32, target32)
    total, pull_back = jax.vjp(loss_of, fields32, expand_weight, expand_bias, reduce_weight, channel_vectors, disco_filter, noise_mixing)
    grad_fields, grad_expand, grad_bias, grad_reduce, grad_vectors, grad_filter, grad_mixing = pull_back(jnp.ones((), jnp.float32))
    live_total = jnp.sum(band_heights).astype(jnp.float32)
    mean_loss = total / (C * LON * live_total)
    squares = jnp.sum(grad_expand * grad_expand) + jnp.sum(grad_bias * grad_bias) + jnp.sum(grad_reduce * grad_reduce)
    squares = squares + jnp.sum(grad_vectors * grad_vectors) + jnp.sum(grad_filter * grad_filter) + jnp.sum(grad_mixing * grad_mixing)
    gradient_norm = jnp.sqrt(squares)
    limit = 0.02 * math.sqrt(HID * C * N_LAT * ROWCAP * LON / ENS)
    factor = jnp.minimum(1.0, limit / (gradient_norm + 1e-06))
    expand_out, expand_first, expand_second = adam_step(expand_weight, factor * grad_expand, first_expand, second_expand, C ** (-0.5))
    bias_out, bias_first, bias_second = adam_step(expand_bias, factor * grad_bias, first_bias, second_bias, SMALL_RATE)
    reduce_out, reduce_first, reduce_second = adam_step(reduce_weight, factor * grad_reduce, first_reduce, second_reduce, HID ** (-0.5))
    vectors_out, vectors_first, vectors_second = adam_step(channel_vectors, factor * grad_vectors, first_vectors, second_vectors, SMALL_RATE)
    filter_out, filter_first, filter_second = adam_step(disco_filter, factor * grad_filter, first_filter, second_filter, SMALL_RATE)
    mixing_out, mixing_first, mixing_second = adam_step(noise_mixing, factor * grad_mixing, first_mixing, second_mixing, SMALL_RATE)
    return (mean_loss, grad_fields.astype(jnp.bfloat16), gradient_norm, expand_out, expand_first, expand_second, bias_out, bias_first, bias_second, reduce_out, reduce_first, reduce_second, vectors_out, vectors_first, vectors_second, filter_out, filter_first, filter_second, mixing_out, mixing_first, mixing_second, expand_out.astype(jnp.bfloat16), reduce_out.astype(jnp.bfloat16))
```

```python
import functools
import math

import jax
import jax.numpy as jnp
from jax import lax
from jax.experimental import pallas as pl
from jax.experimental.pallas import tpu as pltpu
from jax.sharding import Mesh, PartitionSpec as P

STEP = 10
BETA_ONE = 0.9
BETA_TWO = 0.95
ADAM_EPS = 1e-08
DECAY_RATE = 0.1
NORM_EPS = 1e-05
SMALL_RATE = 0.3
REACH = 8
f32 = jnp.float32
bf16 = jnp.bfloat16

NN = (((1,), (0,)), ((), ()))
NT = (((1,), (1,)), ((), ()))
TN = (((0,), (0,)), ((), ()))


def round_up(value, step):
    return -(-value // step) * step


def mm(a, b, dims=NN):
    return lax.dot_general(a, b, dims, preferred_element_type=f32)


class Sizes:
    def __init__(self, members, channels, hidden, noise, lon):
        self.m = members
        self.c = channels
        self.h = hidden
        self.k = noise
        self.lon = lon
        self.q = lon // members
        self.pr = round_up(self.q, 8)
        self.ext = round_up(self.pr + 2 * REACH, 16)
        self.pe = 2 * self.pr
        self.p = members * self.pe
        self.pt = round_up(self.p, 256)
        self.cp = round_up(channels + noise, 128)
        self.ct = self.cp // 128
        self.cr = round_up(channels, 16)
        self.hp = round_up(hidden, 128)
        self.hm = hidden // 1280 * 1280 if hidden > 1280 else hidden


def smem():
    return pl.BlockSpec(memory_space=pltpu.SMEM)


def vmem():
    return pl.BlockSpec(memory_space=pltpu.VMEM)


def column_blocks(width, step):
    return [(i, min(step, width - i)) for i in range(0, width, step)]


def norm_rows(values, channels, lanes):
    inside = lanes < channels
    values = jnp.where(inside, values, 0.0)
    mean = jnp.sum(values, axis=1, keepdims=True) * (1.0 / channels)
    centred = jnp.where(inside, values - mean, 0.0)
    spread = jnp.sum(centred * centred, axis=1, keepdims=True) * (1.0 / channels)
    return centred, lax.rsqrt(spread + NORM_EPS)


def gelu_parts(v):
    size = jnp.abs(v)
    t = 1.0 / (1.0 + (0.3275911 * math.sqrt(0.5)) * size)
    bell = jnp.exp(-0.5 * v * v)
    poly = t * (
        0.5 * 0.254829592
        + t * (-0.5 * 0.284496736 + t * (0.5 * 1.421413741 + t * (-0.5 * 1.453152027 + t * (0.5 * 1.061405429))))
    )
    tail = poly * bell
    cdf = jnp.where(v >= 0.0, 1.0 - tail, tail)
    return v * cdf, cdf + v * bell * (1.0 / math.sqrt(2.0 * math.pi))


def main_kernel(
    sz,
    height_ref,
    taps_ref,
    x_ref,
    prev_ref,
    next_ref,
    target_ref,
    expand_ref,
    bias_ref,
    reduce_ref,
    gain_ref,
    outbias_ref,
    filter_ref,
    noisemix_ref,
    grad_e_ref,
    grad_r_ref,
    bg_ref,
    gn_own_ref,
    gn_prev_ref,
    gn_next_ref,
    filter_grad_ref,
    mixing_grad_ref,
    outbias_grad_ref,
    biasin_grad_ref,
    loss_ref,
    n_ref,
    mx_ref,
    act_ref,
    dg_ref,
    pred_ref,
    tr_ref,
    gn_ref,
    fil_ref,
):
    height = height_ref[0]
    lanes = lax.broadcasted_iota(jnp.int32, (1, sz.cp), 1)
    inside = (lanes < sz.c).astype(f32)
    below_first = jnp.where(height == 2, 2, 3)
    sources = ((0, 1, below_first), (1, 2, 3))
    two_pr = sz.pe

    def forward(e, carry):
        def norm_store(values, row):
            centred, inv = norm_rows(values.astype(f32), sz.c, lanes)
            normed = (centred * inv * gain_ref[...]).astype(bf16).astype(f32)
            for ct in range(sz.ct):
                n_ref[e, row, ct] = normed[:, ct * 128 : (ct + 1) * 128]

        norm_store(prev_ref[e], 0)
        norm_store(x_ref[e, 0], 1)
        norm_store(x_ref[e, 1], 2)
        norm_store(next_ref[e], 3)

        def filter_tile(ct, c):
            for r in range(2):
                acc = jnp.zeros((sz.pr, 128), f32)
                for a in range(3):
                    for j in range(3):
                        tap = 3 * a + j
                        start = taps_ref[tap, r] + REACH
                        moved = n_ref[e, sources[r][a], ct, pl.ds(start, sz.pr), :]
                        acc = acc + filter_ref[ct, tap : tap + 1, :] * moved
                fil_ref[ct, r * sz.pr : (r + 1) * sz.pr, :] = acc
            return c

        lax.fori_loop(0, sz.ct, filter_tile, 0)
        last = (sz.ct - 1) * 128
        noise = jnp.concatenate(
            [x_ref[e, r].astype(f32)[REACH : REACH + sz.pr, last:] for r in range(2)], axis=0
        ).astype(bf16)
        mixed = mm(jnp.concatenate([noise, noise], axis=1), noisemix_ref[...])
        filtered = jnp.concatenate([fil_ref[ct] for ct in range(sz.ct)], axis=1)
        mixed = (filtered + mixed).astype(bf16)
        rows = pl.ds(pl.multiple_of(e * two_pr, 16), two_pr)
        mx_ref[rows, :] = mixed
        for at, width in column_blocks(sz.hp, 256):
            pre = mm(mixed, expand_ref[:, at : at + width]) + bias_ref[:, at : at + width]
            act, slope = gelu_parts(pre)
            act_ref[rows, at : at + width] = act.astype(bf16)
            dg_ref[rows, at : at + width] = slope.astype(bf16)
        branch = mm(act_ref[rows, :], reduce_ref[...], NT) + outbias_ref[...]
        own = jnp.concatenate([x_ref[e, r].astype(f32)[REACH : REACH + sz.pr] for r in range(2)], axis=0)
        pred_ref[e] = own + branch
        return carry

    lax.fori_loop(0, sz.m, forward, 0)

    loss_ref[...] = jnp.zeros_like(loss_ref)
    outbias_grad_ref[...] = jnp.zeros_like(outbias_grad_ref)
    step = 16
    inv_m = 1.0 / sz.m
    inv_mm = inv_m * inv_m

    def score(i, carry):
        at = pl.multiple_of(i * step, step)
        pixel = at + lax.broadcasted_iota(jnp.int32, (step, 1), 0)
        row = (pixel >= sz.pr).astype(jnp.int32)
        use = (pixel - row * sz.pr < sz.q) & (row < height)
        mask_rows = use.astype(f32)
        for ct in range(sz.ct):
            cols = slice(ct * 128, (ct + 1) * 128)
            mask = mask_rows * inside[:, cols]
            preds = [pred_ref[e, pl.ds(at, step), cols] for e in range(sz.m)]
            truth = target_ref[pl.ds(at, step), cols].astype(f32)
            slopes = []
            own_sum = 0.0
            for p in preds:
                d = p - truth
                q = d * d + 1.0
                r = lax.rsqrt(q)
                own_sum = own_sum + q * r
                slopes.append(d * r * inv_m)
            pair_sum = 0.0
            pairs = [0.0] * sz.m
            for a in range(sz.m):
                for b in range(a + 1, sz.m):
                    d = preds[a] - preds[b]
                    q = d * d + 1.0
                    r = lax.rsqrt(q)
                    pair_sum = pair_sum + q * r
                    s = d * r
                    pairs[a] = pairs[a] + s
                    pairs[b] = pairs[b] - s
            value = own_sum * inv_m - (pair_sum + 0.5 * sz.m) * inv_mm
            loss_ref[...] += mask * value
            total = 0.0
            for e in range(sz.m):
                g = (mask * (slopes[e] - pairs[e] * inv_mm)).astype(bf16)
                where = pl.ds(pl.multiple_of(e * two_pr + at, 16), step)
                bg_ref[where, cols] = g
                total = total + g.astype(f32)
            outbias_grad_ref[:, cols] += total[0:8] + total[8:16]
        return carry

    lax.fori_loop(0, two_pr // step, score, 0)
    if sz.pt > sz.p:
        bg_ref[sz.p :, :] = jnp.zeros((sz.pt - sz.p, sz.cp), bf16)
        mx_ref[sz.p :, :] = jnp.zeros((sz.pt - sz.p, sz.cp), bf16)
        act_ref[sz.p :, :] = jnp.zeros((sz.pt - sz.p, sz.hp), bf16)

    def transpose_into(src):
        def body(i, c):
            at = pl.ds(pl.multiple_of(i * 128, 128), 128)
            for ct in range(sz.ct):
                block = src[at, ct * 128 : (ct + 1) * 128].astype(f32).T.astype(bf16)
                size = min(128, sz.cr - ct * 128)
                if size > 0:
                    tr_ref[ct * 128 : ct * 128 + size, at] = block[:size]
            return c

        lax.fori_loop(0, sz.pt // 128, body, 0)

    transpose_into(bg_ref)
    for at, width in column_blocks(sz.hp, 256):
        grad_r_ref[:, at : at + width] = mm(tr_ref[...], act_ref[:, at : at + width]).astype(bf16)

    gn_ref[...] = jnp.zeros_like(gn_ref)
    filter_grad_ref[...] = jnp.zeros_like(filter_grad_ref)
    biasin_grad_ref[...] = jnp.zeros_like(biasin_grad_ref)
    mixing_grad_ref[...] = jnp.zeros_like(mixing_grad_ref)

    def backward(e, carry):
        rows = pl.ds(pl.multiple_of(e * two_pr, 16), two_pr)
        bg = bg_ref[rows, :]
        for at, width in column_blocks(sz.hp, 256):
            grad = mm(bg, reduce_ref[:, at : at + width])
            pre = (grad * dg_ref[rows, at : at + width].astype(f32)).astype(bf16)
            act_ref[rows, at : at + width] = pre
            wide = pre.astype(f32)
            biasin_grad_ref[:, at : at + width] += jnp.sum(wide.reshape(-1, 8, width), axis=0)
        gm = mm(act_ref[rows, :], expand_ref[...], NT)
        for ct in range(sz.ct):
            fil_ref[ct] = gm[:, ct * 128 : (ct + 1) * 128]
        last = (sz.ct - 1) * 128
        noise = jnp.concatenate(
            [x_ref[e, r].astype(f32)[REACH : REACH + sz.pr, last:] for r in range(2)], axis=0
        )
        mixing_grad_ref[...] += mm(noise.T[0:16].astype(bf16), gm.astype(bf16))

        def unfilter_tile(ct, c):
            for r in range(2):
                g = fil_ref[ct, r * sz.pr : (r + 1) * sz.pr, :]
                for a in range(3):
                    source = sources[r][a]
                    for j in range(3):
                        tap = 3 * a + j
                        where = pl.ds(taps_ref[tap, r] + REACH, sz.pr)
                        gn_ref[e, source, ct, where, :] += filter_ref[ct, tap : tap + 1, :] * g
                        product = g * n_ref[e, source, ct, where, :]
                        filter_grad_ref[ct, tap] += jnp.sum(product.reshape(-1, 8, 128), axis=0)
            return c

        lax.fori_loop(0, sz.ct, unfilter_tile, 0)
        for ct in range(sz.ct):
            cols = slice(ct * 128, (ct + 1) * 128)
            gn_prev_ref[e, :, cols] = gn_ref[e, 0, ct].astype(bf16)
            gn_next_ref[e, :, cols] = gn_ref[e, 3, ct].astype(bf16)
            gn_own_ref[e, 0, :, cols] = gn_ref[e, 1, ct]
            gn_own_ref[e, 1, :, cols] = gn_ref[e, 2, ct]
        return carry

    lax.fori_loop(0, sz.m, backward, 0)
    transpose_into(mx_ref)
    for at, width in column_blocks(sz.hp, 256):
        grad_e_ref[:, at : at + width] = mm(tr_ref[...], act_ref[:, at : at + width]).astype(bf16)


def main_call(sz, height, taps, x, prev, after, target, expand, bias, reduce, gain, outbias, filt, noisemix):
    shape = jax.ShapeDtypeStruct
    outs = (
        shape((sz.cr, sz.hp), bf16),
        shape((sz.cr, sz.hp), bf16),
        shape((sz.pt, sz.cp), bf16),
        shape((sz.m, 2, sz.ext, sz.cp), f32),
        shape((sz.m, sz.ext, sz.cp), bf16),
        shape((sz.m, sz.ext, sz.cp), bf16),
        shape((sz.ct, 9, 8, 128), f32),
        shape((16, sz.cp), f32),
        shape((8, sz.cp), f32),
        shape((8, sz.hp), f32),
        shape((16, 128), f32),
    )
    return pl.pallas_call(
        functools.partial(main_kernel, sz),
        out_shape=outs,
        in_specs=[smem(), smem()] + [vmem()] * 11,
        out_specs=tuple(vmem() for _ in outs),
        scratch_shapes=[
            pltpu.VMEM((sz.m, 4, sz.ct, sz.ext, 128), f32),
            pltpu.VMEM((sz.pt, sz.cp), bf16),
            pltpu.VMEM((sz.pt, sz.hp), bf16),
            pltpu.VMEM((sz.p, sz.hp), bf16),
            pltpu.VMEM((sz.m, sz.pe, sz.cp), f32),
            pltpu.VMEM((sz.cr, sz.pt), bf16),
            pltpu.VMEM((sz.m, 4, sz.ct, sz.ext, 128), f32),
            pltpu.VMEM((sz.ct, sz.pe, 128), f32),
        ],
        compiler_params=pltpu.CompilerParams(vmem_limit_bytes=63 * 1024 * 1024),
        name="main",
    )(height, taps, x, prev, after, target, expand, bias, reduce, gain, outbias, filt, noisemix)


def norm_back_kernel(sz, height_ref, x_ref, gn_ref, up_ref, down_ref, bg_ref, gain_ref, out_ref, gain_grad_ref):
    height = height_ref[0]
    lanes = lax.broadcasted_iota(jnp.int32, (1, sz.cp), 1)
    gain_grad_ref[...] = jnp.zeros_like(gain_grad_ref)

    def body(e, carry):
        from_up = up_ref[e].astype(f32)
        from_down = down_ref[e].astype(f32)
        rows = pl.ds(pl.multiple_of(e * sz.pe, 16), sz.pe)
        direct = bg_ref[rows, :].astype(f32)
        for r in range(2):
            centred, inv = norm_rows(x_ref[e, r].astype(f32), sz.c, lanes)
            xhat = centred * inv
            g = gn_ref[e, r] + jnp.where(height == r + 1, from_down, 0.0)
            if r == 0:
                g = g + from_up
            gain_grad_ref[...] += jnp.sum((g * xhat).reshape(-1, 8, sz.cp), axis=0)
            q = g * gain_ref[...]
            mean_q = jnp.sum(q, axis=1, keepdims=True) * (1.0 / sz.c)
            mean_qx = jnp.sum(q * xhat, axis=1, keepdims=True) * (1.0 / sz.c)
            result = (q - mean_q - xhat * mean_qx) * inv
            out_ref[e, r] = result.astype(bf16)
            part = result[REACH : REACH + sz.pr] + direct[r * sz.pr : (r + 1) * sz.pr]
            pieces = [result[:REACH], part, result[REACH + sz.pr :]]
            out_ref[e, r] = jnp.concatenate(pieces, axis=0).astype(bf16)
        return carry

    lax.fori_loop(0, sz.m, body, 0)


def norm_back_call(sz, height, x, gn, up, down, bg, gain):
    shape = jax.ShapeDtypeStruct
    outs = (shape((sz.m, 2, sz.ext, sz.cp), bf16), shape((8, sz.cp), f32))
    return pl.pallas_call(
        functools.partial(norm_back_kernel, sz),
        out_shape=outs,
        in_specs=[smem()] + [vmem()] * 6,
        out_specs=tuple(vmem() for _ in outs),
        compiler_params=pltpu.CompilerParams(vmem_limit_bytes=40 * 1024 * 1024),
        name="norm_back",
    )(height, x, gn, up, down, bg, gain)


def exchange(pieces, axis, count):
    result = [pieces[0]]
    for s in range(1, count):
        result.append(lax.ppermute(pieces[s], axis, [(i, i ^ s) for i in range(count)]))
    return result


def reduce_over(values, axis, count, dim):
    me = lax.axis_index(axis)
    size = values.shape[dim] // count
    pieces = [lax.dynamic_slice_in_dim(values, (me ^ s) * size, size, axis=dim) for s in range(count)]
    arrived = exchange(pieces, axis, count)
    return sum(part.astype(f32) for part in arrived)


def gather_over(values, axis, count, dim):
    me = lax.axis_index(axis)
    stacked = jnp.stack(exchange([values] * count, axis, count))
    ordered = [lax.dynamic_index_in_dim(stacked, me ^ k, 0, keepdims=False) for k in range(count)]
    return jnp.concatenate(ordered, axis=dim)


def adam_step(weight, gradient, first, second, rate):
    first_new = BETA_ONE * first + (1.0 - BETA_ONE) * gradient
    second_new = BETA_TWO * second + (1.0 - BETA_TWO) * gradient * gradient
    first_hat = first_new / (1.0 - BETA_ONE**STEP)
    second_hat = second_new / (1.0 - BETA_TWO**STEP)
    weight_new = weight - rate * (
        first_hat / (jnp.sqrt(second_hat) + ADAM_EPS) + DECAY_RATE * weight
    )
    return (weight_new, first_new, second_new)


def pad_to(values, shape):
    return jnp.pad(values, [(0, n - m) for n, m in zip(shape, values.shape)])


def on_device(
    fields,
    noise_fields,
    target_fields,
    band_heights,
    tap_offsets,
    expand_weight,
    expand_bias,
    reduce_weight,
    channel_vectors,
    disco_filter,
    noise_mixing,
    first_expand,
    second_expand,
    first_bias,
    second_bias,
    first_reduce,
    second_reduce,
    first_vectors,
    second_vectors,
    first_filter,
    second_filter,
    first_mixing,
    second_mixing,
):
    members = lax.axis_size("member")
    stacks = lax.axis_size("stack")
    lat_count = 2 * stacks
    lat = ("stack", "core")
    channels, hidden = expand_weight.shape
    lon = fields.shape[3]
    sz = Sizes(members, channels, hidden, noise_fields.shape[1], lon)
    me = lax.axis_index("member")
    core = lax.axis_index("core")
    band = lax.axis_index("stack") * 2 + core
    height = lax.dynamic_slice_in_dim(band_heights, band, 1)

    both = jnp.concatenate([fields[0], noise_fields[0]], axis=0)
    both = jnp.transpose(both, (1, 2, 0))
    both = pad_to(both, (2, lon, sz.cp))
    tail = sz.ext - REACH - sz.q
    around = jnp.concatenate([both[:, lon - REACH :], both, both[:, :tail]], axis=1)
    pieces = [lax.dynamic_slice_in_dim(around, (me ^ s) * sz.q, sz.ext, axis=1) for s in range(members)]
    x = jnp.stack(exchange(pieces, "member", members))
    upward = [(i, i + 1) for i in range(lat_count - 1)]
    downward = [(i + 1, i) for i in range(lat_count - 1)]
    bottom = lax.dynamic_index_in_dim(x, height[0] - 1, 1, keepdims=False)
    prev = lax.ppermute(bottom, lat, upward)
    after = lax.ppermute(x[:, 0], lat, downward)

    truth = pad_to(target_fields, (channels, 2, lon + sz.pr - sz.q))
    truth = lax.dynamic_slice_in_dim(truth, me * sz.q, sz.pr, axis=2)
    truth = pad_to(jnp.transpose(truth, (1, 2, 0)), (2, sz.pr, sz.cp)).reshape(sz.pe, sz.cp)

    expand_low = pad_to(expand_weight.astype(bf16), (sz.cp, sz.hp))
    reduce_low = pad_to(reduce_weight.T.astype(bf16), (sz.cp, sz.hp))
    bias = pad_to(expand_bias[None], (1, sz.hp))
    gain = pad_to(channel_vectors[0:1], (1, sz.cp))
    outbias = pad_to(channel_vectors[1:2], (1, sz.cp))
    filt = jnp.transpose(pad_to(disco_filter, (16, sz.cp)).reshape(16, sz.ct, 128), (1, 0, 2))
    at = channels - (sz.ct - 1) * 128
    coarse = noise_mixing.astype(bf16)
    fine = (noise_mixing - coarse.astype(f32)).astype(bf16)
    noisemix = jnp.zeros((256, sz.cp), bf16)
    noisemix = noisemix.at[at : at + sz.k, :channels].set(coarse)
    noisemix = noisemix.at[128 + at : 128 + at + sz.k, :channels].set(fine)

    (
        grad_e,
        grad_r,
        bg,
        gn_own,
        gn_prev,
        gn_next,
        filter_part,
        mixing_part,
        outbias_part,
        biasin_part,
        loss_part,
    ) = main_call(
        sz, height, tap_offsets, x, prev, after, truth, expand_low, bias, reduce_low, gain, outbias, filt, noisemix
    )

    up = lax.ppermute(gn_next, lat, upward)
    down = lax.ppermute(gn_prev, lat, downward)
    own_grad, gain_part = norm_back_call(sz, height, x, gn_own, up, down, bg, gain)

    returned = jnp.stack(exchange([own_grad[s] for s in range(members)], "member", members))
    parts = [lax.dynamic_index_in_dim(returned, me ^ j, 0, keepdims=False) for j in range(members)]
    total = jnp.zeros((2, lon, channels), f32)
    lefts, mids, rights = [], [], []
    for part in parts:
        wide = part[:, :, :channels].astype(f32)
        lefts.append(wide[:, :REACH])
        mids.append(wide[:, REACH : REACH + sz.q])
        rights.append(wide[:, REACH + sz.q : 2 * REACH + sz.q])
    rows = []
    for j in range(members):
        extra = jnp.concatenate(
            [rights[j - 1], jnp.zeros((2, sz.q - 2 * REACH, channels), f32), lefts[(j + 1) % members]], axis=1
        )
        rows.append(mids[j] + extra)
    total = jnp.concatenate(rows, axis=1).astype(bf16)
    input_gradient = jnp.transpose(total, (2, 0, 1))[None]

    main_c = channels // (4 * 16 * 2) * (4 * 16 * 2)
    main_h = hidden // 256 * 256
    grads = jnp.stack([grad_e[:main_c, :main_h], grad_r[:main_c, :main_h]])
    half = main_h // 2
    mine = lax.dynamic_slice_in_dim(grads, core * half, half, axis=2)
    other = lax.dynamic_slice_in_dim(grads, (1 - core) * half, half, axis=2)
    swap = [(0, 1), (1, 0)]
    got = lax.ppermute(other, "core", swap)
    part = (mine.astype(f32) + got.astype(f32)).astype(bf16)
    part = reduce_over(part, "member", members, 1).astype(bf16)
    part = reduce_over(part, "stack", stacks, 1).astype(bf16)
    part = gather_over(part, "stack", stacks, 1)
    part = gather_over(part, "member", members, 1)
    got = lax.ppermute(part, "core", swap)
    low_half = jnp.where(core == 0, part, got)
    high_half = jnp.where(core == 0, got, part)
    grads = jnp.concatenate([low_half, high_half], axis=2)

    filter_rows = jnp.transpose(jnp.sum(filter_part, axis=2), (1, 0, 2)).reshape(9, sz.cp)
    small_parts = [
        filter_rows[:, :channels],
        mixing_part[at : at + sz.k, :channels],
        jnp.sum(gain_part, axis=0)[:channels],
        jnp.sum(outbias_part, axis=0)[:channels],
        jnp.sum(biasin_part, axis=0)[:hidden],
        grad_e[main_c:channels, :hidden].astype(f32),
        grad_r[main_c:channels, :hidden].astype(f32),
        grad_e[:main_c, main_h:hidden].astype(f32),
        grad_r[:main_c, main_h:hidden].astype(f32),
        jnp.sum(loss_part),
    ]
    flat = jnp.concatenate([v.reshape(-1) for v in small_parts])
    width = round_up(flat.shape[0], 1024)
    flat = jnp.pad(flat, (0, width - flat.shape[0])).reshape(-1, 128)
    flat = flat + lax.ppermute(flat, "core", swap)
    flat = sum(exchange([flat] * members, "member", members))
    flat = sum(exchange([flat] * stacks, "stack", stacks))
    flat = flat.reshape(-1)
    summed = []
    offset = 0
    for v in small_parts:
        summed.append(flat[offset : offset + v.size].reshape(v.shape))
        offset += v.size
    (
        sum_filter,
        sum_mixing,
        sum_gain,
        sum_bias_out,
        sum_bias_in,
        row_e,
        row_r,
        col_e,
        col_r,
        loss_total,
    ) = summed

    def whole(main, row, col):
        return jnp.concatenate([jnp.concatenate([main.astype(f32), col], axis=1), row], axis=0)

    sum_expand = whole(grads[0], row_e, col_e)
    sum_reduce = whole(grads[1], row_r, col_r)
    sum_vectors = jnp.stack([sum_gain, sum_bias_out])
    live_total = jnp.sum(band_heights).astype(f32)
    mean_loss = loss_total / (channels * lon * live_total)
    squares = (
        jnp.sum(sum_expand * sum_expand)
        + jnp.sum(sum_bias_in * sum_bias_in)
        + jnp.sum(sum_reduce * sum_reduce)
        + jnp.sum(sum_vectors * sum_vectors)
        + jnp.sum(sum_filter * sum_filter)
        + jnp.sum(sum_mixing * sum_mixing)
    )
    gradient_norm = jnp.sqrt(squares)
    limit = 0.02 * math.sqrt(hidden * channels * lat_count * 2 * lon / members)
    factor = jnp.minimum(1.0, limit / (gradient_norm + 1e-06))
    expand_out, expand_first, expand_second = adam_step(
        expand_weight, factor * sum_expand, first_expand, second_expand, channels ** (-0.5)
    )
    bias_out, bias_first, bias_second = adam_step(
        expand_bias, factor * sum_bias_in, first_bias, second_bias, SMALL_RATE
    )
    reduce_out, reduce_first, reduce_second = adam_step(
        reduce_weight.T, factor * sum_reduce, first_reduce.T, second_reduce.T, hidden ** (-0.5)
    )
    vectors_out, vectors_first, vectors_second = adam_step(
        channel_vectors, factor * sum_vectors, first_vectors, second_vectors, SMALL_RATE
    )
    filter_out, filter_first, filter_second = adam_step(
        disco_filter, factor * sum_filter, first_filter, second_filter, SMALL_RATE
    )
    mixing_out, mixing_first, mixing_second = adam_step(
        noise_mixing, factor * sum_mixing, first_mixing, second_mixing, SMALL_RATE
    )
    return (
        mean_loss,
        input_gradient,
        gradient_norm,
        expand_out,
        expand_first,
        expand_second,
        bias_out,
        bias_first,
        bias_second,
        reduce_out.T,
        reduce_first.T,
        reduce_second.T,
        vectors_out,
        vectors_first,
        vectors_second,
        filter_out,
        filter_first,
        filter_second,
        mixing_out,
        mixing_first,
        mixing_second,
        expand_out.astype(bf16),
        reduce_out.astype(bf16).T,
    )


def solution(mesh):
    members = mesh.shape["member"]
    lat = mesh.shape["lat"]
    split = Mesh(mesh.devices.reshape(members, lat // 2, 2), ("member", "stack", "core"))
    rows = ("stack", "core")
    whole = [P()] * 18
    in_specs = (
        P("member", None, rows, None),
        P("member", None, rows, None),
        P(None, rows, None),
        P(),
        P(None, rows),
        *whole,
    )
    out_specs = (P(), P("member", None, rows, None)) + (P(),) * 21
    return jax.shard_map(on_device, mesh=split, in_specs=in_specs, out_specs=out_specs, check_vma=False)
```

```python
import functools
import math

import jax
import jax.numpy as jnp
from jax import lax
from jax.experimental import pallas as pl
from jax.experimental.pallas import tpu as pltpu
from jax.sharding import Mesh, PartitionSpec as P

STEP = 10
BETA_ONE = 0.9
BETA_TWO = 0.95
ADAM_EPS = 1e-08
DECAY_RATE = 0.1
NORM_EPS = 1e-05
SMALL_RATE = 0.3
REACH = 8
f32 = jnp.float32
bf16 = jnp.bfloat16

NN = (((1,), (0,)), ((), ()))
NT = (((1,), (1,)), ((), ()))
TN = (((0,), (0,)), ((), ()))


def round_up(value, step):
    return -(-value // step) * step


def mm(a, b, dims=NN):
    return lax.dot_general(a, b, dims, preferred_element_type=f32)


class Sizes:
    def __init__(self, members, channels, hidden, noise, lon):
        self.m = members
        self.c = channels
        self.h = hidden
        self.k = noise
        self.lon = lon
        self.q = lon // members
        self.pr = round_up(self.q, 8)
        self.ext = round_up(self.pr + 2 * REACH, 16)
        self.pe = 2 * self.pr
        self.p = members * self.pe
        self.cp = round_up(channels + noise, 128)
        self.ct = self.cp // 128
        self.cr = round_up(channels, 16)
        self.hp = round_up(hidden, 128)
        self.mc = channels // 128 * 128
        self.mh = hidden // 256 * 256

    def piece_rows(self, members, stacks):
        each = self.mc // members
        return next(n for n in range(8, each + 1, 8) if each % n == 0 and n * stacks >= each)


class Rows:
    def __init__(self, sz):
        self.mixing = 9
        self.outbias = self.mixing + sz.k
        self.biasin = self.outbias + 1
        self.row_e = self.biasin + 2
        self.row_r = self.row_e + 2
        self.spare = sz.h - sz.mh
        self.col_e = self.row_r + 2
        self.col_r = self.col_e + self.spare
        self.extra = self.col_r + self.spare
        self.count = round_up(self.extra + 1, 32)
        self.x_mixing = 9
        self.x_outbias = self.x_mixing + sz.k
        self.x_biasin = self.x_outbias + 1
        self.x_row_e = self.x_biasin + self.spare
        self.x_row_r = self.x_row_e + self.spare
        self.x_loss = self.x_row_r + self.spare


def smem():
    return pl.BlockSpec(memory_space=pltpu.SMEM)


def vmem():
    return pl.BlockSpec(memory_space=pltpu.VMEM)


def tile_sum(values):
    tiles = [values[i : i + 8] for i in range(0, values.shape[0], 8)]
    while len(tiles) > 1:
        tiles = [a + b for a, b in zip(tiles[::2], tiles[1::2])] + tiles[len(tiles) // 2 * 2 :]
    return tiles[0]


def column_blocks(width, step):
    return [(i, min(step, width - i)) for i in range(0, width, step)]


def norm_rows(values, channels, lanes):
    inside = lanes < channels
    values = jnp.where(inside, values, 0.0)
    mean = jnp.sum(values, axis=1, keepdims=True) * (1.0 / channels)
    centred = jnp.where(inside, values - mean, 0.0)
    spread = jnp.sum(centred * centred, axis=1, keepdims=True) * (1.0 / channels)
    return centred, lax.rsqrt(spread + NORM_EPS)


def gelu_parts(v):
    size = jnp.abs(v)
    t = 1.0 / (1.0 + (0.3275911 * math.sqrt(0.5)) * size)
    bell = jnp.exp(-0.5 * v * v)
    poly = t * (
        0.5 * 0.254829592
        + t * (-0.5 * 0.284496736 + t * (0.5 * 1.421413741 + t * (-0.5 * 1.453152027 + t * (0.5 * 1.061405429))))
    )
    tail = poly * bell
    cdf = jnp.where(v >= 0.0, 1.0 - tail, tail)
    return v * cdf, cdf + v * bell * (1.0 / math.sqrt(2.0 * math.pi))


def cost(microseconds):
    return pl.CostEstimate(flops=int(microseconds * 5e7), bytes_accessed=0, transcendentals=0)


def transpose_into(sz, src, dst):
    def move(at, count):
        for ct in range(sz.ct):
            block = src[pl.ds(at, count), ct * 128 : (ct + 1) * 128].T
            size = min(128, sz.cr - ct * 128)
            if size > 0:
                dst[ct * 128 : ct * 128 + size, pl.ds(at, count)] = block[:size]

    def body(i, c):
        move(pl.multiple_of(i * 128, 128), 128)
        return c

    lax.fori_loop(0, sz.p // 128, body, 0)
    if sz.p % 128:
        move(sz.p // 128 * 128, sz.p % 128)


def weight_grad(sz, core, left_ref, right_ref, left_t_ref, mine_ref, other_ref, row_ref, col_ref):
    transpose_into(sz, left_ref, left_t_ref)
    half = sz.mh // 2
    for half_ref, which in ((other_ref, 1 - core), (mine_ref, core)):
        for at, width in column_blocks(half, 256):
            cols = pl.ds(pl.multiple_of(which * half + at, 128), width)
            block = mm(left_t_ref[...], right_ref[:, cols])
            row_ref[:, cols] = block[sz.mc :]
            half_ref[:, at : at + width] = block[: sz.mc].astype(bf16)
    rest = right_ref[:, sz.mh :]
    row_ref[:, sz.mh :] = mm(left_t_ref[sz.mc :, :], rest)
    col_ref[...] = mm(rest.astype(f32).T[0:16].astype(bf16), left_ref[...])


def split_kernel(sz, shifts, height_ref, me_ref, x_ref, noise_ref, *refs):
    pieces, y_ref, s_ref = refs[: sz.m], refs[sz.m], refs[sz.m + 1]
    for ct in range(sz.ct):
        first = ct * 128
        if ct < sz.ct - 1:
            spans = [(x_ref, first, 128, 0)]
        else:
            rest = sz.c - first
            s_ref[...] = jnp.zeros_like(s_ref)
            spans = [(x_ref, first, rest, 0), (noise_ref, 0, sz.k, rest)]
        for ref, at, count, to in spans:
            for lt, width in column_blocks(sz.lon, 128):
                block = ref[0, at : at + count, :, lt : lt + width].astype(f32)
                s_ref[lt // 128, 2 * to : 2 * (to + count), :width] = block.reshape(2 * count, width)
        for r in range(2):
            for lt, width in column_blocks(sz.lon, 128):
                block = s_ref[lt // 128, pl.ds(r, 128, stride=2), :].T
                y_ref[r, ct, REACH + lt : REACH + lt + width, :] = block[:width]
    for r in range(2):
        for ct in range(sz.ct):
            y_ref[r, ct, :REACH, :] = y_ref[r, ct, sz.lon : sz.lon + REACH, :]
            y_ref[r, ct, REACH + sz.lon :, :] = y_ref[r, ct, REACH : sz.ext - sz.q, :]
    for s in range(sz.m):
        start = (me_ref[0] ^ shifts[s]) * sz.q
        for r, row in enumerate((0, height_ref[0] - 1)):
            for ct in range(sz.ct):
                pieces[s][r, :, ct * 128 : (ct + 1) * 128] = y_ref[row, ct, pl.ds(start, sz.ext), :].astype(bf16)


def split_call(sz, shifts, height, me, x, noise):
    outs = tuple(jax.ShapeDtypeStruct((2, sz.ext, sz.cp), bf16) for _ in range(sz.m))
    return pl.pallas_call(
        functools.partial(split_kernel, sz, shifts),
        out_shape=outs,
        in_specs=[smem(), smem(), vmem(), vmem()],
        out_specs=tuple(vmem() for _ in outs),
        scratch_shapes=[
            pltpu.VMEM((2, sz.ct, sz.lon + sz.ext - sz.q, 128), f32),
            pltpu.VMEM((round_up(sz.lon, 128) // 128, 256, 128), f32),
        ],
        compiler_params=pltpu.CompilerParams(vmem_limit_bytes=24 * 1024 * 1024),
        cost_estimate=cost(5),
        name="split",
    )(height, me, x, noise)


def join_kernel(sz, shifts, me_ref, *refs):
    pieces, out_ref, y_ref, s_ref = refs[: sz.m], refs[sz.m], refs[sz.m + 1], refs[sz.m + 2]
    tail = sz.ext - sz.q - REACH
    y_ref[...] = jnp.zeros_like(y_ref)
    for s in range(sz.m):
        start = (me_ref[0] ^ shifts[s]) * sz.q
        for r in range(2):
            for ct in range(sz.ct):
                part = pieces[s][r, :, ct * 128 : (ct + 1) * 128].astype(f32)
                y_ref[r, ct, pl.ds(start, sz.ext), :] += part
    for r in range(2):
        for ct in range(sz.ct):
            y_ref[r, ct, sz.lon : sz.lon + REACH, :] += y_ref[r, ct, :REACH, :]
            y_ref[r, ct, REACH : REACH + tail, :] += y_ref[r, ct, REACH + sz.lon : REACH + sz.lon + tail, :]
    for ct in range(sz.ct):
        for r in range(2):
            for lt in range(0, sz.lon, 128):
                block = y_ref[r, ct, REACH + lt : REACH + lt + 128, :].T
                s_ref[lt // 128, pl.ds(r, 128, stride=2), :] = block
        size = min(128, sz.c - ct * 128)
        for lt, width in column_blocks(sz.lon, 128):
            block = s_ref[lt // 128, : 2 * size, :width].reshape(size, 2, width)
            out_ref[0, ct * 128 : ct * 128 + size, :, lt : lt + width] = block.astype(bf16)


def join_call(sz, shifts, me, pieces):
    return pl.pallas_call(
        functools.partial(join_kernel, sz, shifts),
        out_shape=jax.ShapeDtypeStruct((1, sz.c, 2, sz.lon), bf16),
        in_specs=[smem()] + [vmem()] * sz.m,
        out_specs=vmem(),
        scratch_shapes=[
            pltpu.VMEM((2, sz.ct, REACH + max(round_up(sz.lon, 128), sz.lon + sz.ext - sz.q - REACH), 128), f32),
            pltpu.VMEM((round_up(sz.lon, 128) // 128, 256, 128), f32),
        ],
        compiler_params=pltpu.CompilerParams(vmem_limit_bytes=24 * 1024 * 1024),
        cost_estimate=cost(6),
        name="join",
    )(me, *pieces)


def norm_and_filter(sz, e, height_ref, taps_ref, x_ref, prev_ref, next_ref, gain_ref, filter_ref, normed_ref, n_ref, fil_ref):
    lanes = lax.broadcasted_iota(jnp.int32, (1, sz.cp), 1)
    below_first = jnp.where(height_ref[0] == 2, 2, 3)
    sources = ((0, 1, below_first), (1, 2, 3))

    def norm_store(values, row):
        centred, inv = norm_rows(values.astype(f32), sz.c, lanes)
        normed = (centred * inv * gain_ref[...]).astype(bf16)
        normed_ref[e, row] = normed
        normed = normed.astype(f32)
        for ct in range(sz.ct):
            n_ref[row, ct] = normed[:, ct * 128 : (ct + 1) * 128]

    norm_store(prev_ref[e], 0)
    norm_store(x_ref[e, 0], 1)
    norm_store(x_ref[e, 1], 2)
    norm_store(next_ref[e], 3)

    def filter_tile(ct, c):
        for r in range(2):
            acc = jnp.zeros((sz.pr, 128), f32)
            for a in range(3):
                for j in range(3):
                    tap = 3 * a + j
                    start = taps_ref[tap, r] + REACH
                    moved = n_ref[sources[r][a], ct, pl.ds(start, sz.pr), :]
                    acc = acc + filter_ref[ct, tap : tap + 1, :] * moved
            fil_ref[ct, r * sz.pr : (r + 1) * sz.pr, :] = acc
        return c

    lax.fori_loop(0, sz.ct, filter_tile, 0)


def feed_forward(sz, e, x_ref, fil_ref, expand_ref, bias_ref, reduce_ref, outbias_ref, noisemix_ref, store):
    own = jnp.concatenate([x_ref[e, r].astype(f32)[REACH : REACH + sz.pr] for r in range(2)], axis=0)
    noise = own[:, (sz.ct - 1) * 128 :].astype(bf16)
    mixed = mm(jnp.concatenate([noise, noise], axis=1), noisemix_ref[...])
    filtered = jnp.concatenate([fil_ref[ct] for ct in range(sz.ct)], axis=1)
    lanes = lax.broadcasted_iota(jnp.int32, (1, sz.cp), 1)
    mixed = jnp.where(lanes == sz.c, 1.0, filtered + mixed).astype(bf16)
    store("mixed", slice(0, sz.cp), mixed)
    acts = []
    for at, width in column_blocks(sz.hp, 256):
        pre = mm(mixed, expand_ref[:, at : at + width]) + bias_ref[:, at : at + width]
        act, slope = gelu_parts(pre)
        if at <= sz.h < at + width:
            units = at + lax.broadcasted_iota(jnp.int32, (1, width), 1)
            act = jnp.where(units == sz.h, 1.0, act)
        acts.append(act.astype(bf16))
        store("act", slice(at, at + width), acts[-1])
        store("slope", slice(at, at + width), slope.astype(bf16))
    act = jnp.concatenate(acts, axis=1)
    return own + (mm(act, reduce_ref[...], NT) + outbias_ref[...])


def own_kernel(
    sz,
    height_ref,
    taps_ref,
    x_ref,
    prev_ref,
    next_ref,
    expand_ref,
    bias_ref,
    reduce_ref,
    gain_ref,
    outbias_ref,
    filter_ref,
    noisemix_ref,
    normed_ref,
    mx_ref,
    act_ref,
    dg_ref,
    pred_ref,
    n_ref,
    fil_ref,
):
    norm_and_filter(sz, 0, height_ref, taps_ref, x_ref, prev_ref, next_ref, gain_ref, filter_ref, normed_ref, n_ref, fil_ref)
    places = {"mixed": mx_ref, "act": act_ref, "slope": dg_ref}

    def store(name, cols, values):
        places[name][:, cols] = values

    pred_ref[...] = feed_forward(
        sz, 0, x_ref, fil_ref, expand_ref, bias_ref, reduce_ref, outbias_ref, noisemix_ref, store
    )


def filter_scratch(sz):
    return [pltpu.VMEM((4, sz.ct, sz.ext, 128), f32), pltpu.VMEM((sz.ct, sz.pe, 128), f32)]


def own_call(sz, height, taps, x, prev, after, weights):
    shape = jax.ShapeDtypeStruct
    outs = (
        shape((sz.m, 4, sz.ext, sz.cp), bf16),
        shape((sz.pe, sz.cp), bf16),
        shape((sz.pe, sz.hp), bf16),
        shape((sz.pe, sz.hp), bf16),
        shape((sz.pe, sz.cp), f32),
    )
    return pl.pallas_call(
        functools.partial(own_kernel, sz),
        grid=(1,),
        out_shape=outs,
        in_specs=[smem(), smem()] + [vmem()] * 10,
        out_specs=(pl.BlockSpec((1, 4, sz.ext, sz.cp), lambda i: (0, 0, 0, 0)),) + (vmem(),) * 4,
        scratch_shapes=filter_scratch(sz),
        compiler_params=pltpu.CompilerParams(vmem_limit_bytes=30 * 1024 * 1024),
        cost_estimate=cost(8),
        name="own",
    )(height, taps, x, prev, after, *weights)


def main_kernel(
    sz,
    height_ref,
    core_ref,
    taps_ref,
    bias_ref,
    gain_ref,
    outbias_ref,
    filter_ref,
    noisemix_ref,
    x_hbm,
    prev_hbm,
    next_hbm,
    target_hbm,
    expand_hbm,
    reduce_hbm,
    normed_own_hbm,
    mx_hbm,
    act_hbm,
    dg_hbm,
    pred_hbm,
    mine_hbm,
    other_hbm,
    bg_hbm,
    pg_hbm,
    normed_hbm,
    small_ref,
    x_ref,
    prev_ref,
    next_ref,
    target_ref,
    expand_ref,
    reduce_ref,
    mine_ref,
    other_ref,
    bg_ref,
    pg_ref,
    n_ref,
    fil_ref,
    nb_ref,
    mx_ref,
    act_ref,
    dg_ref,
    pred_ref,
    tr_ref,
    row_e_ref,
    row_r_ref,
    col_e_ref,
    col_r_ref,
    loss_ref,
    in_sems,
    out_sems,
):
    first = pl.ds(0, sz.pe)
    others = pl.ds(1, sz.m - 1)
    early = [
        pltpu.make_async_copy(x_hbm.at[others], x_ref, in_sems.at[0]),
        pltpu.make_async_copy(prev_hbm, prev_ref, in_sems.at[1]),
        pltpu.make_async_copy(next_hbm, next_ref, in_sems.at[2]),
    ]
    expand_load = pltpu.make_async_copy(expand_hbm, expand_ref, in_sems.at[3])
    reduce_load = pltpu.make_async_copy(reduce_hbm, reduce_ref, in_sems.at[4])
    loads = [
        pltpu.make_async_copy(mx_hbm, mx_ref.at[first], in_sems.at[5]),
        pltpu.make_async_copy(act_hbm, act_ref.at[first], in_sems.at[6]),
        pltpu.make_async_copy(dg_hbm, dg_ref.at[first], in_sems.at[7]),
        pltpu.make_async_copy(pred_hbm, pred_ref.at[0], in_sems.at[8]),
        pltpu.make_async_copy(target_hbm, target_ref, in_sems.at[9]),
    ]
    for load in (*early, expand_load, reduce_load, *loads):
        load.start()
    for load in early:
        load.wait()

    def forward(e, carry):
        norm_and_filter(
            sz, e, height_ref, taps_ref, x_ref, prev_ref, next_ref, gain_ref, filter_ref, nb_ref, n_ref, fil_ref
        )

        @pl.when(e == 0)
        def _():
            expand_load.wait()
            reduce_load.wait()

        rows = pl.ds(pl.multiple_of((e + 1) * sz.pe, 16), sz.pe)
        places = {"mixed": mx_ref, "act": act_ref, "slope": dg_ref}

        def store(name, cols, values):
            places[name][rows, cols] = values

        pred_ref[e + 1] = feed_forward(
            sz, e, x_ref, fil_ref, expand_ref, bias_ref, reduce_ref, outbias_ref, noisemix_ref, store
        )
        return carry

    lax.fori_loop(0, sz.m - 1, forward, 0)
    save = pltpu.make_async_copy(nb_ref, normed_hbm.at[pl.ds(1, sz.m - 1)], out_sems.at[0])
    save.start()
    for load in loads:
        load.wait()

    height = height_ref[0]
    lanes = lax.broadcasted_iota(jnp.int32, (1, sz.cp), 1)
    inside = (lanes < sz.c).astype(f32)
    loss_ref[...] = jnp.zeros_like(loss_ref)
    step = 16
    inv_m = 1.0 / sz.m
    inv_mm = inv_m * inv_m

    def score(i, carry):
        at = pl.multiple_of(i * step, step)
        pixel = at + lax.broadcasted_iota(jnp.int32, (step, 1), 0)
        row = (pixel >= sz.pr).astype(jnp.int32)
        use = (pixel - row * sz.pr < sz.q) & (row < height)
        mask_rows = use.astype(f32)
        for ct in range(sz.ct):
            cols = slice(ct * 128, (ct + 1) * 128)
            mask = mask_rows * inside[:, cols]
            preds = [pred_ref[e, pl.ds(at, step), cols] for e in range(sz.m)]
            truth = target_ref[pl.ds(at, step), cols].astype(f32)
            slopes = []
            own_sum = 0.0
            for p in preds:
                d = p - truth
                q = d * d + 1.0
                r = lax.rsqrt(q)
                own_sum = own_sum + q * r
                slopes.append(d * r * inv_m)
            pair_sum = 0.0
            pairs = [0.0] * sz.m
            for a in range(sz.m):
                for b in range(a + 1, sz.m):
                    d = preds[a] - preds[b]
                    q = d * d + 1.0
                    r = lax.rsqrt(q)
                    pair_sum = pair_sum + q * r
                    s = d * r
                    pairs[a] = pairs[a] + s
                    pairs[b] = pairs[b] - s
            value = own_sum * inv_m - (pair_sum + 0.5 * sz.m) * inv_mm
            value = mask * value
            loss_ref[:, cols] += value[0:8] + value[8:16]
            for e in range(sz.m):
                g = (mask * (slopes[e] - pairs[e] * inv_mm)).astype(bf16)
                where = pl.ds(pl.multiple_of(e * sz.pe + at, 16), step)
                bg_ref[where, cols] = g
        return carry

    lax.fori_loop(0, sz.pe // step, score, 0)
    core = core_ref[0]
    saves = [save]

    def write(here, there, which):
        saves.append(pltpu.make_async_copy(here, there, out_sems.at[which]))
        saves[-1].start()

    write(bg_ref, bg_hbm, 1)
    weight_grad(sz, core, bg_ref, act_ref, tr_ref, mine_ref.at[1], other_ref.at[1], row_r_ref, col_r_ref)
    write(mine_ref.at[1], mine_hbm.at[1], 2)
    write(other_ref.at[1], other_hbm.at[1], 3)


    def backward(e, carry):
        rows = pl.ds(pl.multiple_of(e * sz.pe, 16), sz.pe)
        bg = bg_ref[rows, :]
        for at, width in column_blocks(sz.hp, 256):
            grad = mm(bg, reduce_ref[:, at : at + width])
            pre = (grad * dg_ref[rows, at : at + width].astype(f32)).astype(bf16)
            pg_ref[rows, at : at + width] = pre
        return carry

    lax.fori_loop(0, sz.m, backward, 0)
    write(pg_ref, pg_hbm, 4)
    weight_grad(sz, core, mx_ref, pg_ref, tr_ref, mine_ref.at[0], other_ref.at[0], row_e_ref, col_e_ref)
    write(other_ref.at[0], other_hbm.at[0], 5)
    write(mine_ref.at[0], mine_hbm.at[0], 6)
    at = Rows(sz)
    small_ref[...] = jnp.zeros_like(small_ref)
    lane = lax.broadcasted_iota(jnp.int32, (1, sz.mc), 1)
    half = sz.mh // 2

    def column_sum(ref):
        return jnp.sum(ref[...], axis=0, keepdims=True)

    def long_row(row, place, values, extra):
        small_ref[row : row + 1, :] = values[:, :half]
        small_ref[row + 1 : row + 2, :] = values[:, half : sz.mh]
        for i in range(at.spare):
            extra = jnp.where(lane == place + i, values[:, sz.mh + i : sz.mh + i + 1], extra)
        return extra

    extra = jnp.zeros((1, sz.mc), f32)
    outbias_grad = col_r_ref[at.spare : at.spare + 1, :]
    small_ref[at.outbias : at.outbias + 1, :] = outbias_grad[:, : sz.mc]
    extra = jnp.where(lane == at.x_outbias, outbias_grad[:, sz.mc : sz.mc + 1], extra)
    extra = long_row(at.biasin, at.x_biasin, row_e_ref[sz.c - sz.mc : sz.c - sz.mc + 1, :], extra)
    extra = long_row(at.row_e, at.x_row_e, row_e_ref[0:1, :], extra)
    extra = long_row(at.row_r, at.x_row_r, row_r_ref[0:1, :], extra)
    small_ref[at.col_e : at.col_e + at.spare, :] = col_e_ref[: at.spare, : sz.mc]
    small_ref[at.col_r : at.col_r + at.spare, :] = col_r_ref[: at.spare, : sz.mc]
    extra = jnp.where(lane == at.x_loss, jnp.sum(column_sum(loss_ref), axis=1, keepdims=True), extra)
    small_ref[at.extra : at.extra + 1, :] = extra
    for save in saves:
        save.wait()


def main_call(sz, height, core, taps, x, prev, after, target, weights, state):
    shape = jax.ShapeDtypeStruct
    half = shape((2, sz.mc, sz.mh // 2), bf16)
    outs = (
        half,
        half,
        shape((sz.p, sz.cp), bf16),
        shape((sz.p, sz.hp), bf16),
        shape((sz.m, 4, sz.ext, sz.cp), bf16),
        shape((Rows(sz).count, sz.mc), f32),
    )
    anywhere = pl.BlockSpec(memory_space=pl.ANY)
    expand, bias, reduce, gain, outbias, filt, noisemix = weights
    return pl.pallas_call(
        functools.partial(main_kernel, sz),
        out_shape=outs,
        in_specs=[smem()] * 3 + [vmem()] * 5 + [anywhere] * 11,
        out_specs=(anywhere,) * 5 + (vmem(),),
        input_output_aliases={14: 4},
        scratch_shapes=[
            pltpu.VMEM((sz.m - 1, 2, sz.ext, sz.cp), bf16),
            pltpu.VMEM((sz.m - 1, sz.ext, sz.cp), bf16),
            pltpu.VMEM((sz.m - 1, sz.ext, sz.cp), bf16),
            pltpu.VMEM((sz.pe, sz.cp), bf16),
            pltpu.VMEM((sz.cp, sz.hp), bf16),
            pltpu.VMEM((sz.cp, sz.hp), bf16),
            pltpu.VMEM((2, sz.mc, sz.mh // 2), bf16),
            pltpu.VMEM((2, sz.mc, sz.mh // 2), bf16),
            pltpu.VMEM((sz.p, sz.cp), bf16),
            pltpu.VMEM((sz.p, sz.hp), bf16),
            *filter_scratch(sz),
            pltpu.VMEM((sz.m - 1, 4, sz.ext, sz.cp), bf16),
            pltpu.VMEM((sz.p, sz.cp), bf16),
            pltpu.VMEM((sz.p, sz.hp), bf16),
            pltpu.VMEM((sz.p, sz.hp), bf16),
            pltpu.VMEM((sz.m, sz.pe, sz.cp), f32),
            pltpu.VMEM((sz.cr, sz.p), bf16),
            pltpu.VMEM((sz.cr - sz.mc, sz.hp), f32),
            pltpu.VMEM((sz.cr - sz.mc, sz.hp), f32),
            pltpu.VMEM((16, sz.cp), f32),
            pltpu.VMEM((16, sz.cp), f32),
            pltpu.VMEM((8, sz.cp), f32),
            pltpu.SemaphoreType.DMA((10,)),
            pltpu.SemaphoreType.DMA((7,)),
        ],
        compiler_params=pltpu.CompilerParams(vmem_limit_bytes=50 * 1024 * 1024),
        cost_estimate=cost(40),
        name="main",
    )(height, core, taps, bias, gain, outbias, filt, noisemix, x, prev, after, target, expand, reduce, *state)


def unmix_kernel(
    sz,
    base,
    count,
    height_ref,
    taps_ref,
    filter_ref,
    small_in_ref,
    pg_hbm,
    x_hbm,
    normed_hbm,
    expand_hbm,
    gn_own_hbm,
    gn_prev_hbm,
    gn_next_hbm,
    small_ref,
    pg_ref,
    x_ref,
    normed_ref,
    expand_ref,
    own_ref,
    edge_ref,
    filter_grad_ref,
    mixing_grad_ref,
    n_ref,
    gn_ref,
    gm_ref,
    in_sems,
    out_sems,
):
    below_first = jnp.where(height_ref[0] == 2, 2, 3)
    sources = ((0, 1, below_first), (1, 2, 3))
    last = sz.ct - 1
    weights = pltpu.make_async_copy(expand_hbm, expand_ref, in_sems.at[0])
    weights.start()
    loads = []
    for e in range(count):
        rows = pl.ds((base + e) * sz.pe, sz.pe)
        channels = pl.ds(last * 128, 128)
        loads.append(
            (
                pltpu.make_async_copy(pg_hbm.at[rows], pg_ref.at[e], in_sems.at[3 * e + 1]),
                pltpu.make_async_copy(x_hbm.at[base + e, :, :, channels], x_ref.at[e], in_sems.at[3 * e + 2]),
                pltpu.make_async_copy(normed_hbm.at[base + e], normed_ref.at[e], in_sems.at[3 * e + 3]),
            )
        )
        for load in loads[e]:
            load.start()
    filter_grad_ref[...] = jnp.zeros_like(filter_grad_ref)
    mixing_grad_ref[...] = jnp.zeros_like(mixing_grad_ref)
    pad = 2 * REACH
    for r in range(2):
        for ct in range(sz.ct):
            gm_ref[r, ct, :pad, :] = jnp.zeros((pad, 128), f32)
            gm_ref[r, ct, pad + sz.pr :, :] = jnp.zeros((sz.ext + REACH - sz.pr, 128), f32)
    weights.wait()
    stores = []
    for e in range(count):
        for load in loads[e]:
            load.wait()
        gm = mm(pg_ref[e], expand_ref[...], NT)
        for r in range(2):
            for ct in range(sz.ct):
                gm_ref[r, ct, pad : pad + sz.pr, :] = gm[r * sz.pr : (r + 1) * sz.pr, ct * 128 : (ct + 1) * 128]
        for row in range(4):
            normed = normed_ref[e, row].astype(f32)
            for ct in range(sz.ct):
                n_ref[row, ct] = normed[:, ct * 128 : (ct + 1) * 128]
        noise = jnp.concatenate([x_ref[e, r].astype(f32)[REACH : REACH + sz.pr] for r in range(2)], axis=0)
        mixing_grad_ref[...] += mm(noise.T[0:16].astype(bf16), gm.astype(bf16))

        def unfilter_tile(ct, c):
            def gathered(*readers):
                acc = jnp.zeros((sz.ext, 128), f32)
                for r, a in readers:
                    for tap in range(3 * a, 3 * a + 3):
                        start = REACH - taps_ref[tap, r]
                        acc = acc + filter_ref[ct, tap : tap + 1, :] * gm_ref[r, ct, pl.ds(start, sz.ext), :]
                return acc

            gn_ref[0, ct] = gathered((0, 0))
            gn_ref[1, ct] = gathered((0, 1), (1, 0))
            gn_ref[2, ct] = gathered((1, 1))
            gn_ref[3, ct] = gathered((1, 2))
            gn_ref[below_first, ct] += gathered((0, 2))
            for r in range(2):
                g = gm_ref[r, ct, pad : pad + sz.pr, :]
                for a in range(3):
                    for tap in range(3 * a, 3 * a + 3):
                        read = n_ref[sources[r][a], ct, pl.ds(taps_ref[tap, r] + REACH, sz.pr), :]
                        filter_grad_ref[ct, tap] += tile_sum(g * read)
            return c

        lax.fori_loop(0, sz.ct, unfilter_tile, 0)
        for ct in range(sz.ct):
            cols = slice(ct * 128, (ct + 1) * 128)
            edge_ref[e, 0, :, cols] = gn_ref[0, ct].astype(bf16)
            edge_ref[e, 1, :, cols] = gn_ref[3, ct].astype(bf16)
            own_ref[e, 0, :, cols] = gn_ref[1, ct].astype(bf16)
            own_ref[e, 1, :, cols] = gn_ref[2, ct].astype(bf16)
        stores += [
            pltpu.make_async_copy(own_ref.at[e], gn_own_hbm.at[e], out_sems.at[3 * e]),
            pltpu.make_async_copy(edge_ref.at[e, 0], gn_prev_hbm.at[e], out_sems.at[3 * e + 1]),
            pltpu.make_async_copy(edge_ref.at[e, 1], gn_next_hbm.at[e], out_sems.at[3 * e + 2]),
        ]
        for store in stores[-3:]:
            store.start()

    at = Rows(sz)
    lane = lax.broadcasted_iota(jnp.int32, (1, sz.mc), 1)
    small_ref[...] = small_in_ref[...]
    extra = small_in_ref[at.extra : at.extra + 1, :]
    first = sz.c - last * 128
    for tap in range(9):
        for ct in range(last):
            row = jnp.sum(filter_grad_ref[ct, tap], axis=0, keepdims=True)
            small_ref[tap : tap + 1, ct * 128 : (ct + 1) * 128] += row
        row = jnp.sum(filter_grad_ref[last, tap], axis=0, keepdims=True)
        extra = extra + jnp.where(lane == tap, row[:, 0:1], 0.0)
    mixing = mixing_grad_ref[first : first + sz.k, :]
    small_ref[at.mixing : at.mixing + sz.k, :] += mixing[:, : sz.mc]
    for i in range(sz.k):
        extra = extra + jnp.where(lane == at.x_mixing + i, mixing[i : i + 1, sz.mc : sz.mc + 1], 0.0)
    small_ref[at.extra : at.extra + 1, :] = extra
    for store in stores:
        store.wait()


def unmix_call(sz, base, count, height, taps, pg, x, normed, expand, filt, small):
    shape = jax.ShapeDtypeStruct
    outs = (
        shape((count, 2, sz.ext, sz.cp), bf16),
        shape((count, sz.ext, sz.cp), bf16),
        shape((count, sz.ext, sz.cp), bf16),
        shape(small.shape, f32),
    )
    anywhere = pl.BlockSpec(memory_space=pltpu.HBM)
    return pl.pallas_call(
        functools.partial(unmix_kernel, sz, base, count),
        out_shape=outs,
        in_specs=[smem(), smem(), vmem(), vmem()] + [anywhere] * 4,
        out_specs=(anywhere,) * 3 + (vmem(),),
        scratch_shapes=[
            pltpu.VMEM((count, sz.pe, sz.hp), bf16),
            pltpu.VMEM((count, 2, sz.ext, 128), bf16),
            pltpu.VMEM((count, 4, sz.ext, sz.cp), bf16),
            pltpu.VMEM((sz.cp, sz.hp), bf16),
            pltpu.VMEM((count, 2, sz.ext, sz.cp), bf16),
            pltpu.VMEM((count, 2, sz.ext, sz.cp), bf16),
            pltpu.VMEM((sz.ct, 9, 8, 128), f32),
            pltpu.VMEM((16, sz.cp), f32),
            pltpu.VMEM((4, sz.ct, sz.ext, 128), f32),
            pltpu.VMEM((4, sz.ct, sz.ext, 128), f32),
            pltpu.VMEM((2, sz.ct, sz.ext + 3 * REACH, 128), f32),
            pltpu.SemaphoreType.DMA((3 * count + 1,)),
            pltpu.SemaphoreType.DMA((3 * count,)),
        ],
        compiler_params=pltpu.CompilerParams(vmem_limit_bytes=50 * 1024 * 1024),
        cost_estimate=cost(5 * count),
        name="unmix",
    )(height, taps, filt, small, pg, x, normed, expand)


def norm_back_kernel(sz, height_ref, x_ref, gn_ref, up_ref, down_ref, bg_ref, gain_ref, out_ref):
    height = height_ref[0]
    lanes = lax.broadcasted_iota(jnp.int32, (1, sz.cp), 1)
    from_up = up_ref[0].astype(f32)
    from_down = down_ref[0].astype(f32)
    direct = bg_ref[...].astype(f32)
    for r in range(2):
        centred, inv = norm_rows(x_ref[0, r].astype(f32), sz.c, lanes)
        xhat = centred * inv
        g = gn_ref[0, r].astype(f32) + jnp.where(height == r + 1, from_down, 0.0)
        if r == 0:
            g = g + from_up
        q = g * gain_ref[...]
        mean_q = jnp.sum(q, axis=1, keepdims=True) * (1.0 / sz.c)
        mean_qx = jnp.sum(q * xhat, axis=1, keepdims=True) * (1.0 / sz.c)
        result = (q - mean_q - xhat * mean_qx) * inv
        part = result[REACH : REACH + sz.pr] + direct[r * sz.pr : (r + 1) * sz.pr]
        pieces = [result[:REACH], part, result[REACH + sz.pr :]]
        out_ref[0, r] = jnp.concatenate(pieces, axis=0).astype(bf16)


def norm_back_call(sz, base, count, height, x, gn, up, down, bg, gain):
    return pl.pallas_call(
        functools.partial(norm_back_kernel, sz),
        grid=(count,),
        out_shape=jax.ShapeDtypeStruct((count, 2, sz.ext, sz.cp), bf16),
        in_specs=[
            smem(),
            pl.BlockSpec((1, 2, sz.ext, sz.cp), lambda i: (i + base, 0, 0, 0)),
            pl.BlockSpec((1, 2, sz.ext, sz.cp), lambda i: (i, 0, 0, 0)),
            pl.BlockSpec((1, sz.ext, sz.cp), lambda i: (i, 0, 0)),
            pl.BlockSpec((1, sz.ext, sz.cp), lambda i: (i, 0, 0)),
            pl.BlockSpec((sz.pe, sz.cp), lambda i: (i + base, 0)),
            pl.BlockSpec((1, sz.cp), lambda i: (0, 0)),
        ],
        out_specs=pl.BlockSpec((1, 2, sz.ext, sz.cp), lambda i: (i, 0, 0, 0)),
        compiler_params=pltpu.CompilerParams(vmem_limit_bytes=28 * 1024 * 1024),
        cost_estimate=cost(2 * count),
        name="norm_back",
    )(height, x, gn, up, down, bg, gain)


def adam_kernel(sz, limit, pixels, members, stacks, place_ref, heights_ref, *refs):
    mine_ref, got_ref, small_mine_ref, small_got_ref = refs[:4]
    ins, small_ins, (norm_ref, mean_ref) = refs[4:10], refs[10:22], refs[22:24]
    outs, small_outs = refs[24:32], refs[32:44]
    factor_ref, small_ref, column_ref, cols_ref, gain_ref = refs[44:]
    at = Rows(sz)
    step = pl.program_id(0)
    core, member, stack = place_ref[0], place_ref[1], place_ref[2]
    half = sz.mh // 2
    each = sz.mc // members
    rows = sz.piece_rows(members, stacks)

    def wide(row, count, place):
        return jnp.concatenate([small_ref[row : row + count, :], column_ref[place : place + count, 0:1]], axis=1)

    def long(row, place):
        extra = small_ref[at.extra : at.extra + 1, place : place + at.spare]
        return jnp.concatenate([small_ref[row : row + 1, :], small_ref[row + 1 : row + 2, :], extra], axis=1)

    @pl.when(step == 0)
    def _():
        part = at.count // 2
        for which, ref in ((core, small_mine_ref), (1 - core, small_got_ref)):
            where = pl.ds(pl.multiple_of(which * part, part), part)
            values = ref[...].astype(f32)
            small_ref[where, :] = values[:part] + values[part:]
        extra = small_ref[at.extra : at.extra + 1, 0:128]
        column_ref[...] = jnp.broadcast_to(extra, (8, 128)).T
        total = jnp.zeros((8, half), f32)
        for ref in (mine_ref, got_ref):

            def body(i, acc):
                values = ref[i].astype(f32)
                values = values * values
                for j in range(0, rows, 8):
                    acc = acc + values[j : j + 8]
                return acc

            total = lax.fori_loop(0, 2 * members * stacks, body, total)
        count = jnp.sum(total)
        filter_grad = wide(0, 9, 0)
        gain_row = jnp.sum(small_ins[0][...] * filter_grad, axis=0, keepdims=True) / small_ins[6][0:1, :]
        gain_ref[...] = gain_row
        cols = small_ref[at.col_e : at.extra, :]
        for values in (
            filter_grad,
            wide(at.mixing, sz.k, at.x_mixing),
            gain_row,
            wide(at.outbias, 1, at.x_outbias),
            long(at.biasin, at.x_biasin),
            long(at.row_e, at.x_row_e),
            long(at.row_r, at.x_row_r),
            cols,
        ):
            count = count + jnp.sum(values * values)
        norm = jnp.sqrt(jnp.full((8, 128), count, f32))
        factor_ref[...] = jnp.minimum(1.0, limit / (norm + 1e-06))
        live = heights_ref[0]
        for i in range(1, heights_ref.shape[0]):
            live = live + heights_ref[i]
        loss = column_ref[at.x_loss : at.x_loss + 1, 0:1]
        mean = loss / (jnp.full((8, 128), pixels, f32) * live.astype(f32))
        norm_ref[0] = norm[0, 0]
        mean_ref[0] = mean[0, 0]
        cols_ref[...] = jnp.concatenate([cols, jnp.zeros((8 - 2 * at.spare, sz.mc), f32)], axis=0).T

    factor = factor_ref[0:1, 0:1]

    def adam(w, g, m, v, rate):
        g = factor * g
        m_new = BETA_ONE * m + (1.0 - BETA_ONE) * g
        v_new = BETA_TWO * v + (1.0 - BETA_TWO) * g * g
        m_hat = m_new / (1.0 - BETA_ONE**STEP)
        v_hat = v_new / (1.0 - BETA_TWO**STEP)
        return w - rate * (m_hat / (jnp.sqrt(v_hat) + ADAM_EPS) + DECAY_RATE * w), m_new, v_new

    kinds = ((0, at.row_e, at.x_row_e, sz.c**-0.5), (1, at.row_r, at.x_row_r, sz.h**-0.5))

    @pl.when(step < sz.mc // ROWS)
    def _():
        first_core = core == 0
        for i in range(ROWS // rows):
            first = step * ROWS + i * rows
            t = member ^ (first // each)
            s = stack ^ ((first % each) // rows)
            where = pl.ds(pl.multiple_of(first, 8), rows)
            to = slice(i * rows, (i + 1) * rows)
            for kind, _, _, rate in kinds:
                slot = (t * stacks + s) * 2 + kind
                mine = mine_ref[slot].astype(f32)
                got = got_ref[slot].astype(f32)
                low = jnp.where(first_core, mine, got)
                high = jnp.where(first_core, got, mine)
                cols = cols_ref[where, kind * at.spare : (kind + 1) * at.spare]
                g = jnp.concatenate([low, high, cols], axis=1)
                w_ref, m_ref, v_ref = ins[3 * kind : 3 * kind + 3]
                w_out, m_out, v_out, c_out = outs[4 * kind : 4 * kind + 4]
                at_rows = where if kind == 0 else to
                w, m, v = adam(w_ref[at_rows, :], g, m_ref[at_rows, :], v_ref[at_rows, :], rate)
                w_out[to, :] = w
                m_out[to, :] = m
                v_out[to, :] = v
            if (i + 1) * rows % 16 == 0:
                both = slice((i + 1) * rows // 16 * 16 - max(16, rows * 2), (i + 1) * rows)
                for kind in range(2):
                    outs[4 * kind + 3][both, :] = outs[4 * kind][both, :].astype(bf16)

    @pl.when(step == sz.mc // ROWS)
    def _():
        for kind, row, place, rate in kinds:
            last = slice(sz.mc, sz.c) if kind == 0 else slice(0, 1)
            w_ref, m_ref, v_ref = ins[3 * kind : 3 * kind + 3]
            w_out, m_out, v_out, c_out = outs[4 * kind : 4 * kind + 4]
            w, m, v = adam(w_ref[last, :], long(row, place), m_ref[last, :], v_ref[last, :], rate)
            w_out[0:1, :] = w
            m_out[0:1, :] = m
            v_out[0:1, :] = v
            c_out[0:16, :] = jnp.broadcast_to(w, (16, sz.h)).astype(bf16)

    @pl.when(step == 0)
    def _():
        grads = (
            wide(0, 9, 0),
            wide(at.mixing, sz.k, at.x_mixing),
            jnp.concatenate([gain_ref[...], wide(at.outbias, 1, at.x_outbias)], axis=0),
            long(at.biasin, at.x_biasin),
        )
        for i, g in enumerate(grads):
            new = adam(small_ins[3 * i][...], g, small_ins[3 * i + 1][...], small_ins[3 * i + 2][...], SMALL_RATE)
            for ref, values in zip(small_outs[3 * i : 3 * i + 3], new):
                ref[...] = values


ROWS = 80


def adam_call(sz, limit, pixels, members, stacks, place, heights, grads, weights, small_weights):
    shape = jax.ShapeDtypeStruct
    full = shape((sz.c, sz.h), f32)
    low = shape((sz.c, sz.h), bf16)
    outs = (shape((1,), f32),) * 2 + (full, full, full, low) * 2 + tuple(shape(v.shape, f32) for v in small_weights)
    block = pl.BlockSpec((ROWS, sz.h), lambda i: (i, 0))
    steps = sz.mc // ROWS + 1
    return pl.pallas_call(
        functools.partial(adam_kernel, sz, limit, pixels, members, stacks),
        grid=(steps,),
        out_shape=outs,
        in_specs=[smem()] * 2 + [vmem()] * (4 + 3) + [block] * 3 + [vmem()] * 12,
        out_specs=(smem(),) * 2 + (block,) * 8 + (vmem(),) * 12,
        scratch_shapes=[
            pltpu.VMEM((8, 128), f32),
            pltpu.VMEM((Rows(sz).count, sz.mc), f32),
            pltpu.VMEM((128, 8), f32),
            pltpu.VMEM((sz.mc, 8), f32),
            pltpu.VMEM((1, sz.c), f32),
        ],
        compiler_params=pltpu.CompilerParams(vmem_limit_bytes=24 * 1024 * 1024),
        cost_estimate=cost(16),
        name="adam",
    )(place, heights, *grads, *weights, *small_weights)


def exchange(pieces, axis, count, shifts):
    return [
        piece if s == 0 else lax.ppermute(piece, axis, [(i, i ^ s) for i in range(count)])
        for piece, s in zip(pieces, shifts)
    ]


def scatter_over(values, axis, count, size):
    me = lax.axis_index(axis)
    values = jnp.pad(values, ((0, 0), (0, count * size - values.shape[1]), (0, 0)))
    pieces = [lax.dynamic_slice_in_dim(values, (me ^ s) * size, size, axis=1) for s in range(count)]
    return exchange(pieces, axis, count, range(count))


def added(parts):
    return sum(part.astype(f32) for part in parts).astype(bf16)


def two_parts(values):
    coarse = lax.reduce_precision(values, exponent_bits=8, mantissa_bits=7)
    return coarse.astype(bf16), (values - coarse).astype(bf16)


def after_all(values, *others):
    return lax.optimization_barrier((values, others))[0]


def pad_to(values, shape):
    return jnp.pad(values, [(0, n - m) for n, m in zip(shape, values.shape)])


def on_device(
    fields,
    noise_fields,
    target_fields,
    band_heights,
    tap_offsets,
    expand_weight,
    expand_bias,
    reduce_weight,
    channel_vectors,
    disco_filter,
    noise_mixing,
    first_expand,
    second_expand,
    first_bias,
    second_bias,
    first_reduce,
    second_reduce,
    first_vectors,
    second_vectors,
    first_filter,
    second_filter,
    first_mixing,
    second_mixing,
):
    members = lax.axis_size("member")
    stacks = lax.axis_size("stack")
    lat_count = 2 * stacks
    lat = ("stack", "core")
    channels, hidden = expand_weight.shape
    lon = fields.shape[3]
    sz = Sizes(members, channels, hidden, noise_fields.shape[1], lon)
    me = lax.axis_index("member")
    core = lax.axis_index("core")
    band = lax.axis_index("stack") * 2 + core
    height = lax.dynamic_slice_in_dim(band_heights, band, 1)

    shifts = [0, members - 1, *range(1, members - 1)]
    pieces = split_call(sz, shifts, height, me.reshape(1), fields, noise_fields)
    arrived = exchange(pieces, "member", members, shifts)
    upward = [(i, i + 1) for i in range(lat_count - 1)]
    downward = [(i + 1, i) for i in range(lat_count - 1)]

    def edges(rows):
        bottom = jnp.stack([x[1] for x in rows])
        top = jnp.stack([x[0] for x in rows])
        return lax.ppermute(bottom, lat, upward), lax.ppermute(top, lat, downward)

    truth = pad_to(target_fields, (channels, 2, lon + sz.pr - sz.q))
    truth = lax.dynamic_slice_in_dim(truth, me * sz.q, sz.pr, axis=2)
    truth = pad_to(jnp.transpose(truth, (1, 2, 0)), (2, sz.pr, sz.cp)).reshape(sz.pe, sz.cp)

    expand_low = pad_to(expand_weight.astype(bf16), (sz.cp, sz.hp))
    reduce_low = pad_to(reduce_weight.T.astype(bf16), (sz.cp, sz.hp))
    bias = pad_to(expand_bias[None], (1, sz.hp))
    gain = pad_to(channel_vectors[0:1], (1, sz.cp))
    outbias = pad_to(channel_vectors[1:2], (1, sz.cp))
    filt = jnp.transpose(pad_to(disco_filter, (16, sz.cp)).reshape(16, sz.ct, 128), (1, 0, 2))
    spot = channels - (sz.ct - 1) * 128
    coarse, fine = two_parts(noise_mixing)
    noisemix = jnp.zeros((256, sz.cp), bf16)
    noisemix = noisemix.at[spot : spot + sz.k, :channels].set(coarse)
    noisemix = noisemix.at[128 + spot : 128 + spot + sz.k, :channels].set(fine)

    weights = (expand_low, bias, reduce_low, gain, outbias, filt, noisemix)
    core_id = core.reshape(1)
    own_edges = edges(after_all(arrived[:1], weights, truth))
    state = own_call(sz, height, tap_offsets, arrived[0][None], *own_edges, weights)
    others = after_all(arrived[1:], state)
    other_edges = edges(others)
    x = jnp.stack([arrived[0], *others])
    mine, other, bg, pg, normed, small = main_call(
        sz, height, core_id, tap_offsets, x, *other_edges, truth, weights, state
    )

    swap = [(0, 1), (1, 0)]
    part = (mine.astype(f32) + lax.ppermute(other, "core", swap).astype(f32)).astype(bf16)
    cut = members // 2

    def unmix_raw(base, count, pg, small):
        gn, gn_prev, gn_next, small = unmix_call(
            sz, base, count, height, tap_offsets, pg, x, normed, expand_low, filt, small
        )
        return (gn, gn_prev, gn_next), small

    def edges_back(raw):
        gn, gn_prev, gn_next = raw
        return gn, lax.ppermute(gn_next, lat, upward), lax.ppermute(gn_prev, lat, downward)

    def unmix(base, count, pg, small):
        raw, small = unmix_raw(base, count, pg, small)
        return edges_back(raw), small, raw[1]

    arriving = scatter_over(part, "member", members, sz.mc // members)
    near, small, done = unmix(0, cut, after_all(pg, part), small)
    far_raw, small = unmix_raw(cut, members - cut, after_all(pg, done), small)

    arriving, far_raw, small = after_all((arriving, far_raw, small))
    arriving = scatter_over(added(arriving), "stack", stacks, sz.piece_rows(members, stacks))
    near_grads = norm_back_call(sz, 0, cut, height, x, *near, bg, gain)
    small = small.reshape(2, -1, sz.mc)
    other_small = lax.dynamic_index_in_dim(small, 1 - core, 0, keepdims=False)
    small = lax.dynamic_index_in_dim(small, core, 0, keepdims=False) + lax.ppermute(other_small, "core", swap)

    def packed(main, small):
        return jnp.concatenate([main, *two_parts(small)], axis=0)

    def unpacked(messages):
        cut = messages[0].shape[0] - at.count
        half = at.count // 2
        parts = [m[cut:].astype(f32) for m in messages]
        return jnp.concatenate([m[:cut] for m in messages], axis=0), sum(p[:half] + p[half:] for p in parts)

    at = Rows(sz)
    arriving, far_raw, near_grads, small = after_all((arriving, far_raw, near_grads, small))
    message = packed(added(arriving).reshape(-1, sz.mh // 2), small)
    gathered = exchange([message] * stacks, "stack", stacks, range(stacks))
    returned = exchange([near_grads[s] for s in range(cut)], "member", members, shifts[:cut])

    gathered, far_raw = after_all((gathered, far_raw))
    message = packed(*unpacked(gathered))
    gathered = exchange([message] * members, "member", members, range(members))
    far = edges_back(far_raw)

    far_grads = norm_back_call(sz, cut, members - cut, height, x, *far, bg, gain)
    far_pieces = [far_grads[s] for s in range(members - cut)]

    gathered, far_pieces = after_all((gathered, far_pieces))
    mine, small = unpacked(gathered)
    small = packed(mine[:0], small)
    got = lax.ppermute(mine, "core", swap)
    got_small = lax.ppermute(small, "core", swap)
    returned = returned + exchange(after_all(far_pieces, got), "member", members, shifts[cut:])
    pieces = [v.reshape(-1, sz.piece_rows(members, stacks), sz.mh // 2) for v in (mine, got)]

    limit = 0.02 * math.sqrt(hidden * channels * lat_count * 2 * lon / members)
    norm, mean, we, m_e, v_e, c_e, wr, m_r, v_r, c_r, *rest = adam_call(
        sz,
        limit,
        channels * lon,
        members,
        stacks,
        jnp.stack([core, me, lax.axis_index("stack")]),
        band_heights,
        (*pieces, small, got_small),
        (expand_weight, first_expand, second_expand, reduce_weight.T, first_reduce.T, second_reduce.T),
        (
            disco_filter,
            first_filter,
            second_filter,
            noise_mixing,
            first_mixing,
            second_mixing,
            channel_vectors,
            first_vectors,
            second_vectors,
            expand_bias[None],
            first_bias[None],
            second_bias[None],
        ),
    )
    input_gradient = join_call(sz, shifts, me.reshape(1), after_all(returned, norm))
    return (
        mean[0],
        input_gradient,
        norm[0],
        we,
        m_e,
        v_e,
        rest[9][0],
        rest[10][0],
        rest[11][0],
        wr.T,
        m_r.T,
        v_r.T,
        *rest[6:9],
        *rest[0:3],
        *rest[3:6],
        c_e,
        c_r.T,
    )


def solution(mesh):
    members = mesh.shape["member"]
    lat = mesh.shape["lat"]
    split = Mesh(mesh.devices.reshape(members, lat // 2, 2), ("member", "stack", "core"))
    rows = ("stack", "core")
    whole = [P()] * 18
    in_specs = (
        P("member", None, rows, None),
        P("member", None, rows, None),
        P(None, rows, None),
        P(),
        P(None, rows),
        *whole,
    )
    out_specs = (P(), P("member", None, rows, None)) + (P(),) * 21
    return jax.shard_map(on_device, mesh=split, in_specs=in_specs, out_specs=out_specs, check_vma=False)
```

```python
import functools
import math

import jax
import jax.numpy as jnp
from jax import lax
from jax.experimental import pallas as pl
from jax.experimental.pallas import tpu as pltpu
from jax.sharding import Mesh, PartitionSpec as P

STEP = 10
BETA_ONE = 0.9
BETA_TWO = 0.95
ADAM_EPS = 1e-08
DECAY_RATE = 0.1
NORM_EPS = 1e-05
SMALL_RATE = 0.3
REACH = 8
f32 = jnp.float32
bf16 = jnp.bfloat16

NN = (((1,), (0,)), ((), ()))
NT = (((1,), (1,)), ((), ()))
TN = (((0,), (0,)), ((), ()))


def round_up(value, step):
    return -(-value // step) * step


def mm(a, b, dims=NN):
    return lax.dot_general(a, b, dims, preferred_element_type=f32)


class Sizes:
    def __init__(self, members, channels, hidden, noise, lon):
        self.m = members
        self.c = channels
        self.h = hidden
        self.k = noise
        self.lon = lon
        self.q = lon // members
        self.pr = round_up(self.q, 8)
        self.ext = round_up(self.pr + 2 * REACH, 16)
        self.pe = 2 * self.pr
        self.p = members * self.pe
        self.cp = round_up(channels + noise, 128)
        self.ct = self.cp // 128
        self.cr = round_up(channels, 16)
        self.hp = round_up(hidden, 128)
        self.mc = channels // 128 * 128
        self.mh = hidden // 256 * 256

    def piece_rows(self, members, stacks):
        each = self.mc // members
        return next(n for n in range(8, each + 1, 8) if each % n == 0 and n * stacks >= each)


class Rows:
    def __init__(self, sz):
        self.mixing = 9
        self.outbias = self.mixing + sz.k
        self.biasin = self.outbias + 1
        self.row_e = self.biasin + 2
        self.row_r = self.row_e + 2
        self.spare = sz.h - sz.mh
        self.col_e = self.row_r + 2
        self.col_r = self.col_e + self.spare
        self.extra = self.col_r + self.spare
        self.count = round_up(self.extra + 1, 32)
        self.x_mixing = 9
        self.x_outbias = self.x_mixing + sz.k
        self.x_biasin = self.x_outbias + 1
        self.x_row_e = self.x_biasin + self.spare
        self.x_row_r = self.x_row_e + self.spare
        self.x_loss = self.x_row_r + self.spare


def smem():
    return pl.BlockSpec(memory_space=pltpu.SMEM)


def vmem():
    return pl.BlockSpec(memory_space=pltpu.VMEM)


def tile_sum(values):
    tiles = [values[i : i + 8] for i in range(0, values.shape[0], 8)]
    while len(tiles) > 1:
        tiles = [a + b for a, b in zip(tiles[::2], tiles[1::2])] + tiles[len(tiles) // 2 * 2 :]
    return tiles[0]


def column_blocks(width, step):
    return [(i, min(step, width - i)) for i in range(0, width, step)]


def norm_rows(values, channels, lanes):
    inside = lanes < channels
    values = jnp.where(inside, values, 0.0)
    mean = jnp.sum(values, axis=1, keepdims=True) * (1.0 / channels)
    centred = jnp.where(inside, values - mean, 0.0)
    spread = jnp.sum(centred * centred, axis=1, keepdims=True) * (1.0 / channels)
    return centred, lax.rsqrt(spread + NORM_EPS)


def gelu_parts(v):
    size = jnp.abs(v)
    t = 1.0 / (1.0 + (0.3275911 * math.sqrt(0.5)) * size)
    bell = jnp.exp(-0.5 * v * v)
    poly = t * (
        0.5 * 0.254829592
        + t * (-0.5 * 0.284496736 + t * (0.5 * 1.421413741 + t * (-0.5 * 1.453152027 + t * (0.5 * 1.061405429))))
    )
    tail = poly * bell
    cdf = jnp.where(v >= 0.0, 1.0 - tail, tail)
    return v * cdf, cdf + v * bell * (1.0 / math.sqrt(2.0 * math.pi))


def cost(microseconds):
    return pl.CostEstimate(flops=int(microseconds * 5e7), bytes_accessed=0, transcendentals=0)


def transpose_into(sz, src, dst):
    def move(at, count):
        for ct in range(sz.ct):
            block = src[pl.ds(at, count), ct * 128 : (ct + 1) * 128].T
            size = min(128, sz.cr - ct * 128)
            if size > 0:
                dst[ct * 128 : ct * 128 + size, pl.ds(at, count)] = block[:size]

    def body(i, c):
        move(pl.multiple_of(i * 128, 128), 128)
        return c

    lax.fori_loop(0, sz.p // 128, body, 0)
    if sz.p % 128:
        move(sz.p // 128 * 128, sz.p % 128)


def weight_grad(sz, core, left_ref, right_ref, left_t_ref, mine_ref, other_ref, row_ref, col_ref):
    transpose_into(sz, left_ref, left_t_ref)
    half = sz.mh // 2
    for half_ref, which in ((other_ref, 1 - core), (mine_ref, core)):
        for at, width in column_blocks(half, 256):
            cols = pl.ds(pl.multiple_of(which * half + at, 128), width)
            block = mm(left_t_ref[...], right_ref[:, cols])
            row_ref[:, cols] = block[sz.mc :]
            half_ref[:, at : at + width] = block[: sz.mc].astype(bf16)
    rest = right_ref[:, sz.mh :]
    row_ref[:, sz.mh :] = mm(left_t_ref[sz.mc :, :], rest)
    col_ref[...] = mm(rest.astype(f32).T[0:16].astype(bf16), left_ref[...])


def split_kernel(sz, shifts, heights_ref, band_ref, me_ref, x_ref, noise_ref, *refs):
    pieces, y_ref, s_ref = refs[: sz.m], refs[sz.m], refs[sz.m + 1]
    for ct in range(sz.ct):
        first = ct * 128
        if ct < sz.ct - 1:
            spans = [(x_ref, first, 128, 0)]
        else:
            rest = sz.c - first
            s_ref[...] = jnp.zeros_like(s_ref)
            spans = [(x_ref, first, rest, 0), (noise_ref, 0, sz.k, rest)]
        for ref, at, count, to in spans:
            for lt, width in column_blocks(sz.lon, 128):
                block = ref[0, at : at + count, :, lt : lt + width].astype(f32)
                s_ref[lt // 128, 2 * to : 2 * (to + count), :width] = block.reshape(2 * count, width)
        for r in range(2):
            for lt, width in column_blocks(sz.lon, 128):
                block = s_ref[lt // 128, pl.ds(r, 128, stride=2), :].T
                y_ref[r, ct, REACH + lt : REACH + lt + width, :] = block[:width]
    for r in range(2):
        for ct in range(sz.ct):
            y_ref[r, ct, :REACH, :] = y_ref[r, ct, sz.lon : sz.lon + REACH, :]
            y_ref[r, ct, REACH + sz.lon :, :] = y_ref[r, ct, REACH : sz.ext - sz.q, :]
    for s in range(sz.m):
        start = (me_ref[0] ^ shifts[s]) * sz.q
        for r, row in enumerate((0, heights_ref[band_ref[0]] - 1)):
            for ct in range(sz.ct):
                pieces[s][r, :, ct * 128 : (ct + 1) * 128] = y_ref[row, ct, pl.ds(start, sz.ext), :].astype(bf16)


def split_call(sz, shifts, heights, band, me, x, noise):
    outs = tuple(jax.ShapeDtypeStruct((2, sz.ext, sz.cp), bf16) for _ in range(sz.m))
    return pl.pallas_call(
        functools.partial(split_kernel, sz, shifts),
        out_shape=outs,
        in_specs=[smem(), smem(), smem(), vmem(), vmem()],
        out_specs=tuple(vmem() for _ in outs),
        scratch_shapes=[
            pltpu.VMEM((2, sz.ct, sz.lon + sz.ext - sz.q, 128), f32),
            pltpu.VMEM((round_up(sz.lon, 128) // 128, 256, 128), f32),
        ],
        compiler_params=pltpu.CompilerParams(vmem_limit_bytes=24 * 1024 * 1024),
        cost_estimate=cost(5),
        name="split",
    )(heights, band, me, x, noise)


def join_kernel(sz, shifts, me_ref, *refs):
    pieces, out_ref, y_ref, s_ref = refs[: sz.m], refs[sz.m], refs[sz.m + 1], refs[sz.m + 2]
    tail = sz.ext - sz.q - REACH
    y_ref[...] = jnp.zeros_like(y_ref)
    for s in range(sz.m):
        start = (me_ref[0] ^ shifts[s]) * sz.q
        for r in range(2):
            for ct in range(sz.ct):
                part = pieces[s][r, :, ct * 128 : (ct + 1) * 128].astype(f32)
                y_ref[r, ct, pl.ds(start, sz.ext), :] += part
    for r in range(2):
        for ct in range(sz.ct):
            y_ref[r, ct, sz.lon : sz.lon + REACH, :] += y_ref[r, ct, :REACH, :]
            y_ref[r, ct, REACH : REACH + tail, :] += y_ref[r, ct, REACH + sz.lon : REACH + sz.lon + tail, :]
    for ct in range(sz.ct):
        for r in range(2):
            for lt in range(0, sz.lon, 128):
                block = y_ref[r, ct, REACH + lt : REACH + lt + 128, :].T
                s_ref[lt // 128, pl.ds(r, 128, stride=2), :] = block
        size = min(128, sz.c - ct * 128)
        for lt, width in column_blocks(sz.lon, 128):
            block = s_ref[lt // 128, : 2 * size, :width].reshape(size, 2, width)
            out_ref[0, ct * 128 : ct * 128 + size, :, lt : lt + width] = block.astype(bf16)


def join_call(sz, shifts, me, pieces):
    return pl.pallas_call(
        functools.partial(join_kernel, sz, shifts),
        out_shape=jax.ShapeDtypeStruct((1, sz.c, 2, sz.lon), bf16),
        in_specs=[smem()] + [vmem()] * sz.m,
        out_specs=vmem(),
        scratch_shapes=[
            pltpu.VMEM((2, sz.ct, REACH + max(round_up(sz.lon, 128), sz.lon + sz.ext - sz.q - REACH), 128), f32),
            pltpu.VMEM((round_up(sz.lon, 128) // 128, 256, 128), f32),
        ],
        compiler_params=pltpu.CompilerParams(vmem_limit_bytes=24 * 1024 * 1024),
        cost_estimate=cost(6),
        name="join",
    )(me, *pieces)


def norm_and_filter(sz, e, height_ref, taps_ref, x_ref, prev_ref, next_ref, gain_ref, filter_ref, normed_ref, n_ref, fil_ref):
    lanes = lax.broadcasted_iota(jnp.int32, (1, sz.cp), 1)
    below_first = jnp.where(height_ref[0] == 2, 2, 3)
    sources = ((0, 1, below_first), (1, 2, 3))

    def norm_store(values, row):
        centred, inv = norm_rows(values.astype(f32), sz.c, lanes)
        normed = (centred * inv * gain_ref[...]).astype(bf16)
        normed_ref[e, row] = normed
        normed = normed.astype(f32)
        for ct in range(sz.ct):
            n_ref[row, ct] = normed[:, ct * 128 : (ct + 1) * 128]

    norm_store(prev_ref[e], 0)
    norm_store(x_ref[e, 0], 1)
    norm_store(x_ref[e, 1], 2)
    norm_store(next_ref[e], 3)

    def filter_tile(ct, c):
        for r in range(2):
            acc = jnp.zeros((sz.pr, 128), f32)
            for a in range(3):
                for j in range(3):
                    tap = 3 * a + j
                    start = taps_ref[tap, r] + REACH
                    moved = n_ref[sources[r][a], ct, pl.ds(start, sz.pr), :]
                    acc = acc + filter_ref[ct, tap : tap + 1, :] * moved
            fil_ref[ct, r * sz.pr : (r + 1) * sz.pr, :] = acc
        return c

    lax.fori_loop(0, sz.ct, filter_tile, 0)


def feed_forward(sz, e, x_ref, fil_ref, expand_ref, bias_ref, reduce_ref, outbias_ref, noisemix_ref, store):
    own = jnp.concatenate([x_ref[e, r].astype(f32)[REACH : REACH + sz.pr] for r in range(2)], axis=0)
    noise = own[:, (sz.ct - 1) * 128 :].astype(bf16)
    mixed = mm(jnp.concatenate([noise, noise], axis=1), noisemix_ref[...])
    filtered = jnp.concatenate([fil_ref[ct] for ct in range(sz.ct)], axis=1)
    lanes = lax.broadcasted_iota(jnp.int32, (1, sz.cp), 1)
    mixed = jnp.where(lanes == sz.c, 1.0, filtered + mixed).astype(bf16)
    store("mixed", slice(0, sz.cp), mixed)
    acts = []
    for at, width in column_blocks(sz.hp, 256):
        pre = mm(mixed, expand_ref[:, at : at + width]) + bias_ref[:, at : at + width]
        act, slope = gelu_parts(pre)
        if at <= sz.h < at + width:
            units = at + lax.broadcasted_iota(jnp.int32, (1, width), 1)
            act = jnp.where(units == sz.h, 1.0, act)
        acts.append(act.astype(bf16))
        store("act", slice(at, at + width), acts[-1])
        store("slope", slice(at, at + width), slope.astype(bf16))
    act = jnp.concatenate(acts, axis=1)
    return own + (mm(act, reduce_ref[...], NT) + outbias_ref[...])


def own_kernel(
    sz,
    height_ref,
    taps_ref,
    x_ref,
    prev_ref,
    next_ref,
    expand_ref,
    bias_ref,
    reduce_ref,
    gain_ref,
    outbias_ref,
    filter_ref,
    noisemix_ref,
    normed_ref,
    mx_ref,
    act_ref,
    dg_ref,
    pred_ref,
    n_ref,
    fil_ref,
):
    norm_and_filter(sz, 0, height_ref, taps_ref, x_ref, prev_ref, next_ref, gain_ref, filter_ref, normed_ref, n_ref, fil_ref)
    places = {"mixed": mx_ref, "act": act_ref, "slope": dg_ref}

    def store(name, cols, values):
        places[name][:, cols] = values

    pred_ref[...] = feed_forward(
        sz, 0, x_ref, fil_ref, expand_ref, bias_ref, reduce_ref, outbias_ref, noisemix_ref, store
    )


def filter_scratch(sz):
    return [pltpu.VMEM((4, sz.ct, sz.ext, 128), f32), pltpu.VMEM((sz.ct, sz.pe, 128), f32)]


def own_call(sz, height, taps, x, prev, after, weights):
    shape = jax.ShapeDtypeStruct
    outs = (
        shape((sz.m, 4, sz.ext, sz.cp), bf16),
        shape((sz.pe, sz.cp), bf16),
        shape((sz.pe, sz.hp), bf16),
        shape((sz.pe, sz.hp), bf16),
        shape((sz.pe, sz.cp), f32),
    )
    return pl.pallas_call(
        functools.partial(own_kernel, sz),
        grid=(1,),
        out_shape=outs,
        in_specs=[smem(), smem()] + [vmem()] * 10,
        out_specs=(pl.BlockSpec((1, 4, sz.ext, sz.cp), lambda i: (0, 0, 0, 0)),) + (vmem(),) * 4,
        scratch_shapes=filter_scratch(sz),
        compiler_params=pltpu.CompilerParams(vmem_limit_bytes=50 * 1024 * 1024),
        cost_estimate=cost(8),
        name="own",
    )(height, taps, x, prev, after, *weights)


def main_kernel(
    sz,
    height_ref,
    core_ref,
    taps_ref,
    bias_ref,
    gain_ref,
    outbias_ref,
    filter_ref,
    noisemix_ref,
    x_hbm,
    prev_hbm,
    next_hbm,
    target_hbm,
    expand_hbm,
    reduce_hbm,
    normed_own_hbm,
    mx_hbm,
    act_hbm,
    dg_hbm,
    pred_hbm,
    mine_hbm,
    other_hbm,
    bg_hbm,
    pg_hbm,
    normed_hbm,
    small_ref,
    x_ref,
    prev_ref,
    next_ref,
    target_ref,
    expand_ref,
    reduce_ref,
    mine_ref,
    other_ref,
    bg_ref,
    pg_ref,
    n_ref,
    fil_ref,
    nb_ref,
    mx_ref,
    act_ref,
    dg_ref,
    pred_ref,
    tr_ref,
    row_e_ref,
    row_r_ref,
    col_e_ref,
    col_r_ref,
    loss_ref,
    in_sems,
    out_sems,
):
    first = pl.ds(0, sz.pe)
    others = pl.ds(1, sz.m - 1)
    early = [
        pltpu.make_async_copy(x_hbm.at[others], x_ref, in_sems.at[0]),
        pltpu.make_async_copy(prev_hbm, prev_ref, in_sems.at[1]),
        pltpu.make_async_copy(next_hbm, next_ref, in_sems.at[2]),
    ]
    expand_load = pltpu.make_async_copy(expand_hbm, expand_ref, in_sems.at[3])
    reduce_load = pltpu.make_async_copy(reduce_hbm, reduce_ref, in_sems.at[4])
    loads = [
        pltpu.make_async_copy(mx_hbm, mx_ref.at[first], in_sems.at[5]),
        pltpu.make_async_copy(act_hbm, act_ref.at[first], in_sems.at[6]),
        pltpu.make_async_copy(dg_hbm, dg_ref.at[first], in_sems.at[7]),
        pltpu.make_async_copy(pred_hbm, pred_ref.at[0], in_sems.at[8]),
        pltpu.make_async_copy(target_hbm, target_ref, in_sems.at[9]),
    ]
    for load in (*early, expand_load, reduce_load, *loads):
        load.start()
    for load in early:
        load.wait()

    def forward(e, carry):
        norm_and_filter(
            sz, e, height_ref, taps_ref, x_ref, prev_ref, next_ref, gain_ref, filter_ref, nb_ref, n_ref, fil_ref
        )

        @pl.when(e == 0)
        def _():
            expand_load.wait()
            reduce_load.wait()

        rows = pl.ds(pl.multiple_of((e + 1) * sz.pe, 16), sz.pe)
        places = {"mixed": mx_ref, "act": act_ref, "slope": dg_ref}

        def store(name, cols, values):
            places[name][rows, cols] = values

        pred_ref[e + 1] = feed_forward(
            sz, e, x_ref, fil_ref, expand_ref, bias_ref, reduce_ref, outbias_ref, noisemix_ref, store
        )
        return carry

    lax.fori_loop(0, sz.m - 1, forward, 0)
    save = pltpu.make_async_copy(nb_ref, normed_hbm.at[pl.ds(1, sz.m - 1)], out_sems.at[0])
    save.start()
    for load in loads:
        load.wait()

    height = height_ref[0]
    lanes = lax.broadcasted_iota(jnp.int32, (1, sz.cp), 1)
    inside = (lanes < sz.c).astype(f32)
    loss_ref[...] = jnp.zeros_like(loss_ref)
    step = 16
    inv_m = 1.0 / sz.m
    inv_mm = inv_m * inv_m

    def score(i, carry):
        at = pl.multiple_of(i * step, step)
        pixel = at + lax.broadcasted_iota(jnp.int32, (step, 1), 0)
        row = (pixel >= sz.pr).astype(jnp.int32)
        use = (pixel - row * sz.pr < sz.q) & (row < height)
        mask_rows = use.astype(f32)
        for ct in range(sz.ct):
            cols = slice(ct * 128, (ct + 1) * 128)
            mask = mask_rows * inside[:, cols]
            preds = [pred_ref[e, pl.ds(at, step), cols] for e in range(sz.m)]
            truth = target_ref[pl.ds(at, step), cols].astype(f32)
            slopes = []
            own_sum = 0.0
            for p in preds:
                d = p - truth
                q = d * d + 1.0
                r = lax.rsqrt(q)
                own_sum = own_sum + q * r
                slopes.append(d * r * inv_m)
            pair_sum = 0.0
            pairs = [0.0] * sz.m
            for a in range(sz.m):
                for b in range(a + 1, sz.m):
                    d = preds[a] - preds[b]
                    q = d * d + 1.0
                    r = lax.rsqrt(q)
                    pair_sum = pair_sum + q * r
                    s = d * r
                    pairs[a] = pairs[a] + s
                    pairs[b] = pairs[b] - s
            value = own_sum * inv_m - (pair_sum + 0.5 * sz.m) * inv_mm
            value = mask * value
            loss_ref[:, cols] += value[0:8] + value[8:16]
            for e in range(sz.m):
                g = (mask * (slopes[e] - pairs[e] * inv_mm)).astype(bf16)
                where = pl.ds(pl.multiple_of(e * sz.pe + at, 16), step)
                bg_ref[where, cols] = g
        return carry

    lax.fori_loop(0, sz.pe // step, score, 0)
    core = core_ref[0]
    saves = [save]

    def write(here, there, which):
        saves.append(pltpu.make_async_copy(here, there, out_sems.at[which]))
        saves[-1].start()

    write(bg_ref, bg_hbm, 1)
    weight_grad(sz, core, bg_ref, act_ref, tr_ref, mine_ref.at[1], other_ref.at[1], row_r_ref, col_r_ref)
    write(mine_ref.at[1], mine_hbm.at[1], 2)
    write(other_ref.at[1], other_hbm.at[1], 3)


    def backward(e, carry):
        rows = pl.ds(pl.multiple_of(e * sz.pe, 16), sz.pe)
        bg = bg_ref[rows, :]
        for at, width in column_blocks(sz.hp, 256):
            grad = mm(bg, reduce_ref[:, at : at + width])
            pre = (grad * dg_ref[rows, at : at + width].astype(f32)).astype(bf16)
            pg_ref[rows, at : at + width] = pre
        return carry

    lax.fori_loop(0, sz.m, backward, 0)
    write(pg_ref, pg_hbm, 4)
    weight_grad(sz, core, mx_ref, pg_ref, tr_ref, mine_ref.at[0], other_ref.at[0], row_e_ref, col_e_ref)
    write(other_ref.at[0], other_hbm.at[0], 5)
    write(mine_ref.at[0], mine_hbm.at[0], 6)
    at = Rows(sz)
    small_ref[...] = jnp.zeros_like(small_ref)
    lane = lax.broadcasted_iota(jnp.int32, (1, sz.mc), 1)
    half = sz.mh // 2

    def column_sum(ref):
        return jnp.sum(ref[...], axis=0, keepdims=True)

    def long_row(row, place, values, extra):
        small_ref[row : row + 1, :] = values[:, :half]
        small_ref[row + 1 : row + 2, :] = values[:, half : sz.mh]
        for i in range(at.spare):
            extra = jnp.where(lane == place + i, values[:, sz.mh + i : sz.mh + i + 1], extra)
        return extra

    extra = jnp.zeros((1, sz.mc), f32)
    outbias_grad = col_r_ref[at.spare : at.spare + 1, :]
    small_ref[at.outbias : at.outbias + 1, :] = outbias_grad[:, : sz.mc]
    extra = jnp.where(lane == at.x_outbias, outbias_grad[:, sz.mc : sz.mc + 1], extra)
    extra = long_row(at.biasin, at.x_biasin, row_e_ref[sz.c - sz.mc : sz.c - sz.mc + 1, :], extra)
    extra = long_row(at.row_e, at.x_row_e, row_e_ref[0:1, :], extra)
    extra = long_row(at.row_r, at.x_row_r, row_r_ref[0:1, :], extra)
    small_ref[at.col_e : at.col_e + at.spare, :] = col_e_ref[: at.spare, : sz.mc]
    small_ref[at.col_r : at.col_r + at.spare, :] = col_r_ref[: at.spare, : sz.mc]
    extra = jnp.where(lane == at.x_loss, jnp.sum(column_sum(loss_ref), axis=1, keepdims=True), extra)
    small_ref[at.extra : at.extra + 1, :] = extra
    for save in saves:
        save.wait()


def main_call(sz, height, core, taps, x, prev, after, target, weights, state):
    shape = jax.ShapeDtypeStruct
    half = shape((2, sz.mc, sz.mh // 2), bf16)
    outs = (
        half,
        half,
        shape((sz.p, sz.cp), bf16),
        shape((sz.p, sz.hp), bf16),
        shape((sz.m, 4, sz.ext, sz.cp), bf16),
        shape((Rows(sz).count, sz.mc), f32),
    )
    anywhere = pl.BlockSpec(memory_space=pl.ANY)
    expand, bias, reduce, gain, outbias, filt, noisemix = weights
    return pl.pallas_call(
        functools.partial(main_kernel, sz),
        out_shape=outs,
        in_specs=[smem()] * 3 + [vmem()] * 5 + [anywhere] * 11,
        out_specs=(anywhere,) * 5 + (vmem(),),
        input_output_aliases={14: 4},
        scratch_shapes=[
            pltpu.VMEM((sz.m - 1, 2, sz.ext, sz.cp), bf16),
            pltpu.VMEM((sz.m - 1, sz.ext, sz.cp), bf16),
            pltpu.VMEM((sz.m - 1, sz.ext, sz.cp), bf16),
            pltpu.VMEM((sz.pe, sz.cp), bf16),
            pltpu.VMEM((sz.cp, sz.hp), bf16),
            pltpu.VMEM((sz.cp, sz.hp), bf16),
            pltpu.VMEM((2, sz.mc, sz.mh // 2), bf16),
            pltpu.VMEM((2, sz.mc, sz.mh // 2), bf16),
            pltpu.VMEM((sz.p, sz.cp), bf16),
            pltpu.VMEM((sz.p, sz.hp), bf16),
            *filter_scratch(sz),
            pltpu.VMEM((sz.m - 1, 4, sz.ext, sz.cp), bf16),
            pltpu.VMEM((sz.p, sz.cp), bf16),
            pltpu.VMEM((sz.p, sz.hp), bf16),
            pltpu.VMEM((sz.p, sz.hp), bf16),
            pltpu.VMEM((sz.m, sz.pe, sz.cp), f32),
            pltpu.VMEM((sz.cr, sz.p), bf16),
            pltpu.VMEM((sz.cr - sz.mc, sz.hp), f32),
            pltpu.VMEM((sz.cr - sz.mc, sz.hp), f32),
            pltpu.VMEM((16, sz.cp), f32),
            pltpu.VMEM((16, sz.cp), f32),
            pltpu.VMEM((8, sz.cp), f32),
            pltpu.SemaphoreType.DMA((10,)),
            pltpu.SemaphoreType.DMA((7,)),
        ],
        compiler_params=pltpu.CompilerParams(vmem_limit_bytes=50 * 1024 * 1024),
        cost_estimate=cost(40),
        name="main",
    )(height, core, taps, bias, gain, outbias, filt, noisemix, x, prev, after, target, expand, reduce, *state)


def unmix_kernel(
    sz,
    base,
    count,
    height_ref,
    taps_ref,
    filter_ref,
    small_in_ref,
    pg_hbm,
    x_hbm,
    normed_hbm,
    expand_hbm,
    gn_own_hbm,
    gn_prev_hbm,
    gn_next_hbm,
    small_ref,
    pg_ref,
    x_ref,
    normed_ref,
    expand_ref,
    own_ref,
    edge_ref,
    filter_grad_ref,
    mixing_grad_ref,
    n_ref,
    gn_ref,
    gm_ref,
    in_sems,
    out_sems,
):
    below_first = jnp.where(height_ref[0] == 2, 2, 3)
    sources = ((0, 1, below_first), (1, 2, 3))
    last = sz.ct - 1
    weights = pltpu.make_async_copy(expand_hbm, expand_ref, in_sems.at[0])
    weights.start()
    loads = []
    for e in range(count):
        rows = pl.ds((base + e) * sz.pe, sz.pe)
        channels = pl.ds(last * 128, 128)
        loads.append(
            (
                pltpu.make_async_copy(pg_hbm.at[rows], pg_ref.at[e], in_sems.at[3 * e + 1]),
                pltpu.make_async_copy(x_hbm.at[base + e, :, :, channels], x_ref.at[e], in_sems.at[3 * e + 2]),
                pltpu.make_async_copy(normed_hbm.at[base + e], normed_ref.at[e], in_sems.at[3 * e + 3]),
            )
        )
        for load in loads[e]:
            load.start()
    filter_grad_ref[...] = jnp.zeros_like(filter_grad_ref)
    mixing_grad_ref[...] = jnp.zeros_like(mixing_grad_ref)
    pad = 2 * REACH
    for r in range(2):
        for ct in range(sz.ct):
            gm_ref[r, ct, :pad, :] = jnp.zeros((pad, 128), f32)
            gm_ref[r, ct, pad + sz.pr :, :] = jnp.zeros((sz.ext + REACH - sz.pr, 128), f32)
    weights.wait()
    stores = []
    for e in range(count):
        for load in loads[e]:
            load.wait()
        gm = mm(pg_ref[e], expand_ref[...], NT)
        for r in range(2):
            for ct in range(sz.ct):
                gm_ref[r, ct, pad : pad + sz.pr, :] = gm[r * sz.pr : (r + 1) * sz.pr, ct * 128 : (ct + 1) * 128]
        for row in range(4):
            normed = normed_ref[e, row].astype(f32)
            for ct in range(sz.ct):
                n_ref[row, ct] = normed[:, ct * 128 : (ct + 1) * 128]
        noise = jnp.concatenate([x_ref[e, r].astype(f32)[REACH : REACH + sz.pr] for r in range(2)], axis=0)
        mixing_grad_ref[...] += mm(noise.T[0:16].astype(bf16), gm.astype(bf16))

        def unfilter_tile(ct, c):
            def gathered(*readers):
                acc = jnp.zeros((sz.ext, 128), f32)
                for r, a in readers:
                    for tap in range(3 * a, 3 * a + 3):
                        start = REACH - taps_ref[tap, r]
                        acc = acc + filter_ref[ct, tap : tap + 1, :] * gm_ref[r, ct, pl.ds(start, sz.ext), :]
                return acc

            gn_ref[0, ct] = gathered((0, 0))
            gn_ref[1, ct] = gathered((0, 1), (1, 0))
            gn_ref[2, ct] = gathered((1, 1))
            gn_ref[3, ct] = gathered((1, 2))
            gn_ref[below_first, ct] += gathered((0, 2))
            for r in range(2):
                g = gm_ref[r, ct, pad : pad + sz.pr, :]
                for a in range(3):
                    for tap in range(3 * a, 3 * a + 3):
                        read = n_ref[sources[r][a], ct, pl.ds(taps_ref[tap, r] + REACH, sz.pr), :]
                        filter_grad_ref[ct, tap] += tile_sum(g * read)
            return c

        lax.fori_loop(0, sz.ct, unfilter_tile, 0)
        for ct in range(sz.ct):
            cols = slice(ct * 128, (ct + 1) * 128)
            edge_ref[e, 0, :, cols] = gn_ref[0, ct].astype(bf16)
            edge_ref[e, 1, :, cols] = gn_ref[3, ct].astype(bf16)
            own_ref[e, 0, :, cols] = gn_ref[1, ct].astype(bf16)
            own_ref[e, 1, :, cols] = gn_ref[2, ct].astype(bf16)
        stores += [
            pltpu.make_async_copy(own_ref.at[e], gn_own_hbm.at[e], out_sems.at[3 * e]),
            pltpu.make_async_copy(edge_ref.at[e, 0], gn_prev_hbm.at[e], out_sems.at[3 * e + 1]),
            pltpu.make_async_copy(edge_ref.at[e, 1], gn_next_hbm.at[e], out_sems.at[3 * e + 2]),
        ]
        for store in stores[-3:]:
            store.start()

    at = Rows(sz)
    lane = lax.broadcasted_iota(jnp.int32, (1, sz.mc), 1)
    small_ref[...] = small_in_ref[...]
    extra = small_in_ref[at.extra : at.extra + 1, :]
    first = sz.c - last * 128
    for tap in range(9):
        for ct in range(last):
            row = jnp.sum(filter_grad_ref[ct, tap], axis=0, keepdims=True)
            small_ref[tap : tap + 1, ct * 128 : (ct + 1) * 128] += row
        row = jnp.sum(filter_grad_ref[last, tap], axis=0, keepdims=True)
        extra = extra + jnp.where(lane == tap, row[:, 0:1], 0.0)
    mixing = mixing_grad_ref[first : first + sz.k, :]
    small_ref[at.mixing : at.mixing + sz.k, :] += mixing[:, : sz.mc]
    for i in range(sz.k):
        extra = extra + jnp.where(lane == at.x_mixing + i, mixing[i : i + 1, sz.mc : sz.mc + 1], 0.0)
    small_ref[at.extra : at.extra + 1, :] = extra
    for store in stores:
        store.wait()


def unmix_call(sz, base, count, height, taps, pg, x, normed, expand, filt, small):
    shape = jax.ShapeDtypeStruct
    outs = (
        shape((count, 2, sz.ext, sz.cp), bf16),
        shape((count, sz.ext, sz.cp), bf16),
        shape((count, sz.ext, sz.cp), bf16),
        shape(small.shape, f32),
    )
    anywhere = pl.BlockSpec(memory_space=pltpu.HBM)
    return pl.pallas_call(
        functools.partial(unmix_kernel, sz, base, count),
        out_shape=outs,
        in_specs=[smem(), smem(), vmem(), vmem()] + [anywhere] * 4,
        out_specs=(anywhere,) * 3 + (vmem(),),
        scratch_shapes=[
            pltpu.VMEM((count, sz.pe, sz.hp), bf16),
            pltpu.VMEM((count, 2, sz.ext, 128), bf16),
            pltpu.VMEM((count, 4, sz.ext, sz.cp), bf16),
            pltpu.VMEM((sz.cp, sz.hp), bf16),
            pltpu.VMEM((count, 2, sz.ext, sz.cp), bf16),
            pltpu.VMEM((count, 2, sz.ext, sz.cp), bf16),
            pltpu.VMEM((sz.ct, 9, 8, 128), f32),
            pltpu.VMEM((16, sz.cp), f32),
            pltpu.VMEM((4, sz.ct, sz.ext, 128), f32),
            pltpu.VMEM((4, sz.ct, sz.ext, 128), f32),
            pltpu.VMEM((2, sz.ct, sz.ext + 3 * REACH, 128), f32),
            pltpu.SemaphoreType.DMA((3 * count + 1,)),
            pltpu.SemaphoreType.DMA((3 * count,)),
        ],
        compiler_params=pltpu.CompilerParams(vmem_limit_bytes=50 * 1024 * 1024),
        cost_estimate=cost(5 * count),
        name="unmix",
    )(height, taps, filt, small, pg, x, normed, expand)


def norm_back_kernel(sz, height_ref, x_ref, gn_ref, up_ref, down_ref, bg_ref, gain_ref, out_ref):
    height = height_ref[0]
    lanes = lax.broadcasted_iota(jnp.int32, (1, sz.cp), 1)
    from_up = up_ref[0].astype(f32)
    from_down = down_ref[0].astype(f32)
    direct = bg_ref[...].astype(f32)
    for r in range(2):
        centred, inv = norm_rows(x_ref[0, r].astype(f32), sz.c, lanes)
        xhat = centred * inv
        g = gn_ref[0, r].astype(f32) + jnp.where(height == r + 1, from_down, 0.0)
        if r == 0:
            g = g + from_up
        q = g * gain_ref[...]
        mean_q = jnp.sum(q, axis=1, keepdims=True) * (1.0 / sz.c)
        mean_qx = jnp.sum(q * xhat, axis=1, keepdims=True) * (1.0 / sz.c)
        result = (q - mean_q - xhat * mean_qx) * inv
        part = result[REACH : REACH + sz.pr] + direct[r * sz.pr : (r + 1) * sz.pr]
        pieces = [result[:REACH], part, result[REACH + sz.pr :]]
        out_ref[0, r] = jnp.concatenate(pieces, axis=0).astype(bf16)


def norm_back_call(sz, base, count, height, x, gn, up, down, bg, gain):
    return pl.pallas_call(
        functools.partial(norm_back_kernel, sz),
        grid=(count,),
        out_shape=jax.ShapeDtypeStruct((count, 2, sz.ext, sz.cp), bf16),
        in_specs=[
            smem(),
            pl.BlockSpec((1, 2, sz.ext, sz.cp), lambda i: (i + base, 0, 0, 0)),
            pl.BlockSpec((1, 2, sz.ext, sz.cp), lambda i: (i, 0, 0, 0)),
            pl.BlockSpec((1, sz.ext, sz.cp), lambda i: (i, 0, 0)),
            pl.BlockSpec((1, sz.ext, sz.cp), lambda i: (i, 0, 0)),
            pl.BlockSpec((sz.pe, sz.cp), lambda i: (i + base, 0)),
            pl.BlockSpec((1, sz.cp), lambda i: (0, 0)),
        ],
        out_specs=pl.BlockSpec((1, 2, sz.ext, sz.cp), lambda i: (i, 0, 0, 0)),
        compiler_params=pltpu.CompilerParams(vmem_limit_bytes=28 * 1024 * 1024),
        cost_estimate=cost(2 * count),
        name="norm_back",
    )(height, x, gn, up, down, bg, gain)


def adam_kernel(sz, limit, pixels, members, stacks, place_ref, heights_ref, *refs):
    mine_ref, got_ref, small_mine_ref, small_got_ref = refs[:4]
    ins, small_ins, (norm_ref, mean_ref) = refs[4:10], refs[10:22], refs[22:24]
    outs, small_outs = refs[24:32], refs[32:44]
    factor_ref, small_ref, column_ref, cols_ref, gain_ref = refs[44:]
    at = Rows(sz)
    step = pl.program_id(0)
    core, member, stack = place_ref[0], place_ref[1], place_ref[2]
    half = sz.mh // 2
    each = sz.mc // members
    rows = sz.piece_rows(members, stacks)

    def wide(row, count, place):
        return jnp.concatenate([small_ref[row : row + count, :], column_ref[place : place + count, 0:1]], axis=1)

    def long(row, place):
        extra = small_ref[at.extra : at.extra + 1, place : place + at.spare]
        return jnp.concatenate([small_ref[row : row + 1, :], small_ref[row + 1 : row + 2, :], extra], axis=1)

    @pl.when(step == 0)
    def _():
        part = at.count // 2
        for which, ref in ((core, small_mine_ref), (1 - core, small_got_ref)):
            where = pl.ds(pl.multiple_of(which * part, part), part)
            values = ref[...].astype(f32)
            small_ref[where, :] = values[:part] + values[part:]
        extra = small_ref[at.extra : at.extra + 1, 0:128]
        column_ref[...] = jnp.broadcast_to(extra, (8, 128)).T
        total = jnp.zeros((8, half), f32)
        for ref in (mine_ref, got_ref):

            def body(i, acc):
                values = ref[i].astype(f32)
                values = values * values
                for j in range(0, rows, 8):
                    acc = acc + values[j : j + 8]
                return acc

            total = lax.fori_loop(0, 2 * members * stacks, body, total)
        count = jnp.sum(total)
        filter_grad = wide(0, 9, 0)
        gain_row = jnp.sum(small_ins[0][...] * filter_grad, axis=0, keepdims=True) / small_ins[6][0:1, :]
        gain_ref[...] = gain_row
        cols = small_ref[at.col_e : at.extra, :]
        for values in (
            filter_grad,
            wide(at.mixing, sz.k, at.x_mixing),
            gain_row,
            wide(at.outbias, 1, at.x_outbias),
            long(at.biasin, at.x_biasin),
            long(at.row_e, at.x_row_e),
            long(at.row_r, at.x_row_r),
            cols,
        ):
            count = count + jnp.sum(values * values)
        norm = jnp.sqrt(jnp.full((8, 128), count, f32))
        factor_ref[...] = jnp.minimum(1.0, limit / (norm + 1e-06))
        live = heights_ref[0]
        for i in range(1, heights_ref.shape[0]):
            live = live + heights_ref[i]
        loss = column_ref[at.x_loss : at.x_loss + 1, 0:1]
        mean = loss / (jnp.full((8, 128), pixels, f32) * live.astype(f32))
        norm_ref[0] = norm[0, 0]
        mean_ref[0] = mean[0, 0]
        cols_ref[...] = jnp.concatenate([cols, jnp.zeros((8 - 2 * at.spare, sz.mc), f32)], axis=0).T

    factor = factor_ref[0:1, 0:1]

    def adam(w, g, m, v, rate):
        g = factor * g
        m_new = BETA_ONE * m + (1.0 - BETA_ONE) * g
        v_new = BETA_TWO * v + (1.0 - BETA_TWO) * g * g
        m_hat = m_new / (1.0 - BETA_ONE**STEP)
        v_hat = v_new / (1.0 - BETA_TWO**STEP)
        return w - rate * (m_hat / (jnp.sqrt(v_hat) + ADAM_EPS) + DECAY_RATE * w), m_new, v_new

    kinds = ((0, at.row_e, at.x_row_e, sz.c**-0.5), (1, at.row_r, at.x_row_r, sz.h**-0.5))

    @pl.when(step < sz.mc // ROWS)
    def _():
        first_core = core == 0
        for i in range(ROWS // rows):
            first = step * ROWS + i * rows
            t = member ^ (first // each)
            s = stack ^ ((first % each) // rows)
            where = pl.ds(pl.multiple_of(first, 8), rows)
            to = slice(i * rows, (i + 1) * rows)
            for kind, _, _, rate in kinds:
                slot = (t * stacks + s) * 2 + kind
                mine = mine_ref[slot].astype(f32)
                got = got_ref[slot].astype(f32)
                low = jnp.where(first_core, mine, got)
                high = jnp.where(first_core, got, mine)
                cols = cols_ref[where, kind * at.spare : (kind + 1) * at.spare]
                g = jnp.concatenate([low, high, cols], axis=1)
                w_ref, m_ref, v_ref = ins[3 * kind : 3 * kind + 3]
                w_out, m_out, v_out, c_out = outs[4 * kind : 4 * kind + 4]
                at_rows = where if kind == 0 else to
                w, m, v = adam(w_ref[at_rows, :], g, m_ref[at_rows, :], v_ref[at_rows, :], rate)
                w_out[to, :] = w
                m_out[to, :] = m
                v_out[to, :] = v
            if (i + 1) * rows % 16 == 0:
                both = slice((i + 1) * rows // 16 * 16 - max(16, rows * 2), (i + 1) * rows)
                for kind in range(2):
                    outs[4 * kind + 3][both, :] = outs[4 * kind][both, :].astype(bf16)

    @pl.when(step == sz.mc // ROWS)
    def _():
        for kind, row, place, rate in kinds:
            last = slice(sz.mc, sz.c) if kind == 0 else slice(0, 1)
            w_ref, m_ref, v_ref = ins[3 * kind : 3 * kind + 3]
            w_out, m_out, v_out, c_out = outs[4 * kind : 4 * kind + 4]
            w, m, v = adam(w_ref[last, :], long(row, place), m_ref[last, :], v_ref[last, :], rate)
            w_out[0:1, :] = w
            m_out[0:1, :] = m
            v_out[0:1, :] = v
            c_out[0:16, :] = jnp.broadcast_to(w, (16, sz.h)).astype(bf16)

    @pl.when(step == 0)
    def _():
        grads = (
            wide(0, 9, 0),
            wide(at.mixing, sz.k, at.x_mixing),
            jnp.concatenate([gain_ref[...], wide(at.outbias, 1, at.x_outbias)], axis=0),
            long(at.biasin, at.x_biasin),
        )
        for i, g in enumerate(grads):
            new = adam(small_ins[3 * i][...], g, small_ins[3 * i + 1][...], small_ins[3 * i + 2][...], SMALL_RATE)
            for ref, values in zip(small_outs[3 * i : 3 * i + 3], new):
                ref[...] = values


ROWS = 80


def adam_call(sz, limit, pixels, members, stacks, place, heights, grads, weights, small_weights):
    shape = jax.ShapeDtypeStruct
    full = shape((sz.c, sz.h), f32)
    low = shape((sz.c, sz.h), bf16)
    outs = (shape((1,), f32),) * 2 + (full, full, full, low) * 2 + tuple(shape(v.shape, f32) for v in small_weights)
    block = pl.BlockSpec((ROWS, sz.h), lambda i: (i, 0))
    steps = sz.mc // ROWS + 1
    return pl.pallas_call(
        functools.partial(adam_kernel, sz, limit, pixels, members, stacks),
        grid=(steps,),
        out_shape=outs,
        in_specs=[smem()] * 2 + [vmem()] * (4 + 3) + [block] * 3 + [vmem()] * 12,
        out_specs=(smem(),) * 2 + (block,) * 8 + (vmem(),) * 12,
        scratch_shapes=[
            pltpu.VMEM((8, 128), f32),
            pltpu.VMEM((Rows(sz).count, sz.mc), f32),
            pltpu.VMEM((128, 8), f32),
            pltpu.VMEM((sz.mc, 8), f32),
            pltpu.VMEM((1, sz.c), f32),
        ],
        compiler_params=pltpu.CompilerParams(vmem_limit_bytes=24 * 1024 * 1024),
        cost_estimate=cost(16),
        name="adam",
    )(place, heights, *grads, *weights, *small_weights)


def exchange(pieces, axis, count, shifts):
    return [
        piece if s == 0 else lax.ppermute(piece, axis, [(i, i ^ s) for i in range(count)])
        for piece, s in zip(pieces, shifts)
    ]


def scatter_over(values, axis, count, size):
    me = lax.axis_index(axis)
    values = jnp.pad(values, ((0, 0), (0, count * size - values.shape[1]), (0, 0)))
    pieces = [lax.dynamic_slice_in_dim(values, (me ^ s) * size, size, axis=1) for s in range(count)]
    return exchange(pieces, axis, count, range(count))


def added(parts):
    return sum(part.astype(f32) for part in parts).astype(bf16)


def two_parts(values):
    coarse = lax.reduce_precision(values, exponent_bits=8, mantissa_bits=7)
    return coarse.astype(bf16), (values - coarse).astype(bf16)


def after_all(values, *others):
    return lax.optimization_barrier((values, others))[0]


def pad_to(values, shape):
    return jnp.pad(values, [(0, n - m) for n, m in zip(shape, values.shape)])


def on_device(
    fields,
    noise_fields,
    target_fields,
    band_heights,
    tap_offsets,
    expand_weight,
    expand_bias,
    reduce_weight,
    channel_vectors,
    disco_filter,
    noise_mixing,
    first_expand,
    second_expand,
    first_bias,
    second_bias,
    first_reduce,
    second_reduce,
    first_vectors,
    second_vectors,
    first_filter,
    second_filter,
    first_mixing,
    second_mixing,
):
    members = lax.axis_size("member")
    stacks = lax.axis_size("stack")
    lat_count = 2 * stacks
    lat = ("stack", "core")
    channels, hidden = expand_weight.shape
    lon = fields.shape[3]
    sz = Sizes(members, channels, hidden, noise_fields.shape[1], lon)
    me = lax.axis_index("member")
    core = lax.axis_index("core")
    band = lax.axis_index("stack") * 2 + core
    height = lax.dynamic_slice_in_dim(band_heights, band, 1)

    shifts = [0, members - 1, *range(1, members - 1)]
    pieces = split_call(sz, shifts, band_heights, band.reshape(1), me.reshape(1), fields, noise_fields)
    arrived = exchange(pieces, "member", members, shifts)
    upward = [(i, i + 1) for i in range(lat_count - 1)]
    downward = [(i + 1, i) for i in range(lat_count - 1)]

    def edges(rows):
        bottom = jnp.stack([x[1] for x in rows])
        top = jnp.stack([x[0] for x in rows])
        return lax.ppermute(bottom, lat, upward), lax.ppermute(top, lat, downward)

    truth = pad_to(target_fields, (channels, 2, lon + sz.pr - sz.q))
    truth = lax.dynamic_slice_in_dim(truth, me * sz.q, sz.pr, axis=2)
    truth = pad_to(jnp.transpose(truth, (1, 2, 0)), (2, sz.pr, sz.cp)).reshape(sz.pe, sz.cp)

    expand_low = pad_to(after_all(expand_weight, pieces).astype(bf16), (sz.cp, sz.hp))
    reduce_low = pad_to(reduce_weight.T.astype(bf16), (sz.cp, sz.hp))
    bias = pad_to(expand_bias[None], (1, sz.hp))
    gain = pad_to(channel_vectors[0:1], (1, sz.cp))
    outbias = pad_to(channel_vectors[1:2], (1, sz.cp))
    filt = jnp.transpose(pad_to(disco_filter, (16, sz.cp)).reshape(16, sz.ct, 128), (1, 0, 2))
    spot = channels - (sz.ct - 1) * 128
    coarse, fine = two_parts(noise_mixing)
    noisemix = jnp.zeros((256, sz.cp), bf16)
    noisemix = noisemix.at[spot : spot + sz.k, :channels].set(coarse)
    noisemix = noisemix.at[128 + spot : 128 + spot + sz.k, :channels].set(fine)

    weights = (expand_low, bias, reduce_low, gain, outbias, filt, noisemix)
    core_id = core.reshape(1)
    own_edges = edges(after_all(arrived[:1], expand_low))
    state = own_call(sz, height, tap_offsets, arrived[0][None], *own_edges, weights)
    others = after_all(arrived[1:], state, truth)
    other_edges = edges(others)
    x = jnp.stack([arrived[0], *others])
    mine, other, bg, pg, normed, small = main_call(
        sz, height, core_id, tap_offsets, x, *other_edges, truth, weights, state
    )

    swap = [(0, 1), (1, 0)]
    part = (mine.astype(f32) + lax.ppermute(other, "core", swap).astype(f32)).astype(bf16)
    cut = members // 2

    def unmix_raw(base, count, pg, small):
        gn, gn_prev, gn_next, small = unmix_call(
            sz, base, count, height, tap_offsets, pg, x, normed, expand_low, filt, small
        )
        return (gn, gn_prev, gn_next), small

    def edges_back(raw):
        gn, gn_prev, gn_next = raw
        return gn, lax.ppermute(gn_next, lat, upward), lax.ppermute(gn_prev, lat, downward)

    def unmix(base, count, pg, small):
        raw, small = unmix_raw(base, count, pg, small)
        return edges_back(raw), small, raw[1]

    arriving = scatter_over(part, "member", members, sz.mc // members)
    near, small, done = unmix(0, cut, after_all(pg, part), small)
    far_raw, small = unmix_raw(cut, members - cut, after_all(pg, done), small)

    arriving, far_raw, small = after_all((arriving, far_raw, small))
    arriving = scatter_over(added(arriving), "stack", stacks, sz.piece_rows(members, stacks))
    near_grads = norm_back_call(sz, 0, cut, height, x, *near, bg, gain)
    small = small.reshape(2, -1, sz.mc)
    other_small = lax.dynamic_index_in_dim(small, 1 - core, 0, keepdims=False)
    small = lax.dynamic_index_in_dim(small, core, 0, keepdims=False) + lax.ppermute(other_small, "core", swap)

    def packed(main, small):
        return jnp.concatenate([main, *two_parts(small)], axis=0)

    def unpacked(messages):
        cut = messages[0].shape[0] - at.count
        half = at.count // 2
        parts = [m[cut:].astype(f32) for m in messages]
        return jnp.concatenate([m[:cut] for m in messages], axis=0), sum(p[:half] + p[half:] for p in parts)

    at = Rows(sz)
    arriving, far_raw, near_grads, small = after_all((arriving, far_raw, near_grads, small))
    message = packed(added(arriving).reshape(-1, sz.mh // 2), small)
    gathered = exchange([message] * stacks, "stack", stacks, range(stacks))
    returned = exchange([near_grads[s] for s in range(cut)], "member", members, shifts[:cut])

    gathered, far_raw, returned = after_all((gathered, far_raw, returned))
    message = packed(*unpacked(gathered))
    gathered = exchange([message] * members, "member", members, range(members))
    far = edges_back(far_raw)

    far_grads = norm_back_call(sz, cut, members - cut, height, x, *far, bg, gain)
    far_pieces = [far_grads[s] for s in range(members - cut)]

    gathered, far_pieces = after_all((gathered, far_pieces))
    mine, small = unpacked(gathered)
    small = packed(mine[:0], small)
    got = lax.ppermute(mine, "core", swap)
    got_small = lax.ppermute(small, "core", swap)
    returned = returned + exchange(after_all(far_pieces, got), "member", members, shifts[cut:])
    pieces = [v.reshape(-1, sz.piece_rows(members, stacks), sz.mh // 2) for v in (mine, got)]

    limit = 0.02 * math.sqrt(hidden * channels * lat_count * 2 * lon / members)
    norm, mean, we, m_e, v_e, c_e, wr, m_r, v_r, c_r, *rest = adam_call(
        sz,
        limit,
        channels * lon,
        members,
        stacks,
        jnp.stack([core, me, lax.axis_index("stack")]),
        band_heights,
        (*pieces, small, got_small),
        (expand_weight, first_expand, second_expand, reduce_weight.T, first_reduce.T, second_reduce.T),
        (
            disco_filter,
            first_filter,
            second_filter,
            noise_mixing,
            first_mixing,
            second_mixing,
            channel_vectors,
            first_vectors,
            second_vectors,
            expand_bias[None],
            first_bias[None],
            second_bias[None],
        ),
    )
    input_gradient = join_call(sz, shifts, me.reshape(1), after_all(returned, norm))
    return (
        mean[0],
        input_gradient,
        norm[0],
        we,
        m_e,
        v_e,
        rest[9][0],
        rest[10][0],
        rest[11][0],
        wr.T,
        m_r.T,
        v_r.T,
        *rest[6:9],
        *rest[0:3],
        *rest[3:6],
        c_e,
        c_r.T,
    )


def solution(mesh):
    members = mesh.shape["member"]
    lat = mesh.shape["lat"]
    split = Mesh(mesh.devices.reshape(members, lat // 2, 2), ("member", "stack", "core"))
    rows = ("stack", "core")
    whole = [P()] * 18
    in_specs = (
        P("member", None, rows, None),
        P("member", None, rows, None),
        P(None, rows, None),
        P(),
        P(None, rows),
        *whole,
    )
    out_specs = (P(), P("member", None, rows, None)) + (P(),) * 21
    return jax.shard_map(on_device, mesh=split, in_specs=in_specs, out_specs=out_specs, check_vma=False)
```

```python
import functools
import math

import jax
import jax.numpy as jnp
from jax import lax
from jax.experimental import pallas as pl
from jax.experimental.pallas import tpu as pltpu
from jax.sharding import Mesh, PartitionSpec as P

STEP = 10
BETA_ONE = 0.9
BETA_TWO = 0.95
ADAM_EPS = 1e-08
DECAY_RATE = 0.1
NORM_EPS = 1e-05
SMALL_RATE = 0.3
REACH = 8
f32 = jnp.float32
bf16 = jnp.bfloat16

NN = (((1,), (0,)), ((), ()))
NT = (((1,), (1,)), ((), ()))
TN = (((0,), (0,)), ((), ()))


def round_up(value, step):
    return -(-value // step) * step


def mm(a, b, dims=NN):
    return lax.dot_general(a, b, dims, preferred_element_type=f32)


class Sizes:
    def __init__(self, members, channels, hidden, noise, lon):
        self.m = members
        self.c = channels
        self.h = hidden
        self.k = noise
        self.lon = lon
        self.q = lon // members
        self.pr = round_up(self.q, 8)
        self.ext = round_up(self.pr + 2 * REACH, 8)
        self.pe = 2 * self.pr
        self.p = members * self.pe
        self.cp = round_up(channels + noise, 128)
        self.ct = self.cp // 128
        self.cr = round_up(channels, 16)
        self.hp = round_up(hidden, 128)
        self.mc = channels // 128 * 128
        self.mh = hidden // 256 * 256

    def piece_rows(self, members, stacks):
        each = self.mc // members
        return next(n for n in range(8, each + 1, 8) if each % n == 0 and n * stacks >= each)


class Rows:
    def __init__(self, sz):
        self.mixing = 9
        self.outbias = self.mixing + sz.k
        self.biasin = self.outbias + 1
        self.row_e = self.biasin + 2
        self.row_r = self.row_e + 2
        self.spare = sz.h - sz.mh
        self.col_e = self.row_r + 2
        self.col_r = self.col_e + self.spare
        self.extra = self.col_r + self.spare
        self.count = round_up(self.extra + 1, 32)
        self.x_mixing = 9
        self.x_outbias = self.x_mixing + sz.k
        self.x_biasin = self.x_outbias + 1
        self.x_row_e = self.x_biasin + self.spare
        self.x_row_r = self.x_row_e + self.spare
        self.x_loss = self.x_row_r + self.spare


def smem():
    return pl.BlockSpec(memory_space=pltpu.SMEM)


def vmem():
    return pl.BlockSpec(memory_space=pltpu.VMEM)


def tile_sum(values):
    tiles = [values[i : i + 8] for i in range(0, values.shape[0], 8)]
    while len(tiles) > 1:
        tiles = [a + b for a, b in zip(tiles[::2], tiles[1::2])] + tiles[len(tiles) // 2 * 2 :]
    return tiles[0]


def column_blocks(width, step):
    return [(i, min(step, width - i)) for i in range(0, width, step)]


def norm_rows(values, channels, lanes):
    inside = lanes < channels
    values = jnp.where(inside, values, 0.0)
    mean = jnp.sum(values, axis=1, keepdims=True) * (1.0 / channels)
    centred = jnp.where(inside, values - mean, 0.0)
    spread = jnp.sum(centred * centred, axis=1, keepdims=True) * (1.0 / channels)
    return centred, lax.rsqrt(spread + NORM_EPS)


def gelu_parts(v):
    size = jnp.abs(v)
    t = 1.0 / (1.0 + (0.3275911 * math.sqrt(0.5)) * size)
    bell = jnp.exp(-0.5 * v * v)
    poly = t * (
        0.5 * 0.254829592
        + t * (-0.5 * 0.284496736 + t * (0.5 * 1.421413741 + t * (-0.5 * 1.453152027 + t * (0.5 * 1.061405429))))
    )
    tail = poly * bell
    cdf = jnp.where(v >= 0.0, 1.0 - tail, tail)
    return v * cdf, cdf + v * bell * (1.0 / math.sqrt(2.0 * math.pi))


def cost(microseconds):
    return pl.CostEstimate(flops=int(microseconds * 5e7), bytes_accessed=0, transcendentals=0)


def transpose_into(sz, src, dst):
    def move(at, count):
        for ct in range(sz.ct):
            block = src[pl.ds(at, count), ct * 128 : (ct + 1) * 128].T
            size = min(128, sz.cr - ct * 128)
            if size > 0:
                dst[ct * 128 : ct * 128 + size, pl.ds(at, count)] = block[:size]

    def body(i, c):
        move(pl.multiple_of(i * 128, 128), 128)
        return c

    lax.fori_loop(0, sz.p // 128, body, 0)
    if sz.p % 128:
        move(sz.p // 128 * 128, sz.p % 128)


def weight_grad(sz, core, left_ref, right_ref, left_t_ref, mine_ref, other_ref, row_ref, col_ref):
    transpose_into(sz, left_ref, left_t_ref)
    half = sz.mh // 2
    for half_ref, which in ((other_ref, 1 - core), (mine_ref, core)):
        for at, width in column_blocks(half, 256):
            cols = pl.ds(pl.multiple_of(which * half + at, 128), width)
            block = mm(left_t_ref[...], right_ref[:, cols])
            row_ref[:, cols] = block[sz.mc :]
            half_ref[:, at : at + width] = block[: sz.mc].astype(bf16)
    rest = right_ref[:, sz.mh :]
    row_ref[:, sz.mh :] = mm(left_t_ref[sz.mc :, :], rest)
    col_ref[...] = mm(rest.astype(f32).T[0:16].astype(bf16), left_ref[...])


def split_kernel(sz, shifts, heights_ref, band_ref, me_ref, x_hbm, noise_hbm, *refs):
    places, (y_ref, s_ref, x_ref, noise_ref, out_ref, in_sems, out_sems) = refs[: sz.m], refs[sz.m :]
    loads = []
    for ct in range(sz.ct):
        channels = pl.ds(ct * 128, min(128, sz.c - ct * 128))
        loads.append(pltpu.make_async_copy(x_hbm.at[:, channels], x_ref.at[:, channels], in_sems.at[ct]))
    loads.append(pltpu.make_async_copy(noise_hbm, noise_ref, in_sems.at[sz.ct]))
    for load in loads:
        load.start()
    for ct in range(sz.ct):
        first = ct * 128
        loads[ct].wait()
        if ct < sz.ct - 1:
            spans = [(x_ref, first, 128, 0)]
        else:
            rest = sz.c - first
            loads[sz.ct].wait()
            s_ref[...] = jnp.zeros_like(s_ref)
            spans = [(x_ref, first, rest, 0), (noise_ref, 0, sz.k, rest)]
        for ref, at, count, to in spans:
            for lt, width in column_blocks(sz.lon, 128):
                block = ref[0, at : at + count, :, lt : lt + width].astype(f32)
                s_ref[lt // 128, 2 * to : 2 * (to + count), :width] = block.reshape(2 * count, width)
        for r in range(2):
            for lt, width in column_blocks(sz.lon, 128):
                block = s_ref[lt // 128, pl.ds(r, 128, stride=2), :].T
                y_ref[r, ct, REACH + lt : REACH + lt + width, :] = block[:width]
    for r in range(2):
        for ct in range(sz.ct):
            y_ref[r, ct, :REACH, :] = y_ref[r, ct, sz.lon : sz.lon + REACH, :]
            y_ref[r, ct, REACH + sz.lon :, :] = y_ref[r, ct, REACH : sz.ext - sz.q, :]
    stores = []
    for s in (*range(1, sz.m), 0):
        start = (me_ref[0] ^ shifts[s]) * sz.q
        for r, row in enumerate((0, heights_ref[band_ref[0]] - 1)):
            for ct in range(sz.ct):
                out_ref[s, r, :, ct * 128 : (ct + 1) * 128] = y_ref[row, ct, pl.ds(start, sz.ext), :].astype(bf16)
        stores.append(pltpu.make_async_copy(out_ref.at[s], places[s], out_sems.at[s]))
        stores[-1].start()
    for store in stores:
        store.wait()


def split_call(sz, shifts, heights, band, me, x, noise):
    outs = tuple(jax.ShapeDtypeStruct((2, sz.ext, sz.cp), bf16) for _ in range(sz.m))
    anywhere = pl.BlockSpec(memory_space=pltpu.HBM)
    return pl.pallas_call(
        functools.partial(split_kernel, sz, shifts),
        out_shape=outs,
        in_specs=[smem(), smem(), smem(), anywhere, anywhere],
        out_specs=tuple(anywhere for _ in outs),
        scratch_shapes=[
            pltpu.VMEM((2, sz.ct, sz.lon + sz.ext - sz.q, 128), f32),
            pltpu.VMEM((round_up(sz.lon, 128) // 128, 256, 128), f32),
            pltpu.VMEM(x.shape, bf16),
            pltpu.VMEM(noise.shape, bf16),
            pltpu.VMEM((sz.m, 2, sz.ext, sz.cp), bf16),
            pltpu.SemaphoreType.DMA((sz.ct + 1,)),
            pltpu.SemaphoreType.DMA((sz.m,)),
        ],
        compiler_params=pltpu.CompilerParams(vmem_limit_bytes=50 * 1024 * 1024),
        cost_estimate=cost(5),
        name="split",
    )(heights, band, me, x, noise)


def join_kernel(sz, shifts, me_ref, *refs):
    pieces, out_ref, y_ref, t_ref, s_ref = refs[: sz.m], *refs[sz.m :]
    inner = slice(REACH, REACH + sz.q)
    starts = [(me_ref[0] ^ shift) * sz.q for shift in shifts]
    for s in range(sz.m):
        for r in range(2):
            for ct in range(sz.ct):
                part = pieces[s][r, :, ct * 128 : (ct + 1) * 128].astype(f32)
                y_ref[r, ct, pl.ds(starts[s] + REACH, sz.q), :] = part[inner]
                s_ref[s, r, ct, :REACH] = part[:REACH]
                s_ref[s, r, ct, REACH:] = part[REACH + sz.q : 2 * REACH + sz.q]
    for s in range(sz.m):
        left = jnp.where(starts[s] == 0, sz.lon, starts[s])
        right = jnp.where(starts[s] == sz.lon - sz.q, REACH, starts[s] + REACH + sz.q)
        for r in range(2):
            for ct in range(sz.ct):
                y_ref[r, ct, pl.ds(left, REACH), :] += s_ref[s, r, ct, :REACH]
                y_ref[r, ct, pl.ds(right, REACH), :] += s_ref[s, r, ct, REACH:]
    for ct in range(sz.ct):
        for r in range(2):
            for lt in range(0, sz.lon, 128):
                block = y_ref[r, ct, REACH + lt : REACH + lt + 128, :].T
                t_ref[lt // 128, pl.ds(r, 128, stride=2), :] = block
        size = min(128, sz.c - ct * 128)
        for lt, width in column_blocks(sz.lon, 128):
            block = t_ref[lt // 128, : 2 * size, :width].reshape(size, 2, width)
            out_ref[0, ct * 128 : ct * 128 + size, :, lt : lt + width] = block.astype(bf16)


def join_call(sz, shifts, me, pieces):
    return pl.pallas_call(
        functools.partial(join_kernel, sz, shifts),
        out_shape=jax.ShapeDtypeStruct((1, sz.c, 2, sz.lon), bf16),
        in_specs=[smem()] + [vmem()] * sz.m,
        out_specs=vmem(),
        scratch_shapes=[
            pltpu.VMEM((2, sz.ct, REACH + max(round_up(sz.lon, 128), sz.lon + sz.ext - sz.q - REACH), 128), f32),
            pltpu.VMEM((round_up(sz.lon, 128) // 128, 256, 128), f32),
            pltpu.VMEM((sz.m, 2, sz.ct, 2 * REACH, 128), f32),
        ],
        compiler_params=pltpu.CompilerParams(vmem_limit_bytes=24 * 1024 * 1024),
        cost_estimate=cost(6),
        name="join",
    )(me, *pieces)


def norm_and_filter(sz, e, height_ref, taps_ref, x_ref, prev_ref, next_ref, gain_ref, filter_ref, normed_ref, n_ref, fil_ref):
    lanes = lax.broadcasted_iota(jnp.int32, (1, sz.cp), 1)
    below_first = jnp.where(height_ref[0] == 2, 2, 3)
    sources = ((0, 1, below_first), (1, 2, 3))

    def norm_store(values, row):
        centred, inv = norm_rows(values.astype(f32), sz.c, lanes)
        normed = (centred * inv * gain_ref[...]).astype(bf16)
        normed_ref[e, row] = normed
        normed = normed.astype(f32)
        for ct in range(sz.ct):
            n_ref[row, ct] = normed[:, ct * 128 : (ct + 1) * 128]

    norm_store(prev_ref[e], 0)
    norm_store(x_ref[e, 0], 1)
    norm_store(x_ref[e, 1], 2)
    norm_store(next_ref[e], 3)

    def filter_tile(ct, c):
        for r in range(2):
            acc = jnp.zeros((sz.pr, 128), f32)
            for a in range(3):
                for j in range(3):
                    tap = 3 * a + j
                    start = taps_ref[tap, r] + REACH
                    moved = n_ref[sources[r][a], ct, pl.ds(start, sz.pr), :]
                    acc = acc + filter_ref[ct, tap : tap + 1, :] * moved
            fil_ref[ct, r * sz.pr : (r + 1) * sz.pr, :] = acc
        return c

    lax.fori_loop(0, sz.ct, filter_tile, 0)


def feed_forward(sz, e, x_ref, fil_ref, expand_ref, bias_ref, reduce_ref, outbias_ref, noisemix_ref, store):
    own = jnp.concatenate([x_ref[e, r].astype(f32)[REACH : REACH + sz.pr] for r in range(2)], axis=0)
    noise = own[:, (sz.ct - 1) * 128 :].astype(bf16)
    mixed = mm(jnp.concatenate([noise, noise], axis=1), noisemix_ref[...])
    filtered = jnp.concatenate([fil_ref[ct] for ct in range(sz.ct)], axis=1)
    lanes = lax.broadcasted_iota(jnp.int32, (1, sz.cp), 1)
    mixed = jnp.where(lanes == sz.c, 1.0, filtered + mixed).astype(bf16)
    store("mixed", slice(0, sz.cp), mixed)
    acts = []
    for at, width in column_blocks(sz.hp, 256):
        pre = mm(mixed, expand_ref[:, at : at + width]) + bias_ref[:, at : at + width]
        act, slope = gelu_parts(pre)
        if at <= sz.h < at + width:
            units = at + lax.broadcasted_iota(jnp.int32, (1, width), 1)
            act = jnp.where(units == sz.h, 1.0, act)
        acts.append(act.astype(bf16))
        store("act", slice(at, at + width), acts[-1])
        store("slope", slice(at, at + width), slope.astype(bf16))
    act = jnp.concatenate(acts, axis=1)
    return own + (mm(act, reduce_ref[...], NT) + outbias_ref[...])


def own_kernel(
    sz,
    height_ref,
    taps_ref,
    x_ref,
    prev_ref,
    next_ref,
    expand_ref,
    bias_ref,
    reduce_ref,
    gain_ref,
    outbias_ref,
    filter_ref,
    noisemix_ref,
    normed_ref,
    mx_ref,
    act_ref,
    dg_ref,
    pred_ref,
    n_ref,
    fil_ref,
):
    norm_and_filter(sz, 0, height_ref, taps_ref, x_ref, prev_ref, next_ref, gain_ref, filter_ref, normed_ref, n_ref, fil_ref)
    places = {"mixed": mx_ref, "act": act_ref, "slope": dg_ref}

    def store(name, cols, values):
        places[name][:, cols] = values

    pred_ref[...] = feed_forward(
        sz, 0, x_ref, fil_ref, expand_ref, bias_ref, reduce_ref, outbias_ref, noisemix_ref, store
    )


def filter_scratch(sz):
    return [pltpu.VMEM((4, sz.ct, sz.ext, 128), f32), pltpu.VMEM((sz.ct, sz.pe, 128), f32)]


def own_call(sz, height, taps, x, prev, after, weights):
    shape = jax.ShapeDtypeStruct
    outs = (
        shape((sz.m, 4, sz.ext, sz.cp), bf16),
        shape((sz.pe, sz.cp), bf16),
        shape((sz.pe, sz.hp), bf16),
        shape((sz.pe, sz.hp), bf16),
        shape((sz.pe, sz.cp), f32),
    )
    return pl.pallas_call(
        functools.partial(own_kernel, sz),
        grid=(1,),
        out_shape=outs,
        in_specs=[smem(), smem()] + [vmem()] * 10,
        out_specs=(pl.BlockSpec((1, 4, sz.ext, sz.cp), lambda i: (0, 0, 0, 0)),) + (vmem(),) * 4,
        scratch_shapes=filter_scratch(sz),
        compiler_params=pltpu.CompilerParams(vmem_limit_bytes=50 * 1024 * 1024),
        cost_estimate=cost(8),
        name="own",
    )(height, taps, x, prev, after, *weights)


def main_kernel(
    sz,
    height_ref,
    core_ref,
    taps_ref,
    bias_ref,
    gain_ref,
    outbias_ref,
    filter_ref,
    noisemix_ref,
    x_hbm,
    prev_hbm,
    next_hbm,
    target_hbm,
    expand_hbm,
    reduce_hbm,
    normed_own_hbm,
    mx_hbm,
    act_hbm,
    dg_hbm,
    pred_hbm,
    mine_hbm,
    other_hbm,
    bg_hbm,
    pg_hbm,
    normed_hbm,
    small_ref,
    x_ref,
    prev_ref,
    next_ref,
    target_ref,
    expand_ref,
    reduce_ref,
    mine_ref,
    other_ref,
    bg_ref,
    pg_ref,
    n_ref,
    fil_ref,
    nb_ref,
    mx_ref,
    act_ref,
    dg_ref,
    pred_ref,
    tr_ref,
    row_e_ref,
    row_r_ref,
    col_e_ref,
    col_r_ref,
    loss_ref,
    in_sems,
    out_sems,
):
    first = pl.ds(0, sz.pe)
    others = pl.ds(1, sz.m - 1)
    early = [
        pltpu.make_async_copy(x_hbm.at[others], x_ref, in_sems.at[0]),
        pltpu.make_async_copy(prev_hbm, prev_ref, in_sems.at[1]),
        pltpu.make_async_copy(next_hbm, next_ref, in_sems.at[2]),
    ]
    expand_load = pltpu.make_async_copy(expand_hbm, expand_ref, in_sems.at[3])
    reduce_load = pltpu.make_async_copy(reduce_hbm, reduce_ref, in_sems.at[4])
    loads = [
        pltpu.make_async_copy(mx_hbm, mx_ref.at[first], in_sems.at[5]),
        pltpu.make_async_copy(act_hbm, act_ref.at[first], in_sems.at[6]),
        pltpu.make_async_copy(dg_hbm, dg_ref.at[first], in_sems.at[7]),
        pltpu.make_async_copy(pred_hbm, pred_ref.at[0], in_sems.at[8]),
        pltpu.make_async_copy(target_hbm, target_ref, in_sems.at[9]),
    ]
    for load in (*early, expand_load, reduce_load, *loads):
        load.start()
    for load in early:
        load.wait()

    def forward(e, carry):
        norm_and_filter(
            sz, e, height_ref, taps_ref, x_ref, prev_ref, next_ref, gain_ref, filter_ref, nb_ref, n_ref, fil_ref
        )

        @pl.when(e == 0)
        def _():
            expand_load.wait()
            reduce_load.wait()

        rows = pl.ds(pl.multiple_of((e + 1) * sz.pe, 16), sz.pe)
        places = {"mixed": mx_ref, "act": act_ref, "slope": dg_ref}

        def store(name, cols, values):
            places[name][rows, cols] = values

        pred_ref[e + 1] = feed_forward(
            sz, e, x_ref, fil_ref, expand_ref, bias_ref, reduce_ref, outbias_ref, noisemix_ref, store
        )
        return carry

    lax.fori_loop(0, sz.m - 1, forward, 0)
    save = pltpu.make_async_copy(nb_ref, normed_hbm.at[pl.ds(1, sz.m - 1)], out_sems.at[0])
    save.start()
    for load in loads:
        load.wait()

    height = height_ref[0]
    lanes = lax.broadcasted_iota(jnp.int32, (1, sz.cp), 1)
    inside = (lanes < sz.c).astype(f32)
    loss_ref[...] = jnp.zeros_like(loss_ref)
    step = 16
    inv_m = 1.0 / sz.m
    inv_mm = inv_m * inv_m

    def score(i, carry):
        at = pl.multiple_of(i * step, step)
        pixel = at + lax.broadcasted_iota(jnp.int32, (step, 1), 0)
        row = (pixel >= sz.pr).astype(jnp.int32)
        use = (pixel - row * sz.pr < sz.q) & (row < height)
        mask_rows = use.astype(f32)
        for ct in range(sz.ct):
            cols = slice(ct * 128, (ct + 1) * 128)
            mask = mask_rows * inside[:, cols]
            preds = [pred_ref[e, pl.ds(at, step), cols] for e in range(sz.m)]
            truth = target_ref[pl.ds(at, step), cols].astype(f32)
            slopes = []
            own_sum = 0.0
            for p in preds:
                d = p - truth
                q = d * d + 1.0
                r = lax.rsqrt(q)
                own_sum = own_sum + q * r
                slopes.append(d * r * inv_m)
            pair_sum = 0.0
            pairs = [0.0] * sz.m
            for a in range(sz.m):
                for b in range(a + 1, sz.m):
                    d = preds[a] - preds[b]
                    q = d * d + 1.0
                    r = lax.rsqrt(q)
                    pair_sum = pair_sum + q * r
                    s = d * r
                    pairs[a] = pairs[a] + s
                    pairs[b] = pairs[b] - s
            value = own_sum * inv_m - (pair_sum + 0.5 * sz.m) * inv_mm
            value = mask * value
            loss_ref[:, cols] += value[0:8] + value[8:16]
            for e in range(sz.m):
                g = (mask * (slopes[e] - pairs[e] * inv_mm)).astype(bf16)
                where = pl.ds(pl.multiple_of(e * sz.pe + at, 16), step)
                bg_ref[where, cols] = g
        return carry

    lax.fori_loop(0, sz.pe // step, score, 0)
    core = core_ref[0]
    saves = [save]

    def write(here, there, which):
        saves.append(pltpu.make_async_copy(here, there, out_sems.at[which]))
        saves[-1].start()

    write(bg_ref, bg_hbm, 1)
    weight_grad(sz, core, bg_ref, act_ref, tr_ref, mine_ref.at[1], other_ref.at[1], row_r_ref, col_r_ref)
    write(mine_ref.at[1], mine_hbm.at[1], 2)
    write(other_ref.at[1], other_hbm.at[1], 3)


    def backward(e, carry):
        rows = pl.ds(pl.multiple_of(e * sz.pe, 16), sz.pe)
        bg = bg_ref[rows, :]
        for at, width in column_blocks(sz.hp, 256):
            grad = mm(bg, reduce_ref[:, at : at + width])
            pre = (grad * dg_ref[rows, at : at + width].astype(f32)).astype(bf16)
            pg_ref[rows, at : at + width] = pre
        return carry

    lax.fori_loop(0, sz.m, backward, 0)
    write(pg_ref, pg_hbm, 4)
    weight_grad(sz, core, mx_ref, pg_ref, tr_ref, mine_ref.at[0], other_ref.at[0], row_e_ref, col_e_ref)
    write(other_ref.at[0], other_hbm.at[0], 5)
    write(mine_ref.at[0], mine_hbm.at[0], 6)
    at = Rows(sz)
    small_ref[...] = jnp.zeros_like(small_ref)
    lane = lax.broadcasted_iota(jnp.int32, (1, sz.mc), 1)
    half = sz.mh // 2

    def column_sum(ref):
        return jnp.sum(ref[...], axis=0, keepdims=True)

    def long_row(row, place, values, extra):
        small_ref[row : row + 1, :] = values[:, :half]
        small_ref[row + 1 : row + 2, :] = values[:, half : sz.mh]
        for i in range(at.spare):
            extra = jnp.where(lane == place + i, values[:, sz.mh + i : sz.mh + i + 1], extra)
        return extra

    extra = jnp.zeros((1, sz.mc), f32)
    outbias_grad = col_r_ref[at.spare : at.spare + 1, :]
    small_ref[at.outbias : at.outbias + 1, :] = outbias_grad[:, : sz.mc]
    extra = jnp.where(lane == at.x_outbias, outbias_grad[:, sz.mc : sz.mc + 1], extra)
    extra = long_row(at.biasin, at.x_biasin, row_e_ref[sz.c - sz.mc : sz.c - sz.mc + 1, :], extra)
    extra = long_row(at.row_e, at.x_row_e, row_e_ref[0:1, :], extra)
    extra = long_row(at.row_r, at.x_row_r, row_r_ref[0:1, :], extra)
    small_ref[at.col_e : at.col_e + at.spare, :] = col_e_ref[: at.spare, : sz.mc]
    small_ref[at.col_r : at.col_r + at.spare, :] = col_r_ref[: at.spare, : sz.mc]
    extra = jnp.where(lane == at.x_loss, jnp.sum(column_sum(loss_ref), axis=1, keepdims=True), extra)
    small_ref[at.extra : at.extra + 1, :] = extra
    for save in saves:
        save.wait()


def main_call(sz, height, core, taps, x, prev, after, target, weights, state):
    shape = jax.ShapeDtypeStruct
    half = shape((2, sz.mc, sz.mh // 2), bf16)
    outs = (
        half,
        half,
        shape((sz.p, sz.cp), bf16),
        shape((sz.p, sz.hp), bf16),
        shape((sz.m, 4, sz.ext, sz.cp), bf16),
        shape((Rows(sz).count, sz.mc), f32),
    )
    anywhere = pl.BlockSpec(memory_space=pl.ANY)
    expand, bias, reduce, gain, outbias, filt, noisemix = weights
    return pl.pallas_call(
        functools.partial(main_kernel, sz),
        out_shape=outs,
        in_specs=[smem()] * 3 + [vmem()] * 5 + [anywhere] * 11,
        out_specs=(anywhere,) * 5 + (vmem(),),
        input_output_aliases={14: 4},
        scratch_shapes=[
            pltpu.VMEM((sz.m - 1, 2, sz.ext, sz.cp), bf16),
            pltpu.VMEM((sz.m - 1, sz.ext, sz.cp), bf16),
            pltpu.VMEM((sz.m - 1, sz.ext, sz.cp), bf16),
            pltpu.VMEM((sz.pe, sz.cp), bf16),
            pltpu.VMEM((sz.cp, sz.hp), bf16),
            pltpu.VMEM((sz.cp, sz.hp), bf16),
            pltpu.VMEM((2, sz.mc, sz.mh // 2), bf16),
            pltpu.VMEM((2, sz.mc, sz.mh // 2), bf16),
            pltpu.VMEM((sz.p, sz.cp), bf16),
            pltpu.VMEM((sz.p, sz.hp), bf16),
            *filter_scratch(sz),
            pltpu.VMEM((sz.m - 1, 4, sz.ext, sz.cp), bf16),
            pltpu.VMEM((sz.p, sz.cp), bf16),
            pltpu.VMEM((sz.p, sz.hp), bf16),
            pltpu.VMEM((sz.p, sz.hp), bf16),
            pltpu.VMEM((sz.m, sz.pe, sz.cp), f32),
            pltpu.VMEM((sz.cr, sz.p), bf16),
            pltpu.VMEM((sz.cr - sz.mc, sz.hp), f32),
            pltpu.VMEM((sz.cr - sz.mc, sz.hp), f32),
            pltpu.VMEM((16, sz.cp), f32),
            pltpu.VMEM((16, sz.cp), f32),
            pltpu.VMEM((8, sz.cp), f32),
            pltpu.SemaphoreType.DMA((10,)),
            pltpu.SemaphoreType.DMA((7,)),
        ],
        compiler_params=pltpu.CompilerParams(vmem_limit_bytes=50 * 1024 * 1024),
        cost_estimate=cost(40),
        name="main",
    )(height, core, taps, bias, gain, outbias, filt, noisemix, x, prev, after, target, expand, reduce, *state)


def unmix_kernel(
    sz,
    base,
    count,
    height_ref,
    taps_ref,
    filter_ref,
    small_in_ref,
    pg_hbm,
    x_hbm,
    normed_hbm,
    expand_hbm,
    gn_own_hbm,
    gn_prev_hbm,
    gn_next_hbm,
    small_ref,
    pg_ref,
    x_ref,
    normed_ref,
    expand_ref,
    own_ref,
    edge_ref,
    filter_grad_ref,
    mixing_grad_ref,
    n_ref,
    gn_ref,
    gm_ref,
    in_sems,
    out_sems,
):
    below_first = jnp.where(height_ref[0] == 2, 2, 3)
    sources = ((0, 1, below_first), (1, 2, 3))
    last = sz.ct - 1
    weights = pltpu.make_async_copy(expand_hbm, expand_ref, in_sems.at[0])
    weights.start()
    loads = []
    for e in range(count):
        rows = pl.ds((base + e) * sz.pe, sz.pe)
        channels = pl.ds(last * 128, 128)
        loads.append(
            (
                pltpu.make_async_copy(pg_hbm.at[rows], pg_ref.at[e], in_sems.at[3 * e + 1]),
                pltpu.make_async_copy(x_hbm.at[base + e, :, :, channels], x_ref.at[e], in_sems.at[3 * e + 2]),
                pltpu.make_async_copy(normed_hbm.at[base + e], normed_ref.at[e], in_sems.at[3 * e + 3]),
            )
        )
    for load in loads[0]:
        load.start()
    filter_grad_ref[...] = jnp.zeros_like(filter_grad_ref)
    mixing_grad_ref[...] = jnp.zeros_like(mixing_grad_ref)
    pad = 2 * REACH
    for r in range(2):
        for ct in range(sz.ct):
            gm_ref[r, ct, :pad, :] = jnp.zeros((pad, 128), f32)
            gm_ref[r, ct, pad + sz.pr :, :] = jnp.zeros((sz.ext + REACH - sz.pr, 128), f32)
    weights.wait()
    stores = []
    for e in range(count):
        loads[e][0].wait()
        if e + 1 < count:
            for load in loads[e + 1]:
                load.start()
        gm = mm(pg_ref[e], expand_ref[...], NT)
        for r in range(2):
            for ct in range(sz.ct):
                gm_ref[r, ct, pad : pad + sz.pr, :] = gm[r * sz.pr : (r + 1) * sz.pr, ct * 128 : (ct + 1) * 128]
        for load in loads[e][1:]:
            load.wait()
        for row in range(4):
            normed = normed_ref[e, row].astype(f32)
            for ct in range(sz.ct):
                n_ref[row, ct] = normed[:, ct * 128 : (ct + 1) * 128]
        noise = jnp.concatenate([x_ref[e, r].astype(f32)[REACH : REACH + sz.pr] for r in range(2)], axis=0)
        mixing_grad_ref[...] += mm(noise.T[0:16].astype(bf16), gm.astype(bf16))

        def unfilter_tile(ct, c):
            def gathered(*readers):
                acc = jnp.zeros((sz.ext, 128), f32)
                for r, a in readers:
                    for tap in range(3 * a, 3 * a + 3):
                        start = REACH - taps_ref[tap, r]
                        acc = acc + filter_ref[ct, tap : tap + 1, :] * gm_ref[r, ct, pl.ds(start, sz.ext), :]
                return acc

            gn_ref[0, ct] = gathered((0, 0))
            gn_ref[1, ct] = gathered((0, 1), (1, 0))
            gn_ref[2, ct] = gathered((1, 1))
            gn_ref[3, ct] = gathered((1, 2))
            gn_ref[below_first, ct] += gathered((0, 2))
            for r in range(2):
                g = gm_ref[r, ct, pad : pad + sz.pr, :]
                for a in range(3):
                    for tap in range(3 * a, 3 * a + 3):
                        read = n_ref[sources[r][a], ct, pl.ds(taps_ref[tap, r] + REACH, sz.pr), :]
                        filter_grad_ref[ct, tap] += tile_sum(g * read)
            return c

        lax.fori_loop(0, sz.ct, unfilter_tile, 0)
        for ct in range(sz.ct):
            cols = slice(ct * 128, (ct + 1) * 128)
            edge_ref[e, 0, :, cols] = gn_ref[0, ct].astype(bf16)
            edge_ref[e, 1, :, cols] = gn_ref[3, ct].astype(bf16)
            own_ref[e, 0, :, cols] = gn_ref[1, ct].astype(bf16)
            own_ref[e, 1, :, cols] = gn_ref[2, ct].astype(bf16)
        stores += [
            pltpu.make_async_copy(own_ref.at[e], gn_own_hbm.at[e], out_sems.at[3 * e]),
            pltpu.make_async_copy(edge_ref.at[e, 0], gn_prev_hbm.at[e], out_sems.at[3 * e + 1]),
            pltpu.make_async_copy(edge_ref.at[e, 1], gn_next_hbm.at[e], out_sems.at[3 * e + 2]),
        ]
        for store in stores[-3:]:
            store.start()

    at = Rows(sz)
    lane = lax.broadcasted_iota(jnp.int32, (1, sz.mc), 1)
    small_ref[...] = small_in_ref[...]
    extra = small_in_ref[at.extra : at.extra + 1, :]
    first = sz.c - last * 128
    for tap in range(9):
        for ct in range(last):
            row = jnp.sum(filter_grad_ref[ct, tap], axis=0, keepdims=True)
            small_ref[tap : tap + 1, ct * 128 : (ct + 1) * 128] += row
        row = jnp.sum(filter_grad_ref[last, tap], axis=0, keepdims=True)
        extra = extra + jnp.where(lane == tap, row[:, 0:1], 0.0)
    mixing = mixing_grad_ref[first : first + sz.k, :]
    small_ref[at.mixing : at.mixing + sz.k, :] += mixing[:, : sz.mc]
    for i in range(sz.k):
        extra = extra + jnp.where(lane == at.x_mixing + i, mixing[i : i + 1, sz.mc : sz.mc + 1], 0.0)
    small_ref[at.extra : at.extra + 1, :] = extra
    for store in stores:
        store.wait()


def unmix_call(sz, base, count, height, taps, pg, x, normed, expand, filt, small):
    shape = jax.ShapeDtypeStruct
    outs = (
        shape((count, 2, sz.ext, sz.cp), bf16),
        shape((count, sz.ext, sz.cp), bf16),
        shape((count, sz.ext, sz.cp), bf16),
        shape(small.shape, f32),
    )
    anywhere = pl.BlockSpec(memory_space=pltpu.HBM)
    return pl.pallas_call(
        functools.partial(unmix_kernel, sz, base, count),
        out_shape=outs,
        in_specs=[smem(), smem(), vmem(), vmem()] + [anywhere] * 4,
        out_specs=(anywhere,) * 3 + (vmem(),),
        scratch_shapes=[
            pltpu.VMEM((count, sz.pe, sz.hp), bf16),
            pltpu.VMEM((count, 2, sz.ext, 128), bf16),
            pltpu.VMEM((count, 4, sz.ext, sz.cp), bf16),
            pltpu.VMEM((sz.cp, sz.hp), bf16),
            pltpu.VMEM((count, 2, sz.ext, sz.cp), bf16),
            pltpu.VMEM((count, 2, sz.ext, sz.cp), bf16),
            pltpu.VMEM((sz.ct, 9, 8, 128), f32),
            pltpu.VMEM((16, sz.cp), f32),
            pltpu.VMEM((4, sz.ct, sz.ext, 128), f32),
            pltpu.VMEM((4, sz.ct, sz.ext, 128), f32),
            pltpu.VMEM((2, sz.ct, sz.ext + 3 * REACH, 128), f32),
            pltpu.SemaphoreType.DMA((3 * count + 1,)),
            pltpu.SemaphoreType.DMA((3 * count,)),
        ],
        compiler_params=pltpu.CompilerParams(vmem_limit_bytes=28 * 1024 * 1024),
        cost_estimate=cost(5 * count),
        name="unmix",
    )(height, taps, filt, small, *(pltpu.with_memory_space_constraint(v, pltpu.HBM) for v in (pg, x, normed, expand)))


def norm_back_kernel(sz, height_ref, x_ref, gn_ref, up_ref, down_ref, bg_ref, gain_ref, out_ref):
    height = height_ref[0]
    lanes = lax.broadcasted_iota(jnp.int32, (1, sz.cp), 1)
    from_up = up_ref[0].astype(f32)
    from_down = down_ref[0].astype(f32)
    direct = bg_ref[...].astype(f32)
    for r in range(2):
        centred, inv = norm_rows(x_ref[0, r].astype(f32), sz.c, lanes)
        xhat = centred * inv
        g = gn_ref[0, r].astype(f32) + jnp.where(height == r + 1, from_down, 0.0)
        if r == 0:
            g = g + from_up
        q = g * gain_ref[...]
        mean_q = jnp.sum(q, axis=1, keepdims=True) * (1.0 / sz.c)
        mean_qx = jnp.sum(q * xhat, axis=1, keepdims=True) * (1.0 / sz.c)
        result = (q - mean_q - xhat * mean_qx) * inv
        part = result[REACH : REACH + sz.pr] + direct[r * sz.pr : (r + 1) * sz.pr]
        pieces = [result[:REACH], part, result[REACH + sz.pr :]]
        out_ref[0, r] = jnp.concatenate(pieces, axis=0).astype(bf16)


def norm_back_call(sz, base, count, height, x, gn, up, down, bg, gain):
    return pl.pallas_call(
        functools.partial(norm_back_kernel, sz),
        grid=(count,),
        out_shape=jax.ShapeDtypeStruct((count, 2, sz.ext, sz.cp), bf16),
        in_specs=[
            smem(),
            pl.BlockSpec((1, 2, sz.ext, sz.cp), lambda i: (i + base, 0, 0, 0)),
            pl.BlockSpec((1, 2, sz.ext, sz.cp), lambda i: (i, 0, 0, 0)),
            pl.BlockSpec((1, sz.ext, sz.cp), lambda i: (i, 0, 0)),
            pl.BlockSpec((1, sz.ext, sz.cp), lambda i: (i, 0, 0)),
            pl.BlockSpec((sz.pe, sz.cp), lambda i: (i + base, 0)),
            pl.BlockSpec((1, sz.cp), lambda i: (0, 0)),
        ],
        out_specs=pl.BlockSpec((1, 2, sz.ext, sz.cp), lambda i: (i, 0, 0, 0)),
        compiler_params=pltpu.CompilerParams(vmem_limit_bytes=14 * 1024 * 1024),
        cost_estimate=cost(2 * count),
        name="norm_back",
    )(height, x, gn, up, down, bg, gain)


def adam_kernel(sz, limit, pixels, members, stacks, place_ref, heights_ref, *refs):
    mine_ref, got_ref, small_mine_ref, small_got_ref = refs[:4]
    ins, small_ins, (norm_ref, mean_ref) = refs[4:10], refs[10:22], refs[22:24]
    outs, small_outs = refs[24:32], refs[32:44]
    factor_ref, small_ref, column_ref, cols_ref, gain_ref = refs[44:]
    at = Rows(sz)
    step = pl.program_id(0)
    core, member, stack = place_ref[0], place_ref[1], place_ref[2]
    half = sz.mh // 2
    each = sz.mc // members
    rows = sz.piece_rows(members, stacks)

    def wide(row, count, place):
        return jnp.concatenate([small_ref[row : row + count, :], column_ref[place : place + count, 0:1]], axis=1)

    def long(row, place):
        extra = small_ref[at.extra : at.extra + 1, place : place + at.spare]
        return jnp.concatenate([small_ref[row : row + 1, :], small_ref[row + 1 : row + 2, :], extra], axis=1)

    @pl.when(step == 0)
    def _():
        part = at.count // 2
        for which, ref in ((core, small_mine_ref), (1 - core, small_got_ref)):
            where = pl.ds(pl.multiple_of(which * part, part), part)
            values = ref[...].astype(f32)
            small_ref[where, :] = values[:part] + values[part:]
        extra = small_ref[at.extra : at.extra + 1, 0:128]
        column_ref[...] = jnp.broadcast_to(extra, (8, 128)).T
        total = jnp.zeros((8, half), f32)
        for ref in (mine_ref, got_ref):

            def body(i, acc):
                values = ref[i].astype(f32)
                values = values * values
                for j in range(0, rows, 8):
                    acc = acc + values[j : j + 8]
                return acc

            total = lax.fori_loop(0, 2 * members * stacks, body, total)
        count = jnp.sum(total)
        filter_grad = wide(0, 9, 0)
        gain_row = jnp.sum(small_ins[0][...] * filter_grad, axis=0, keepdims=True) / small_ins[6][0:1, :]
        gain_ref[...] = gain_row
        cols = small_ref[at.col_e : at.extra, :]
        for values in (
            filter_grad,
            wide(at.mixing, sz.k, at.x_mixing),
            gain_row,
            wide(at.outbias, 1, at.x_outbias),
            long(at.biasin, at.x_biasin),
            long(at.row_e, at.x_row_e),
            long(at.row_r, at.x_row_r),
            cols,
        ):
            count = count + jnp.sum(values * values)
        norm = jnp.sqrt(jnp.full((8, 128), count, f32))
        factor_ref[...] = jnp.minimum(1.0, limit / (norm + 1e-06))
        live = heights_ref[0]
        for i in range(1, heights_ref.shape[0]):
            live = live + heights_ref[i]
        loss = column_ref[at.x_loss : at.x_loss + 1, 0:1]
        mean = loss / (jnp.full((8, 128), pixels, f32) * live.astype(f32))
        norm_ref[0] = norm[0, 0]
        mean_ref[0] = mean[0, 0]
        cols_ref[...] = jnp.concatenate([cols, jnp.zeros((8 - 2 * at.spare, sz.mc), f32)], axis=0).T

    factor = factor_ref[0:1, 0:1]

    def adam(w, g, m, v, rate):
        g = factor * g
        m_new = BETA_ONE * m + (1.0 - BETA_ONE) * g
        v_new = BETA_TWO * v + (1.0 - BETA_TWO) * g * g
        v_hat = v_new * (1.0 / (1.0 - BETA_TWO**STEP))
        root = v_hat * lax.rsqrt(v_hat) + ADAM_EPS
        inverse = pl.reciprocal(root, approx=True)
        inverse = inverse * (2.0 - root * inverse)
        change = m_new * (rate / (1.0 - BETA_ONE**STEP)) * inverse
        return w * (1.0 - rate * DECAY_RATE) - change, m_new, v_new

    kinds = ((0, at.row_e, at.x_row_e, sz.c**-0.5), (1, at.row_r, at.x_row_r, sz.h**-0.5))

    @pl.when(step < sz.mc // ROWS)
    def _():
        first_core = core == 0
        for i in range(ROWS // rows):
            first = step * ROWS + i * rows
            t = member ^ (first // each)
            s = stack ^ ((first % each) // rows)
            where = pl.ds(pl.multiple_of(first, 8), rows)
            to = slice(i * rows, (i + 1) * rows)
            for kind, _, _, rate in kinds:
                slot = (t * stacks + s) * 2 + kind
                mine = mine_ref[slot].astype(f32)
                got = got_ref[slot].astype(f32)
                low = jnp.where(first_core, mine, got)
                high = jnp.where(first_core, got, mine)
                cols = cols_ref[where, kind * at.spare : (kind + 1) * at.spare]
                g = jnp.concatenate([low, high, cols], axis=1)
                w_ref, m_ref, v_ref = ins[3 * kind : 3 * kind + 3]
                w_out, m_out, v_out, c_out = outs[4 * kind : 4 * kind + 4]
                w, m, v = adam(w_ref[where, :], g, m_ref[where, :], v_ref[where, :], rate)
                w_out[to, :] = w
                m_out[to, :] = m
                v_out[to, :] = v
            if (i + 1) * rows % 16 == 0:
                both = slice((i + 1) * rows // 16 * 16 - max(16, rows * 2), (i + 1) * rows)
                for kind in range(2):
                    outs[4 * kind + 3][both, :] = outs[4 * kind][both, :].astype(bf16)

    @pl.when(step == sz.mc // ROWS)
    def _():
        last = slice(sz.mc, sz.c)
        for kind, row, place, rate in kinds:
            w_ref, m_ref, v_ref = ins[3 * kind : 3 * kind + 3]
            w_out, m_out, v_out, c_out = outs[4 * kind : 4 * kind + 4]
            w, m, v = adam(w_ref[last, :], long(row, place), m_ref[last, :], v_ref[last, :], rate)
            w_out[0:1, :] = w
            m_out[0:1, :] = m
            v_out[0:1, :] = v
            c_out[0:16, :] = jnp.broadcast_to(w, (16, sz.h)).astype(bf16)

    @pl.when(step == 0)
    def _():
        grads = (
            wide(0, 9, 0),
            wide(at.mixing, sz.k, at.x_mixing),
            jnp.concatenate([gain_ref[...], wide(at.outbias, 1, at.x_outbias)], axis=0),
            long(at.biasin, at.x_biasin),
        )
        for i, g in enumerate(grads):
            new = adam(small_ins[3 * i][...], g, small_ins[3 * i + 1][...], small_ins[3 * i + 2][...], SMALL_RATE)
            for ref, values in zip(small_outs[3 * i : 3 * i + 3], new):
                ref[...] = values.reshape(ref.shape)


ROWS = 80


def adam_call(sz, limit, pixels, members, stacks, place, heights, grads, weights, small_weights):
    shape = jax.ShapeDtypeStruct
    full = shape((sz.c, sz.h), f32)
    low = shape((sz.c, sz.h), bf16)
    outs = (shape((1,), f32),) * 2 + (full, full, full, low) * 2 + tuple(shape(v.shape if v.shape[0] > 1 else v.shape[1:], f32) for v in small_weights)
    block = pl.BlockSpec((ROWS, sz.h), lambda i: (i, 0))
    steps = sz.mc // ROWS + 1
    return pl.pallas_call(
        functools.partial(adam_kernel, sz, limit, pixels, members, stacks),
        grid=(steps,),
        out_shape=outs,
        in_specs=[smem()] * 2 + [vmem()] * (4 + 6) + [vmem()] * 12,
        out_specs=(smem(),) * 2 + (block,) * 8 + (vmem(),) * 12,
        scratch_shapes=[
            pltpu.VMEM((8, 128), f32),
            pltpu.VMEM((Rows(sz).count, sz.mc), f32),
            pltpu.VMEM((128, 8), f32),
            pltpu.VMEM((sz.mc, 8), f32),
            pltpu.VMEM((1, sz.c), f32),
        ],
        compiler_params=pltpu.CompilerParams(vmem_limit_bytes=24 * 1024 * 1024),
        cost_estimate=cost(16),
        name="adam",
    )(place, heights, *grads, *weights, *small_weights)


def exchange(pieces, axis, count, shifts):
    return [
        piece if s == 0 else lax.ppermute(piece, axis, [(i, i ^ s) for i in range(count)])
        for piece, s in zip(pieces, shifts)
    ]


def scatter_over(values, axis, count, size):
    me = lax.axis_index(axis)
    values = jnp.pad(values, ((0, 0), (0, count * size - values.shape[1]), (0, 0)))
    pieces = [lax.dynamic_slice_in_dim(values, (me ^ s) * size, size, axis=1) for s in range(count)]
    return exchange(pieces, axis, count, range(count))


def added(parts):
    return sum(part.astype(f32) for part in parts).astype(bf16)


def two_parts(values):
    coarse = lax.reduce_precision(values, exponent_bits=8, mantissa_bits=7)
    return coarse.astype(bf16), (values - coarse).astype(bf16)


def after_all(values, *others):
    return lax.optimization_barrier((values, others))[0]


def pad_to(values, shape):
    return jnp.pad(values, [(0, n - m) for n, m in zip(shape, values.shape)])


def on_device(
    fields,
    noise_fields,
    target_fields,
    band_heights,
    tap_offsets,
    expand_weight,
    expand_bias,
    reduce_weight,
    channel_vectors,
    disco_filter,
    noise_mixing,
    first_expand,
    second_expand,
    first_bias,
    second_bias,
    first_reduce,
    second_reduce,
    first_vectors,
    second_vectors,
    first_filter,
    second_filter,
    first_mixing,
    second_mixing,
):
    members = lax.axis_size("member")
    stacks = lax.axis_size("stack")
    lat_count = 2 * stacks
    lat = ("stack", "core")
    channels, hidden = expand_weight.shape
    lon = fields.shape[3]
    sz = Sizes(members, channels, hidden, noise_fields.shape[1], lon)
    me = lax.axis_index("member")
    core = lax.axis_index("core")
    band = lax.axis_index("stack") * 2 + core
    height = lax.dynamic_slice_in_dim(band_heights, band, 1)

    shifts = [0, members - 1, *range(1, members - 1)]
    pieces = split_call(sz, shifts, band_heights, band.reshape(1), me.reshape(1), fields, noise_fields)
    arrived = exchange(pieces, "member", members, shifts)
    upward = [(i, i + 1) for i in range(lat_count - 1)]
    downward = [(i + 1, i) for i in range(lat_count - 1)]

    def edges(rows):
        bottom = jnp.stack([x[1] for x in rows])
        top = jnp.stack([x[0] for x in rows])
        return lax.ppermute(bottom, lat, upward), lax.ppermute(top, lat, downward)

    truth = pad_to(target_fields, (channels, 2, lon + sz.pr - sz.q))
    truth = lax.dynamic_slice_in_dim(truth, me * sz.q, sz.pr, axis=2)
    truth = pad_to(jnp.transpose(truth, (1, 2, 0)), (2, sz.pr, sz.cp)).reshape(sz.pe, sz.cp)

    expand_low = pad_to(after_all(expand_weight, pieces).astype(bf16), (sz.cp, sz.hp))
    reduce_low = pad_to(reduce_weight.T.astype(bf16), (sz.cp, sz.hp))
    bias = pad_to(expand_bias[None], (1, sz.hp))
    gain = pad_to(channel_vectors[0:1], (1, sz.cp))
    outbias = pad_to(channel_vectors[1:2], (1, sz.cp))
    filt = jnp.transpose(pad_to(disco_filter, (16, sz.cp)).reshape(16, sz.ct, 128), (1, 0, 2))
    spot = channels - (sz.ct - 1) * 128
    coarse, fine = two_parts(noise_mixing)
    noisemix = jnp.zeros((256, sz.cp), bf16)
    noisemix = noisemix.at[spot : spot + sz.k, :channels].set(coarse)
    noisemix = noisemix.at[128 + spot : 128 + spot + sz.k, :channels].set(fine)

    weights = (expand_low, bias, reduce_low, gain, outbias, filt, noisemix)
    core_id = core.reshape(1)
    own_edges = edges(after_all(arrived[:1], expand_low))
    state = own_call(sz, height, tap_offsets, arrived[0][None], *own_edges, weights)
    others = after_all(arrived[1:], state)
    other_edges = edges(others)
    x = jnp.stack([arrived[0], *others])
    mine, other, bg, pg, normed, small = main_call(
        sz, height, core_id, tap_offsets, x, *other_edges, truth, weights, state
    )

    swap = [(0, 1), (1, 0)]
    part = (mine.astype(f32) + lax.ppermute(other, "core", swap).astype(f32)).astype(bf16)
    cut = members // 2

    def unmix_raw(base, count, pg, small):
        gn, gn_prev, gn_next, small = unmix_call(
            sz, base, count, height, tap_offsets, pg, x, normed, expand_low, filt, small
        )
        return (gn, gn_prev, gn_next), small

    def edges_back(raw):
        gn, gn_prev, gn_next = raw
        return gn, lax.ppermute(gn_next, lat, upward), lax.ppermute(gn_prev, lat, downward)

    def unmix(base, count, pg, small):
        raw, small = unmix_raw(base, count, pg, small)
        return edges_back(raw), small, raw[1]

    arriving = scatter_over(part, "member", members, sz.mc // members)
    near, small, done = unmix(0, cut, after_all(pg, part), small)
    arriving, done = after_all((arriving, done))
    arriving = scatter_over(added(arriving), "stack", stacks, sz.piece_rows(members, stacks))
    far_raw, small = unmix_raw(cut, members - cut, after_all(pg, done), small)

    def packed(main, small):
        return jnp.concatenate([main, *two_parts(small)], axis=0)

    def unpacked(messages):
        cut = messages[0].shape[0] - at.count
        half = at.count // 2
        parts = [m[cut:].astype(f32) for m in messages]
        return jnp.concatenate([m[:cut] for m in messages], axis=0), sum(p[:half] + p[half:] for p in parts)

    at = Rows(sz)
    arriving, far_raw, near, small = after_all((arriving, far_raw, near, small))
    small = small.reshape(2, -1, sz.mc)
    other_small = lax.dynamic_index_in_dim(small, 1 - core, 0, keepdims=False)
    small = lax.dynamic_index_in_dim(small, core, 0, keepdims=False) + lax.ppermute(other_small, "core", swap)
    near_grads = norm_back_call(sz, 0, cut, height, x, *near, bg, gain)
    small, part = after_all((small, added(arriving)))
    message = packed(part.reshape(-1, sz.mh // 2), small)
    gathered = exchange([message] * stacks, "stack", stacks, range(stacks))
    returned = exchange([near_grads[s] for s in range(cut)], "member", members, shifts[:cut])

    gathered, far_raw, returned = after_all((gathered, far_raw, returned))
    message = packed(*unpacked(gathered))
    gathered = exchange([message] * members, "member", members, range(members))
    far = edges_back(far_raw)

    far_grads = norm_back_call(sz, cut, members - cut, height, x, *far, bg, gain)
    far_pieces = [far_grads[s] for s in range(members - cut)]

    gathered, far_pieces = after_all((gathered, far_pieces))
    mine, small = unpacked(gathered)
    small = packed(mine[:0], small)
    got = lax.ppermute(mine, "core", swap)
    got_small = lax.ppermute(small, "core", swap)
    returned = returned + exchange(far_pieces, "member", members, shifts[cut:])
    pieces = [v.reshape(-1, sz.piece_rows(members, stacks), sz.mh // 2) for v in (mine, got)]

    limit = 0.02 * math.sqrt(hidden * channels * lat_count * 2 * lon / members)
    norm, mean, we, m_e, v_e, c_e, wr, m_r, v_r, c_r, *rest = adam_call(
        sz,
        limit,
        channels * lon,
        members,
        stacks,
        jnp.stack([core, me, lax.axis_index("stack")]),
        band_heights,
        (*pieces, small, got_small),
        (expand_weight, first_expand, second_expand, reduce_weight.T, first_reduce.T, second_reduce.T),
        (
            disco_filter,
            first_filter,
            second_filter,
            noise_mixing,
            first_mixing,
            second_mixing,
            channel_vectors,
            first_vectors,
            second_vectors,
            expand_bias[None],
            first_bias[None],
            second_bias[None],
        ),
    )
    input_gradient = join_call(sz, shifts, me.reshape(1), after_all(returned, norm))
    return (
        mean[0],
        input_gradient,
        norm[0],
        we,
        m_e,
        v_e,
        *rest[9:12],
        wr.T,
        m_r.T,
        v_r.T,
        *rest[6:9],
        *rest[0:3],
        *rest[3:6],
        c_e,
        c_r.T,
    )


def solution(mesh):
    members = mesh.shape["member"]
    lat = mesh.shape["lat"]
    split = Mesh(mesh.devices.reshape(members, lat // 2, 2), ("member", "stack", "core"))
    rows = ("stack", "core")
    whole = [P()] * 18
    in_specs = (
        P("member", None, rows, None),
        P("member", None, rows, None),
        P(None, rows, None),
        P(),
        P(None, rows),
        *whole,
    )
    out_specs = (P(), P("member", None, rows, None)) + (P(),) * 21
    return jax.shard_map(on_device, mesh=split, in_specs=in_specs, out_specs=out_specs, check_vma=False)
```

```python
import functools
import math

import jax
import jax.numpy as jnp
from jax import lax
from jax.experimental import pallas as pl
from jax.experimental.pallas import tpu as pltpu
from jax.sharding import Mesh, PartitionSpec as P

STEP = 10
BETA_ONE = 0.9
BETA_TWO = 0.95
ADAM_EPS = 1e-08
DECAY_RATE = 0.1
NORM_EPS = 1e-05
SMALL_RATE = 0.3
REACH = 8
f32 = jnp.float32
bf16 = jnp.bfloat16

NN = (((1,), (0,)), ((), ()))
NT = (((1,), (1,)), ((), ()))
TN = (((0,), (0,)), ((), ()))


def round_up(value, step):
    return -(-value // step) * step


def mm(a, b, dims=NN):
    return lax.dot_general(a, b, dims, preferred_element_type=f32)


class Sizes:
    def __init__(self, members, channels, hidden, noise, lon):
        self.m = members
        self.c = channels
        self.h = hidden
        self.k = noise
        self.lon = lon
        self.q = lon // members
        self.pr = round_up(self.q, 8)
        self.ext = round_up(self.pr + 2 * REACH, 8)
        self.pe = 2 * self.pr
        self.p = members * self.pe
        self.cp = round_up(channels + noise, 128)
        self.ct = self.cp // 128
        self.cr = round_up(channels, 16)
        self.hp = round_up(hidden, 128)
        self.mc = channels // 128 * 128
        self.mh = hidden // 256 * 256

    def piece_rows(self, members, stacks):
        each = self.mc // members
        return next(n for n in range(8, each + 1, 8) if each % n == 0 and n * stacks >= each)


class Rows:
    def __init__(self, sz):
        self.mixing = 9
        self.outbias = self.mixing + sz.k
        self.biasin = self.outbias + 1
        self.row_e = self.biasin + 2
        self.row_r = self.row_e + 2
        self.spare = sz.h - sz.mh
        self.col_e = self.row_r + 2
        self.col_r = self.col_e + self.spare
        self.extra = self.col_r + self.spare
        self.count = round_up(self.extra + 1, 32)
        self.x_mixing = 9
        self.x_outbias = self.x_mixing + sz.k
        self.x_biasin = self.x_outbias + 1
        self.x_row_e = self.x_biasin + self.spare
        self.x_row_r = self.x_row_e + self.spare
        self.x_loss = self.x_row_r + self.spare


def smem():
    return pl.BlockSpec(memory_space=pltpu.SMEM)


def vmem():
    return pl.BlockSpec(memory_space=pltpu.VMEM)


def tile_sum(values):
    tiles = [values[i : i + 8] for i in range(0, values.shape[0], 8)]
    while len(tiles) > 1:
        tiles = [a + b for a, b in zip(tiles[::2], tiles[1::2])] + tiles[len(tiles) // 2 * 2 :]
    return tiles[0]


def column_blocks(width, step):
    return [(i, min(step, width - i)) for i in range(0, width, step)]


def norm_rows(values, channels, lanes):
    inside = lanes < channels
    values = jnp.where(inside, values, 0.0)
    mean = jnp.sum(values, axis=1, keepdims=True) * (1.0 / channels)
    centred = jnp.where(inside, values - mean, 0.0)
    spread = jnp.sum(centred * centred, axis=1, keepdims=True) * (1.0 / channels)
    return centred, lax.rsqrt(spread + NORM_EPS)


def gelu_parts(v):
    size = jnp.abs(v)
    t = 1.0 / (1.0 + (0.3275911 * math.sqrt(0.5)) * size)
    bell = jnp.exp(-0.5 * v * v)
    poly = t * (
        0.5 * 0.254829592
        + t * (-0.5 * 0.284496736 + t * (0.5 * 1.421413741 + t * (-0.5 * 1.453152027 + t * (0.5 * 1.061405429))))
    )
    tail = poly * bell
    cdf = jnp.where(v >= 0.0, 1.0 - tail, tail)
    return v * cdf, cdf + v * bell * (1.0 / math.sqrt(2.0 * math.pi))


def cost(microseconds):
    return pl.CostEstimate(flops=int(microseconds * 5e7), bytes_accessed=0, transcendentals=0)


def transpose_into(sz, src, dst):
    def move(at, count):
        for ct in range(sz.ct):
            block = src[pl.ds(at, count), ct * 128 : (ct + 1) * 128].T
            size = min(128, sz.cr - ct * 128)
            if size > 0:
                dst[ct * 128 : ct * 128 + size, pl.ds(at, count)] = block[:size]

    def body(i, c):
        move(pl.multiple_of(i * 128, 128), 128)
        return c

    lax.fori_loop(0, sz.p // 128, body, 0)
    if sz.p % 128:
        move(sz.p // 128 * 128, sz.p % 128)


def weight_grad(sz, core, left_ref, right_ref, left_t_ref, mine_ref, other_ref, row_ref, col_ref):
    transpose_into(sz, left_ref, left_t_ref)
    half = sz.mh // 2
    for half_ref, which in ((other_ref, 1 - core), (mine_ref, core)):
        for at, width in column_blocks(half, 256):
            cols = pl.ds(pl.multiple_of(which * half + at, 128), width)
            block = mm(left_t_ref[...], right_ref[:, cols])
            row_ref[:, cols] = block[sz.mc :]
            half_ref[:, at : at + width] = block[: sz.mc].astype(bf16)
    rest = right_ref[:, sz.mh :]
    row_ref[:, sz.mh :] = mm(left_t_ref[sz.mc :, :], rest)
    col_ref[...] = mm(rest.astype(f32).T[0:16].astype(bf16), left_ref[...])


def split_kernel(sz, shifts, heights_ref, band_ref, me_ref, x_hbm, noise_hbm, *refs):
    places, (y_ref, s_ref, x_ref, noise_ref, out_ref, in_sems, out_sems) = refs[: sz.m], refs[sz.m :]
    loads = []
    for ct in range(sz.ct):
        channels = pl.ds(ct * 128, min(128, sz.c - ct * 128))
        loads.append(pltpu.make_async_copy(x_hbm.at[:, channels], x_ref.at[:, channels], in_sems.at[ct]))
    loads.append(pltpu.make_async_copy(noise_hbm, noise_ref, in_sems.at[sz.ct]))
    for load in loads:
        load.start()
    for ct in range(sz.ct):
        first = ct * 128
        loads[ct].wait()
        if ct < sz.ct - 1:
            spans = [(x_ref, first, 128, 0)]
        else:
            rest = sz.c - first
            loads[sz.ct].wait()
            s_ref[...] = jnp.zeros_like(s_ref)
            spans = [(x_ref, first, rest, 0), (noise_ref, 0, sz.k, rest)]
        for ref, at, count, to in spans:
            for lt, width in column_blocks(sz.lon, 128):
                block = ref[0, at : at + count, :, lt : lt + width].astype(f32)
                s_ref[lt // 128, 2 * to : 2 * (to + count), :width] = block.reshape(2 * count, width)
        for r in range(2):
            for lt, width in column_blocks(sz.lon, 128):
                block = s_ref[lt // 128, pl.ds(r, 128, stride=2), :].T
                y_ref[r, ct, REACH + lt : REACH + lt + width, :] = block[:width]
    for r in range(2):
        for ct in range(sz.ct):
            y_ref[r, ct, :REACH, :] = y_ref[r, ct, sz.lon : sz.lon + REACH, :]
            y_ref[r, ct, REACH + sz.lon :, :] = y_ref[r, ct, REACH : sz.ext - sz.q, :]
    stores = []
    for s in (*range(1, sz.m), 0):
        start = (me_ref[0] ^ shifts[s]) * sz.q
        for r, row in enumerate((0, heights_ref[band_ref[0]] - 1)):
            for ct in range(sz.ct):
                out_ref[s, r, :, ct * 128 : (ct + 1) * 128] = y_ref[row, ct, pl.ds(start, sz.ext), :].astype(bf16)
        stores.append(pltpu.make_async_copy(out_ref.at[s], places[s], out_sems.at[s]))
        stores[-1].start()
    for store in stores:
        store.wait()


def split_call(sz, shifts, heights, band, me, x, noise):
    outs = tuple(jax.ShapeDtypeStruct((2, sz.ext, sz.cp), bf16) for _ in range(sz.m))
    anywhere = pl.BlockSpec(memory_space=pltpu.HBM)
    return pl.pallas_call(
        functools.partial(split_kernel, sz, shifts),
        out_shape=outs,
        in_specs=[smem(), smem(), smem(), anywhere, anywhere],
        out_specs=tuple(anywhere for _ in outs),
        scratch_shapes=[
            pltpu.VMEM((2, sz.ct, sz.lon + sz.ext - sz.q, 128), f32),
            pltpu.VMEM((round_up(sz.lon, 128) // 128, 256, 128), f32),
            pltpu.VMEM(x.shape, bf16),
            pltpu.VMEM(noise.shape, bf16),
            pltpu.VMEM((sz.m, 2, sz.ext, sz.cp), bf16),
            pltpu.SemaphoreType.DMA((sz.ct + 1,)),
            pltpu.SemaphoreType.DMA((sz.m,)),
        ],
        compiler_params=pltpu.CompilerParams(vmem_limit_bytes=50 * 1024 * 1024),
        cost_estimate=cost(5),
        name="split",
    )(heights, band, me, x, noise)


def join_kernel(sz, shifts, me_ref, *refs):
    pieces, out_ref, y_ref, t_ref, s_ref = refs[: sz.m], *refs[sz.m :]
    inner = slice(REACH, REACH + sz.q)
    starts = [(me_ref[0] ^ shift) * sz.q for shift in shifts]
    for s in range(sz.m):
        for r in range(2):
            for ct in range(sz.ct):
                part = pieces[s][r, :, ct * 128 : (ct + 1) * 128].astype(f32)
                y_ref[r, ct, pl.ds(starts[s] + REACH, sz.q), :] = part[inner]
                s_ref[s, r, ct, :REACH] = part[:REACH]
                s_ref[s, r, ct, REACH:] = part[REACH + sz.q : 2 * REACH + sz.q]
    for s in range(sz.m):
        left = jnp.where(starts[s] == 0, sz.lon, starts[s])
        right = jnp.where(starts[s] == sz.lon - sz.q, REACH, starts[s] + REACH + sz.q)
        for r in range(2):
            for ct in range(sz.ct):
                y_ref[r, ct, pl.ds(left, REACH), :] += s_ref[s, r, ct, :REACH]
                y_ref[r, ct, pl.ds(right, REACH), :] += s_ref[s, r, ct, REACH:]
    for ct in range(sz.ct):
        for r in range(2):
            for lt in range(0, sz.lon, 128):
                block = y_ref[r, ct, REACH + lt : REACH + lt + 128, :].T
                t_ref[lt // 128, pl.ds(r, 128, stride=2), :] = block
        size = min(128, sz.c - ct * 128)
        for lt, width in column_blocks(sz.lon, 128):
            block = t_ref[lt // 128, : 2 * size, :width].reshape(size, 2, width)
            out_ref[0, ct * 128 : ct * 128 + size, :, lt : lt + width] = block.astype(bf16)


def join_call(sz, shifts, me, pieces):
    return pl.pallas_call(
        functools.partial(join_kernel, sz, shifts),
        out_shape=jax.ShapeDtypeStruct((1, sz.c, 2, sz.lon), bf16),
        in_specs=[smem()] + [vmem()] * sz.m,
        out_specs=vmem(),
        scratch_shapes=[
            pltpu.VMEM((2, sz.ct, REACH + max(round_up(sz.lon, 128), sz.lon + sz.ext - sz.q - REACH), 128), f32),
            pltpu.VMEM((round_up(sz.lon, 128) // 128, 256, 128), f32),
            pltpu.VMEM((sz.m, 2, sz.ct, 2 * REACH, 128), f32),
        ],
        compiler_params=pltpu.CompilerParams(vmem_limit_bytes=24 * 1024 * 1024),
        cost_estimate=cost(6),
        name="join",
    )(me, *pieces)


def norm_and_filter(sz, e, height_ref, taps_ref, x_ref, prev_ref, next_ref, gain_ref, filter_ref, normed_ref, n_ref, fil_ref):
    lanes = lax.broadcasted_iota(jnp.int32, (1, sz.cp), 1)
    below_first = jnp.where(height_ref[0] == 2, 2, 3)
    sources = ((0, 1, below_first), (1, 2, 3))

    def norm_store(values, row):
        centred, inv = norm_rows(values.astype(f32), sz.c, lanes)
        normed = (centred * inv * gain_ref[...]).astype(bf16)
        normed_ref[e, row] = normed
        normed = normed.astype(f32)
        for ct in range(sz.ct):
            n_ref[row, ct] = normed[:, ct * 128 : (ct + 1) * 128]

    norm_store(prev_ref[e], 0)
    norm_store(x_ref[e, 0], 1)
    norm_store(x_ref[e, 1], 2)
    norm_store(next_ref[e], 3)

    def filter_tile(ct, c):
        for r in range(2):
            acc = jnp.zeros((sz.pr, 128), f32)
            for a in range(3):
                for j in range(3):
                    tap = 3 * a + j
                    start = taps_ref[tap, r] + REACH
                    moved = n_ref[sources[r][a], ct, pl.ds(start, sz.pr), :]
                    acc = acc + filter_ref[ct, tap : tap + 1, :] * moved
            fil_ref[ct, r * sz.pr : (r + 1) * sz.pr, :] = acc
        return c

    lax.fori_loop(0, sz.ct, filter_tile, 0)


def feed_forward(sz, e, x_ref, fil_ref, expand_ref, bias_ref, reduce_ref, outbias_ref, noisemix_ref, store):
    own = jnp.concatenate([x_ref[e, r].astype(f32)[REACH : REACH + sz.pr] for r in range(2)], axis=0)
    noise = own[:, (sz.ct - 1) * 128 :].astype(bf16)
    mixed = mm(jnp.concatenate([noise, noise], axis=1), noisemix_ref[...])
    filtered = jnp.concatenate([fil_ref[ct] for ct in range(sz.ct)], axis=1)
    lanes = lax.broadcasted_iota(jnp.int32, (1, sz.cp), 1)
    mixed = jnp.where(lanes == sz.c, 1.0, filtered + mixed).astype(bf16)
    store("mixed", slice(0, sz.cp), mixed)
    acts = []
    for at, width in column_blocks(sz.hp, 256):
        pre = mm(mixed, expand_ref[:, at : at + width]) + bias_ref[:, at : at + width]
        act, slope = gelu_parts(pre)
        if at <= sz.h < at + width:
            units = at + lax.broadcasted_iota(jnp.int32, (1, width), 1)
            act = jnp.where(units == sz.h, 1.0, act)
        acts.append(act.astype(bf16))
        store("act", slice(at, at + width), acts[-1])
        store("slope", slice(at, at + width), slope.astype(bf16))
    act = jnp.concatenate(acts, axis=1)
    return own + (mm(act, reduce_ref[...], NT) + outbias_ref[...])


def own_kernel(
    sz,
    height_ref,
    taps_ref,
    x_ref,
    prev_ref,
    next_ref,
    expand_ref,
    bias_ref,
    reduce_ref,
    gain_ref,
    outbias_ref,
    filter_ref,
    noisemix_ref,
    normed_ref,
    mx_ref,
    act_ref,
    dg_ref,
    pred_ref,
    n_ref,
    fil_ref,
):
    norm_and_filter(sz, 0, height_ref, taps_ref, x_ref, prev_ref, next_ref, gain_ref, filter_ref, normed_ref, n_ref, fil_ref)
    places = {"mixed": mx_ref, "act": act_ref, "slope": dg_ref}

    def store(name, cols, values):
        places[name][:, cols] = values

    pred_ref[...] = feed_forward(
        sz, 0, x_ref, fil_ref, expand_ref, bias_ref, reduce_ref, outbias_ref, noisemix_ref, store
    )


def filter_scratch(sz):
    return [pltpu.VMEM((4, sz.ct, sz.ext, 128), f32), pltpu.VMEM((sz.ct, sz.pe, 128), f32)]


def own_call(sz, height, taps, x, prev, after, weights):
    shape = jax.ShapeDtypeStruct
    outs = (
        shape((sz.m, 4, sz.ext, sz.cp), bf16),
        shape((sz.pe, sz.cp), bf16),
        shape((sz.pe, sz.hp), bf16),
        shape((sz.pe, sz.hp), bf16),
        shape((sz.pe, sz.cp), f32),
    )
    return pl.pallas_call(
        functools.partial(own_kernel, sz),
        grid=(1,),
        out_shape=outs,
        in_specs=[smem(), smem()] + [vmem()] * 10,
        out_specs=(pl.BlockSpec((1, 4, sz.ext, sz.cp), lambda i: (0, 0, 0, 0)),) + (vmem(),) * 4,
        scratch_shapes=filter_scratch(sz),
        compiler_params=pltpu.CompilerParams(vmem_limit_bytes=50 * 1024 * 1024),
        cost_estimate=cost(8),
        name="own",
    )(height, taps, x, prev, after, *weights)


def main_kernel(
    sz,
    height_ref,
    core_ref,
    taps_ref,
    bias_ref,
    gain_ref,
    outbias_ref,
    filter_ref,
    noisemix_ref,
    x_hbm,
    prev_hbm,
    next_hbm,
    target_hbm,
    expand_hbm,
    reduce_hbm,
    normed_own_hbm,
    mx_hbm,
    act_hbm,
    dg_hbm,
    pred_hbm,
    mine_hbm,
    other_hbm,
    bg_hbm,
    pg_hbm,
    normed_hbm,
    small_ref,
    x_ref,
    prev_ref,
    next_ref,
    target_ref,
    expand_ref,
    reduce_ref,
    mine_ref,
    other_ref,
    bg_ref,
    pg_ref,
    n_ref,
    fil_ref,
    nb_ref,
    mx_ref,
    act_ref,
    dg_ref,
    pred_ref,
    tr_ref,
    row_e_ref,
    row_r_ref,
    col_e_ref,
    col_r_ref,
    loss_ref,
    in_sems,
    out_sems,
):
    first = pl.ds(0, sz.pe)
    others = pl.ds(1, sz.m - 1)
    early = [
        pltpu.make_async_copy(x_hbm.at[others], x_ref, in_sems.at[0]),
        pltpu.make_async_copy(prev_hbm, prev_ref, in_sems.at[1]),
        pltpu.make_async_copy(next_hbm, next_ref, in_sems.at[2]),
    ]
    expand_load = pltpu.make_async_copy(expand_hbm, expand_ref, in_sems.at[3])
    reduce_load = pltpu.make_async_copy(reduce_hbm, reduce_ref, in_sems.at[4])
    loads = [
        pltpu.make_async_copy(mx_hbm, mx_ref.at[first], in_sems.at[5]),
        pltpu.make_async_copy(act_hbm, act_ref.at[first], in_sems.at[6]),
        pltpu.make_async_copy(dg_hbm, dg_ref.at[first], in_sems.at[7]),
        pltpu.make_async_copy(pred_hbm, pred_ref.at[0], in_sems.at[8]),
        pltpu.make_async_copy(target_hbm, target_ref, in_sems.at[9]),
    ]
    for load in (*early, expand_load, reduce_load, *loads):
        load.start()
    for load in early:
        load.wait()

    def forward(e, carry):
        norm_and_filter(
            sz, e, height_ref, taps_ref, x_ref, prev_ref, next_ref, gain_ref, filter_ref, nb_ref, n_ref, fil_ref
        )

        @pl.when(e == 0)
        def _():
            expand_load.wait()
            reduce_load.wait()

        rows = pl.ds(pl.multiple_of((e + 1) * sz.pe, 16), sz.pe)
        places = {"mixed": mx_ref, "act": act_ref, "slope": dg_ref}

        def store(name, cols, values):
            places[name][rows, cols] = values

        pred_ref[e + 1] = feed_forward(
            sz, e, x_ref, fil_ref, expand_ref, bias_ref, reduce_ref, outbias_ref, noisemix_ref, store
        )
        return carry

    lax.fori_loop(0, sz.m - 1, forward, 0)
    save = pltpu.make_async_copy(nb_ref, normed_hbm.at[pl.ds(1, sz.m - 1)], out_sems.at[0])
    save.start()
    for load in loads:
        load.wait()

    height = height_ref[0]
    lanes = lax.broadcasted_iota(jnp.int32, (1, sz.cp), 1)
    inside = (lanes < sz.c).astype(f32)
    loss_ref[...] = jnp.zeros_like(loss_ref)
    step = 16
    inv_m = 1.0 / sz.m
    inv_mm = inv_m * inv_m

    def score(i, carry):
        at = pl.multiple_of(i * step, step)
        pixel = at + lax.broadcasted_iota(jnp.int32, (step, 1), 0)
        row = (pixel >= sz.pr).astype(jnp.int32)
        use = (pixel - row * sz.pr < sz.q) & (row < height)
        mask_rows = use.astype(f32)
        for ct in range(sz.ct):
            cols = slice(ct * 128, (ct + 1) * 128)
            mask = mask_rows * inside[:, cols]
            preds = [pred_ref[e, pl.ds(at, step), cols] for e in range(sz.m)]
            truth = target_ref[pl.ds(at, step), cols].astype(f32)
            slopes = []
            own_sum = 0.0
            for p in preds:
                d = p - truth
                q = d * d + 1.0
                r = lax.rsqrt(q)
                own_sum = own_sum + q * r
                slopes.append(d * r * inv_m)
            pair_sum = 0.0
            pairs = [0.0] * sz.m
            for a in range(sz.m):
                for b in range(a + 1, sz.m):
                    d = preds[a] - preds[b]
                    q = d * d + 1.0
                    r = lax.rsqrt(q)
                    pair_sum = pair_sum + q * r
                    s = d * r
                    pairs[a] = pairs[a] + s
                    pairs[b] = pairs[b] - s
            value = own_sum * inv_m - (pair_sum + 0.5 * sz.m) * inv_mm
            value = mask * value
            loss_ref[:, cols] += value[0:8] + value[8:16]
            for e in range(sz.m):
                g = (mask * (slopes[e] - pairs[e] * inv_mm)).astype(bf16)
                where = pl.ds(pl.multiple_of(e * sz.pe + at, 16), step)
                bg_ref[where, cols] = g
        return carry

    lax.fori_loop(0, sz.pe // step, score, 0)
    core = core_ref[0]
    saves = [save]

    def write(here, there, which):
        saves.append(pltpu.make_async_copy(here, there, out_sems.at[which]))
        saves[-1].start()

    write(bg_ref, bg_hbm, 1)
    weight_grad(sz, core, bg_ref, act_ref, tr_ref, mine_ref.at[1], other_ref.at[1], row_r_ref, col_r_ref)
    write(mine_ref.at[1], mine_hbm.at[1], 2)
    write(other_ref.at[1], other_hbm.at[1], 3)


    def backward(e, carry):
        rows = pl.ds(pl.multiple_of(e * sz.pe, 16), sz.pe)
        bg = bg_ref[rows, :]
        for at, width in column_blocks(sz.hp, 256):
            grad = mm(bg, reduce_ref[:, at : at + width])
            pre = (grad * dg_ref[rows, at : at + width].astype(f32)).astype(bf16)
            pg_ref[rows, at : at + width] = pre
        return carry

    lax.fori_loop(0, sz.m, backward, 0)
    write(pg_ref, pg_hbm, 4)
    weight_grad(sz, core, mx_ref, pg_ref, tr_ref, mine_ref.at[0], other_ref.at[0], row_e_ref, col_e_ref)
    write(other_ref.at[0], other_hbm.at[0], 5)
    write(mine_ref.at[0], mine_hbm.at[0], 6)
    at = Rows(sz)
    small_ref[...] = jnp.zeros_like(small_ref)
    lane = lax.broadcasted_iota(jnp.int32, (1, sz.mc), 1)
    half = sz.mh // 2

    def column_sum(ref):
        return jnp.sum(ref[...], axis=0, keepdims=True)

    def long_row(row, place, values, extra):
        small_ref[row : row + 1, :] = values[:, :half]
        small_ref[row + 1 : row + 2, :] = values[:, half : sz.mh]
        for i in range(at.spare):
            extra = jnp.where(lane == place + i, values[:, sz.mh + i : sz.mh + i + 1], extra)
        return extra

    extra = jnp.zeros((1, sz.mc), f32)
    outbias_grad = col_r_ref[at.spare : at.spare + 1, :]
    small_ref[at.outbias : at.outbias + 1, :] = outbias_grad[:, : sz.mc]
    extra = jnp.where(lane == at.x_outbias, outbias_grad[:, sz.mc : sz.mc + 1], extra)
    extra = long_row(at.biasin, at.x_biasin, row_e_ref[sz.c - sz.mc : sz.c - sz.mc + 1, :], extra)
    extra = long_row(at.row_e, at.x_row_e, row_e_ref[0:1, :], extra)
    extra = long_row(at.row_r, at.x_row_r, row_r_ref[0:1, :], extra)
    small_ref[at.col_e : at.col_e + at.spare, :] = col_e_ref[: at.spare, : sz.mc]
    small_ref[at.col_r : at.col_r + at.spare, :] = col_r_ref[: at.spare, : sz.mc]
    extra = jnp.where(lane == at.x_loss, jnp.sum(column_sum(loss_ref), axis=1, keepdims=True), extra)
    small_ref[at.extra : at.extra + 1, :] = extra
    for save in saves:
        save.wait()


def main_call(sz, height, core, taps, x, prev, after, target, weights, state):
    shape = jax.ShapeDtypeStruct
    half = shape((2, sz.mc, sz.mh // 2), bf16)
    outs = (
        half,
        half,
        shape((sz.p, sz.cp), bf16),
        shape((sz.p, sz.hp), bf16),
        shape((sz.m, 4, sz.ext, sz.cp), bf16),
        shape((Rows(sz).count, sz.mc), f32),
    )
    anywhere = pl.BlockSpec(memory_space=pl.ANY)
    expand, bias, reduce, gain, outbias, filt, noisemix = weights
    return pl.pallas_call(
        functools.partial(main_kernel, sz),
        out_shape=outs,
        in_specs=[smem()] * 3 + [vmem()] * 5 + [anywhere] * 11,
        out_specs=(anywhere,) * 5 + (vmem(),),
        input_output_aliases={14: 4},
        scratch_shapes=[
            pltpu.VMEM((sz.m - 1, 2, sz.ext, sz.cp), bf16),
            pltpu.VMEM((sz.m - 1, sz.ext, sz.cp), bf16),
            pltpu.VMEM((sz.m - 1, sz.ext, sz.cp), bf16),
            pltpu.VMEM((sz.pe, sz.cp), bf16),
            pltpu.VMEM((sz.cp, sz.hp), bf16),
            pltpu.VMEM((sz.cp, sz.hp), bf16),
            pltpu.VMEM((2, sz.mc, sz.mh // 2), bf16),
            pltpu.VMEM((2, sz.mc, sz.mh // 2), bf16),
            pltpu.VMEM((sz.p, sz.cp), bf16),
            pltpu.VMEM((sz.p, sz.hp), bf16),
            *filter_scratch(sz),
            pltpu.VMEM((sz.m - 1, 4, sz.ext, sz.cp), bf16),
            pltpu.VMEM((sz.p, sz.cp), bf16),
            pltpu.VMEM((sz.p, sz.hp), bf16),
            pltpu.VMEM((sz.p, sz.hp), bf16),
            pltpu.VMEM((sz.m, sz.pe, sz.cp), f32),
            pltpu.VMEM((sz.cr, sz.p), bf16),
            pltpu.VMEM((sz.cr - sz.mc, sz.hp), f32),
            pltpu.VMEM((sz.cr - sz.mc, sz.hp), f32),
            pltpu.VMEM((16, sz.cp), f32),
            pltpu.VMEM((16, sz.cp), f32),
            pltpu.VMEM((8, sz.cp), f32),
            pltpu.SemaphoreType.DMA((10,)),
            pltpu.SemaphoreType.DMA((7,)),
        ],
        compiler_params=pltpu.CompilerParams(vmem_limit_bytes=50 * 1024 * 1024),
        cost_estimate=cost(40),
        name="main",
    )(height, core, taps, bias, gain, outbias, filt, noisemix, x, prev, after, target, expand, reduce, *state)


def share_kernel(size, me_ref, mine_ref, got_ref, *outs):
    for s, out_ref in enumerate(outs):
        rows = pl.ds(pl.multiple_of((me_ref[0] ^ s) * size, 16), size)
        for kind in range(2):
            total = mine_ref[kind, rows, :].astype(f32) + got_ref[kind, rows, :].astype(f32)
            out_ref[kind] = total.astype(bf16)


def share_call(me, mine, got, count):
    kinds, rows, width = mine.shape
    size = rows // count
    outs = tuple(jax.ShapeDtypeStruct((kinds, size, width), bf16) for _ in range(count))
    return pl.pallas_call(
        functools.partial(share_kernel, size),
        out_shape=outs,
        in_specs=[smem(), vmem(), vmem()],
        out_specs=tuple(vmem() for _ in outs),
        compiler_params=pltpu.CompilerParams(vmem_limit_bytes=16 * 1024 * 1024),
        cost_estimate=cost(2),
        name="share",
    )(me, mine, got)


def unmix_kernel(
    sz,
    base,
    count,
    height_ref,
    taps_ref,
    filter_ref,
    small_in_ref,
    pg_hbm,
    x_hbm,
    normed_hbm,
    expand_hbm,
    gn_own_hbm,
    gn_prev_hbm,
    gn_next_hbm,
    small_ref,
    pg_ref,
    x_ref,
    normed_ref,
    expand_ref,
    own_ref,
    edge_ref,
    filter_grad_ref,
    mixing_grad_ref,
    n_ref,
    gn_ref,
    gm_ref,
    in_sems,
    out_sems,
):
    below_first = jnp.where(height_ref[0] == 2, 2, 3)
    sources = ((0, 1, below_first), (1, 2, 3))
    last = sz.ct - 1
    weights = pltpu.make_async_copy(expand_hbm, expand_ref, in_sems.at[0])
    weights.start()
    loads = []
    for e in range(count):
        rows = pl.ds((base + e) * sz.pe, sz.pe)
        channels = pl.ds(last * 128, 128)
        loads.append(
            (
                pltpu.make_async_copy(pg_hbm.at[rows], pg_ref.at[e], in_sems.at[3 * e + 1]),
                pltpu.make_async_copy(x_hbm.at[base + e, :, :, channels], x_ref.at[e], in_sems.at[3 * e + 2]),
                pltpu.make_async_copy(normed_hbm.at[base + e], normed_ref.at[e], in_sems.at[3 * e + 3]),
            )
        )
    for load in loads[0]:
        load.start()
    filter_grad_ref[...] = jnp.zeros_like(filter_grad_ref)
    mixing_grad_ref[...] = jnp.zeros_like(mixing_grad_ref)
    pad = 2 * REACH
    for r in range(2):
        for ct in range(sz.ct):
            gm_ref[r, ct, :pad, :] = jnp.zeros((pad, 128), f32)
            gm_ref[r, ct, pad + sz.pr :, :] = jnp.zeros((sz.ext + REACH - sz.pr, 128), f32)
    weights.wait()
    stores = []
    for e in range(count):
        loads[e][0].wait()
        if e + 1 < count:
            for load in loads[e + 1]:
                load.start()
        gm = mm(pg_ref[e], expand_ref[...], NT)
        for r in range(2):
            for ct in range(sz.ct):
                gm_ref[r, ct, pad : pad + sz.pr, :] = gm[r * sz.pr : (r + 1) * sz.pr, ct * 128 : (ct + 1) * 128]
        for load in loads[e][1:]:
            load.wait()
        for row in range(4):
            normed = normed_ref[e, row].astype(f32)
            for ct in range(sz.ct):
                n_ref[row, ct] = normed[:, ct * 128 : (ct + 1) * 128]
        noise = jnp.concatenate([x_ref[e, r].astype(f32)[REACH : REACH + sz.pr] for r in range(2)], axis=0)
        mixing_grad_ref[...] += mm(noise.T[0:16].astype(bf16), gm.astype(bf16))

        def unfilter_tile(ct, c):
            def gathered(*readers):
                acc = jnp.zeros((sz.ext, 128), f32)
                for r, a in readers:
                    for tap in range(3 * a, 3 * a + 3):
                        start = REACH - taps_ref[tap, r]
                        acc = acc + filter_ref[ct, tap : tap + 1, :] * gm_ref[r, ct, pl.ds(start, sz.ext), :]
                return acc

            gn_ref[0, ct] = gathered((0, 0))
            gn_ref[1, ct] = gathered((0, 1), (1, 0))
            gn_ref[2, ct] = gathered((1, 1))
            gn_ref[3, ct] = gathered((1, 2))
            gn_ref[below_first, ct] += gathered((0, 2))
            for r in range(2):
                g = gm_ref[r, ct, pad : pad + sz.pr, :]
                for a in range(3):
                    for tap in range(3 * a, 3 * a + 3):
                        read = n_ref[sources[r][a], ct, pl.ds(taps_ref[tap, r] + REACH, sz.pr), :]
                        filter_grad_ref[ct, tap] += tile_sum(g * read)
            return c

        lax.fori_loop(0, sz.ct, unfilter_tile, 0)
        for ct in range(sz.ct):
            cols = slice(ct * 128, (ct + 1) * 128)
            edge_ref[e, 0, :, cols] = gn_ref[0, ct].astype(bf16)
            edge_ref[e, 1, :, cols] = gn_ref[3, ct].astype(bf16)
            own_ref[e, 0, :, cols] = gn_ref[1, ct].astype(bf16)
            own_ref[e, 1, :, cols] = gn_ref[2, ct].astype(bf16)
        stores += [
            pltpu.make_async_copy(own_ref.at[e], gn_own_hbm.at[e], out_sems.at[3 * e]),
            pltpu.make_async_copy(edge_ref.at[e, 0], gn_prev_hbm.at[e], out_sems.at[3 * e + 1]),
            pltpu.make_async_copy(edge_ref.at[e, 1], gn_next_hbm.at[e], out_sems.at[3 * e + 2]),
        ]
        for store in stores[-3:]:
            store.start()

    at = Rows(sz)
    lane = lax.broadcasted_iota(jnp.int32, (1, sz.mc), 1)
    small_ref[...] = small_in_ref[...]
    extra = small_in_ref[at.extra : at.extra + 1, :]
    first = sz.c - last * 128
    for tap in range(9):
        for ct in range(last):
            row = jnp.sum(filter_grad_ref[ct, tap], axis=0, keepdims=True)
            small_ref[tap : tap + 1, ct * 128 : (ct + 1) * 128] += row
        row = jnp.sum(filter_grad_ref[last, tap], axis=0, keepdims=True)
        extra = extra + jnp.where(lane == tap, row[:, 0:1], 0.0)
    mixing = mixing_grad_ref[first : first + sz.k, :]
    small_ref[at.mixing : at.mixing + sz.k, :] += mixing[:, : sz.mc]
    for i in range(sz.k):
        extra = extra + jnp.where(lane == at.x_mixing + i, mixing[i : i + 1, sz.mc : sz.mc + 1], 0.0)
    small_ref[at.extra : at.extra + 1, :] = extra
    for store in stores:
        store.wait()


def unmix_call(sz, base, count, height, taps, pg, x, normed, expand, filt, small):
    shape = jax.ShapeDtypeStruct
    outs = (
        shape((count, 2, sz.ext, sz.cp), bf16),
        shape((count, sz.ext, sz.cp), bf16),
        shape((count, sz.ext, sz.cp), bf16),
        shape(small.shape, f32),
    )
    anywhere = pl.BlockSpec(memory_space=pltpu.HBM)
    return pl.pallas_call(
        functools.partial(unmix_kernel, sz, base, count),
        out_shape=outs,
        in_specs=[smem(), smem(), vmem(), vmem()] + [anywhere] * 4,
        out_specs=(anywhere,) * 3 + (vmem(),),
        scratch_shapes=[
            pltpu.VMEM((count, sz.pe, sz.hp), bf16),
            pltpu.VMEM((count, 2, sz.ext, 128), bf16),
            pltpu.VMEM((count, 4, sz.ext, sz.cp), bf16),
            pltpu.VMEM((sz.cp, sz.hp), bf16),
            pltpu.VMEM((count, 2, sz.ext, sz.cp), bf16),
            pltpu.VMEM((count, 2, sz.ext, sz.cp), bf16),
            pltpu.VMEM((sz.ct, 9, 8, 128), f32),
            pltpu.VMEM((16, sz.cp), f32),
            pltpu.VMEM((4, sz.ct, sz.ext, 128), f32),
            pltpu.VMEM((4, sz.ct, sz.ext, 128), f32),
            pltpu.VMEM((2, sz.ct, sz.ext + 3 * REACH, 128), f32),
            pltpu.SemaphoreType.DMA((3 * count + 1,)),
            pltpu.SemaphoreType.DMA((3 * count,)),
        ],
        compiler_params=pltpu.CompilerParams(vmem_limit_bytes=28 * 1024 * 1024),
        cost_estimate=cost(5 * count),
        name="unmix",
    )(height, taps, filt, small, *(pltpu.with_memory_space_constraint(v, pltpu.HBM) for v in (pg, x, normed, expand)))


def norm_back_kernel(sz, height_ref, x_ref, gn_ref, up_ref, down_ref, bg_ref, gain_ref, out_ref):
    height = height_ref[0]
    lanes = lax.broadcasted_iota(jnp.int32, (1, sz.cp), 1)
    from_up = up_ref[0].astype(f32)
    from_down = down_ref[0].astype(f32)
    direct = bg_ref[...].astype(f32)
    for r in range(2):
        centred, inv = norm_rows(x_ref[0, r].astype(f32), sz.c, lanes)
        xhat = centred * inv
        g = gn_ref[0, r].astype(f32) + jnp.where(height == r + 1, from_down, 0.0)
        if r == 0:
            g = g + from_up
        q = g * gain_ref[...]
        mean_q = jnp.sum(q, axis=1, keepdims=True) * (1.0 / sz.c)
        mean_qx = jnp.sum(q * xhat, axis=1, keepdims=True) * (1.0 / sz.c)
        result = (q - mean_q - xhat * mean_qx) * inv
        part = result[REACH : REACH + sz.pr] + direct[r * sz.pr : (r + 1) * sz.pr]
        pieces = [result[:REACH], part, result[REACH + sz.pr :]]
        out_ref[0, r] = jnp.concatenate(pieces, axis=0).astype(bf16)


def norm_back_call(sz, base, count, height, x, gn, up, down, bg, gain):
    return pl.pallas_call(
        functools.partial(norm_back_kernel, sz),
        grid=(count,),
        out_shape=jax.ShapeDtypeStruct((count, 2, sz.ext, sz.cp), bf16),
        in_specs=[
            smem(),
            pl.BlockSpec((1, 2, sz.ext, sz.cp), lambda i: (i + base, 0, 0, 0)),
            pl.BlockSpec((1, 2, sz.ext, sz.cp), lambda i: (i, 0, 0, 0)),
            pl.BlockSpec((1, sz.ext, sz.cp), lambda i: (i, 0, 0)),
            pl.BlockSpec((1, sz.ext, sz.cp), lambda i: (i, 0, 0)),
            pl.BlockSpec((sz.pe, sz.cp), lambda i: (i + base, 0)),
            pl.BlockSpec((1, sz.cp), lambda i: (0, 0)),
        ],
        out_specs=pl.BlockSpec((1, 2, sz.ext, sz.cp), lambda i: (i, 0, 0, 0)),
        compiler_params=pltpu.CompilerParams(vmem_limit_bytes=14 * 1024 * 1024),
        cost_estimate=cost(2 * count),
        name="norm_back",
    )(height, x, gn, up, down, bg, gain)


def adam_kernel(sz, limit, pixels, members, stacks, place_ref, heights_ref, *refs):
    mine_ref, got_ref, small_mine_ref, small_got_ref = refs[:4]
    ins, small_ins, (norm_ref, mean_ref) = refs[4:10], refs[10:22], refs[22:24]
    outs, small_outs = refs[24:32], refs[32:44]
    factor_ref, small_ref, column_ref, cols_ref, gain_ref = refs[44:]
    at = Rows(sz)
    step = pl.program_id(0)
    core, member, stack = place_ref[0], place_ref[1], place_ref[2]
    half = sz.mh // 2
    each = sz.mc // members
    rows = sz.piece_rows(members, stacks)

    def wide(row, count, place):
        return jnp.concatenate([small_ref[row : row + count, :], column_ref[place : place + count, 0:1]], axis=1)

    def long(row, place):
        extra = small_ref[at.extra : at.extra + 1, place : place + at.spare]
        return jnp.concatenate([small_ref[row : row + 1, :], small_ref[row + 1 : row + 2, :], extra], axis=1)

    @pl.when(step == 0)
    def _():
        part = at.count // 2
        for which, ref in ((core, small_mine_ref), (1 - core, small_got_ref)):
            where = pl.ds(pl.multiple_of(which * part, part), part)
            values = ref[...].astype(f32)
            small_ref[where, :] = values[:part] + values[part:]
        extra = small_ref[at.extra : at.extra + 1, 0:128]
        column_ref[...] = jnp.broadcast_to(extra, (8, 128)).T
        total = jnp.zeros((8, half), f32)
        for ref in (mine_ref, got_ref):

            def body(i, acc):
                values = ref[i].astype(f32)
                values = values * values
                for j in range(0, rows, 8):
                    acc = acc + values[j : j + 8]
                return acc

            total = lax.fori_loop(0, 2 * members * stacks, body, total)
        count = jnp.sum(total)
        filter_grad = wide(0, 9, 0)
        gain_row = jnp.sum(small_ins[0][...] * filter_grad, axis=0, keepdims=True) / small_ins[6][0:1, :]
        gain_ref[...] = gain_row
        cols = small_ref[at.col_e : at.extra, :]
        for values in (
            filter_grad,
            wide(at.mixing, sz.k, at.x_mixing),
            gain_row,
            wide(at.outbias, 1, at.x_outbias),
            long(at.biasin, at.x_biasin),
            long(at.row_e, at.x_row_e),
            long(at.row_r, at.x_row_r),
            cols,
        ):
            count = count + jnp.sum(values * values)
        norm = jnp.sqrt(jnp.full((8, 128), count, f32))
        factor_ref[...] = jnp.minimum(1.0, limit / (norm + 1e-06))
        live = heights_ref[0]
        for i in range(1, heights_ref.shape[0]):
            live = live + heights_ref[i]
        loss = column_ref[at.x_loss : at.x_loss + 1, 0:1]
        mean = loss / (jnp.full((8, 128), pixels, f32) * live.astype(f32))
        norm_ref[0] = norm[0, 0]
        mean_ref[0] = mean[0, 0]
        cols_ref[...] = jnp.concatenate([cols, jnp.zeros((8 - 2 * at.spare, sz.mc), f32)], axis=0).T

    factor = factor_ref[0:1, 0:1]

    def adam(w, g, m, v, rate):
        g = factor * g
        m_new = BETA_ONE * m + (1.0 - BETA_ONE) * g
        v_new = BETA_TWO * v + (1.0 - BETA_TWO) * g * g
        v_hat = v_new * (1.0 / (1.0 - BETA_TWO**STEP))
        root = v_hat * lax.rsqrt(v_hat) + ADAM_EPS
        inverse = pl.reciprocal(root, approx=True)
        inverse = inverse * (2.0 - root * inverse)
        change = m_new * (rate / (1.0 - BETA_ONE**STEP)) * inverse
        return w * (1.0 - rate * DECAY_RATE) - change, m_new, v_new

    kinds = ((0, at.row_e, at.x_row_e, sz.c**-0.5), (1, at.row_r, at.x_row_r, sz.h**-0.5))

    @pl.when(step < sz.mc // ROWS)
    def _():
        first_core = core == 0
        for i in range(ROWS // rows):
            first = step * ROWS + i * rows
            t = member ^ (first // each)
            s = stack ^ ((first % each) // rows)
            where = pl.ds(pl.multiple_of(first, 8), rows)
            to = slice(i * rows, (i + 1) * rows)
            for kind, _, _, rate in kinds:
                slot = (t * stacks + s) * 2 + kind
                mine = mine_ref[slot].astype(f32)
                got = got_ref[slot].astype(f32)
                low = jnp.where(first_core, mine, got)
                high = jnp.where(first_core, got, mine)
                cols = cols_ref[where, kind * at.spare : (kind + 1) * at.spare]
                g = jnp.concatenate([low, high, cols], axis=1)
                w_ref, m_ref, v_ref = ins[3 * kind : 3 * kind + 3]
                w_out, m_out, v_out, c_out = outs[4 * kind : 4 * kind + 4]
                w, m, v = adam(w_ref[where, :], g, m_ref[where, :], v_ref[where, :], rate)
                w_out[to, :] = w
                m_out[to, :] = m
                v_out[to, :] = v
            if (i + 1) * rows % 16 == 0:
                both = slice((i + 1) * rows // 16 * 16 - max(16, rows * 2), (i + 1) * rows)
                for kind in range(2):
                    outs[4 * kind + 3][both, :] = outs[4 * kind][both, :].astype(bf16)

    @pl.when(step == sz.mc // ROWS)
    def _():
        last = slice(sz.mc, sz.c)
        for kind, row, place, rate in kinds:
            w_ref, m_ref, v_ref = ins[3 * kind : 3 * kind + 3]
            w_out, m_out, v_out, c_out = outs[4 * kind : 4 * kind + 4]
            w, m, v = adam(w_ref[last, :], long(row, place), m_ref[last, :], v_ref[last, :], rate)
            w_out[0:1, :] = w
            m_out[0:1, :] = m
            v_out[0:1, :] = v
            c_out[0:16, :] = jnp.broadcast_to(w, (16, sz.h)).astype(bf16)

    @pl.when(step == 0)
    def _():
        grads = (
            wide(0, 9, 0),
            wide(at.mixing, sz.k, at.x_mixing),
            jnp.concatenate([gain_ref[...], wide(at.outbias, 1, at.x_outbias)], axis=0),
            long(at.biasin, at.x_biasin),
        )
        for i, g in enumerate(grads):
            new = adam(small_ins[3 * i][...], g, small_ins[3 * i + 1][...], small_ins[3 * i + 2][...], SMALL_RATE)
            for ref, values in zip(small_outs[3 * i : 3 * i + 3], new):
                ref[...] = values.reshape(ref.shape)


ROWS = 80


def adam_call(sz, limit, pixels, members, stacks, place, heights, grads, weights, small_weights):
    shape = jax.ShapeDtypeStruct
    full = shape((sz.c, sz.h), f32)
    low = shape((sz.c, sz.h), bf16)
    outs = (shape((1,), f32),) * 2 + (full, full, full, low) * 2 + tuple(shape(v.shape if v.shape[0] > 1 else v.shape[1:], f32) for v in small_weights)
    block = pl.BlockSpec((ROWS, sz.h), lambda i: (i, 0))
    steps = sz.mc // ROWS + 1
    return pl.pallas_call(
        functools.partial(adam_kernel, sz, limit, pixels, members, stacks),
        grid=(steps,),
        out_shape=outs,
        in_specs=[smem()] * 2 + [vmem()] * (4 + 6) + [vmem()] * 12,
        out_specs=(smem(),) * 2 + (block,) * 8 + (vmem(),) * 12,
        scratch_shapes=[
            pltpu.VMEM((8, 128), f32),
            pltpu.VMEM((Rows(sz).count, sz.mc), f32),
            pltpu.VMEM((128, 8), f32),
            pltpu.VMEM((sz.mc, 8), f32),
            pltpu.VMEM((1, sz.c), f32),
        ],
        compiler_params=pltpu.CompilerParams(vmem_limit_bytes=24 * 1024 * 1024),
        cost_estimate=cost(16),
        name="adam",
    )(place, heights, *grads, *weights, *small_weights)


def exchange(pieces, axis, count, shifts):
    return [
        piece if s == 0 else lax.ppermute(piece, axis, [(i, i ^ s) for i in range(count)])
        for piece, s in zip(pieces, shifts)
    ]


def scatter_over(values, axis, count, size):
    me = lax.axis_index(axis)
    values = jnp.pad(values, ((0, 0), (0, count * size - values.shape[1]), (0, 0)))
    pieces = [lax.dynamic_slice_in_dim(values, (me ^ s) * size, size, axis=1) for s in range(count)]
    return exchange(pieces, axis, count, range(count))


def added(parts):
    return sum(part.astype(f32) for part in parts).astype(bf16)


def two_parts(values):
    coarse = lax.reduce_precision(values, exponent_bits=8, mantissa_bits=7)
    return coarse.astype(bf16), (values - coarse).astype(bf16)


def after_all(values, *others):
    return lax.optimization_barrier((values, others))[0]


def pad_to(values, shape):
    return jnp.pad(values, [(0, n - m) for n, m in zip(shape, values.shape)])


def on_device(
    fields,
    noise_fields,
    target_fields,
    band_heights,
    tap_offsets,
    expand_weight,
    expand_bias,
    reduce_weight,
    channel_vectors,
    disco_filter,
    noise_mixing,
    first_expand,
    second_expand,
    first_bias,
    second_bias,
    first_reduce,
    second_reduce,
    first_vectors,
    second_vectors,
    first_filter,
    second_filter,
    first_mixing,
    second_mixing,
):
    members = lax.axis_size("member")
    stacks = lax.axis_size("stack")
    lat_count = 2 * stacks
    lat = ("stack", "core")
    channels, hidden = expand_weight.shape
    lon = fields.shape[3]
    sz = Sizes(members, channels, hidden, noise_fields.shape[1], lon)
    me = lax.axis_index("member")
    core = lax.axis_index("core")
    band = lax.axis_index("stack") * 2 + core
    height = lax.dynamic_slice_in_dim(band_heights, band, 1)

    shifts = [0, members - 1, *range(1, members - 1)]
    pieces = split_call(sz, shifts, band_heights, band.reshape(1), me.reshape(1), fields, noise_fields)
    arrived = exchange(pieces, "member", members, shifts)
    upward = [(i, i + 1) for i in range(lat_count - 1)]
    downward = [(i + 1, i) for i in range(lat_count - 1)]

    def edges(rows):
        bottom = jnp.stack([x[1] for x in rows])
        top = jnp.stack([x[0] for x in rows])
        return lax.ppermute(bottom, lat, upward), lax.ppermute(top, lat, downward)

    truth = pad_to(target_fields, (channels, 2, lon + sz.pr - sz.q))
    truth = lax.dynamic_slice_in_dim(truth, me * sz.q, sz.pr, axis=2)
    truth = pad_to(jnp.transpose(truth, (1, 2, 0)), (2, sz.pr, sz.cp)).reshape(sz.pe, sz.cp)

    expand_low = pad_to(after_all(expand_weight, pieces).astype(bf16), (sz.cp, sz.hp))
    reduce_low = pad_to(reduce_weight.T.astype(bf16), (sz.cp, sz.hp))
    bias = pad_to(expand_bias[None], (1, sz.hp))
    gain = pad_to(channel_vectors[0:1], (1, sz.cp))
    outbias = pad_to(channel_vectors[1:2], (1, sz.cp))
    filt = jnp.transpose(pad_to(disco_filter, (16, sz.cp)).reshape(16, sz.ct, 128), (1, 0, 2))
    spot = channels - (sz.ct - 1) * 128
    coarse, fine = two_parts(noise_mixing)
    noisemix = jnp.zeros((256, sz.cp), bf16)
    noisemix = noisemix.at[spot : spot + sz.k, :channels].set(coarse)
    noisemix = noisemix.at[128 + spot : 128 + spot + sz.k, :channels].set(fine)

    weights = (expand_low, bias, reduce_low, gain, outbias, filt, noisemix)
    core_id = core.reshape(1)
    own_edges = edges(after_all(arrived[:1], expand_low))
    state = own_call(sz, height, tap_offsets, arrived[0][None], *own_edges, weights)
    others = after_all(arrived[1:], state)
    other_edges = edges(others)
    x = jnp.stack([arrived[0], *others])
    mine, other, bg, pg, normed, small = main_call(
        sz, height, core_id, tap_offsets, x, *other_edges, truth, weights, state
    )

    swap = [(0, 1), (1, 0)]
    pieces = share_call(me.reshape(1), mine, lax.ppermute(other, "core", swap), members)
    cut = members // 2

    def unmix_raw(base, count, pg, small):
        gn, gn_prev, gn_next, small = unmix_call(
            sz, base, count, height, tap_offsets, pg, x, normed, expand_low, filt, small
        )
        return (gn, gn_prev, gn_next), small

    def edges_back(raw):
        gn, gn_prev, gn_next = raw
        return gn, lax.ppermute(gn_next, lat, upward), lax.ppermute(gn_prev, lat, downward)

    def unmix(base, count, pg, small):
        raw, small = unmix_raw(base, count, pg, small)
        return edges_back(raw), small, raw[1]

    arriving = exchange(pieces, "member", members, range(members))
    near, small, done = unmix(0, cut, after_all(pg, pieces), small)
    arriving, done = after_all((arriving, done))
    arriving = scatter_over(added(arriving), "stack", stacks, sz.piece_rows(members, stacks))
    far_raw, small = unmix_raw(cut, members - cut, after_all(pg, done), small)

    def packed(main, small):
        return jnp.concatenate([main, *two_parts(small)], axis=0)

    def unpacked(messages):
        cut = messages[0].shape[0] - at.count
        half = at.count // 2
        parts = [m[cut:].astype(f32) for m in messages]
        return jnp.concatenate([m[:cut] for m in messages], axis=0), sum(p[:half] + p[half:] for p in parts)

    at = Rows(sz)
    arriving, far_raw, near, small = after_all((arriving, far_raw, near, small))
    small = small.reshape(2, -1, sz.mc)
    other_small = lax.dynamic_index_in_dim(small, 1 - core, 0, keepdims=False)
    small = lax.dynamic_index_in_dim(small, core, 0, keepdims=False) + lax.ppermute(other_small, "core", swap)
    near_grads = norm_back_call(sz, 0, cut, height, x, *near, bg, gain)
    small, part = after_all((small, added(arriving)))
    message = packed(part.reshape(-1, sz.mh // 2), small)
    gathered = exchange([message] * stacks, "stack", stacks, range(stacks))
    returned = exchange([near_grads[s] for s in range(cut)], "member", members, shifts[:cut])

    gathered, far_raw, returned = after_all((gathered, far_raw, returned))
    message = packed(*unpacked(gathered))
    gathered = exchange([message] * members, "member", members, range(members))
    far = edges_back(far_raw)

    far_grads = norm_back_call(sz, cut, members - cut, height, x, *far, bg, gain)
    far_pieces = [far_grads[s] for s in range(members - cut)]

    gathered, far_pieces = after_all((gathered, far_pieces))
    mine, small = unpacked(gathered)
    small = packed(mine[:0], small)
    got = lax.ppermute(mine, "core", swap)
    got_small = lax.ppermute(small, "core", swap)
    returned = returned + exchange(far_pieces, "member", members, shifts[cut:])
    pieces = [v.reshape(-1, sz.piece_rows(members, stacks), sz.mh // 2) for v in (mine, got)]

    limit = 0.02 * math.sqrt(hidden * channels * lat_count * 2 * lon / members)
    norm, mean, we, m_e, v_e, c_e, wr, m_r, v_r, c_r, *rest = adam_call(
        sz,
        limit,
        channels * lon,
        members,
        stacks,
        jnp.stack([core, me, lax.axis_index("stack")]),
        band_heights,
        (*pieces, small, got_small),
        (expand_weight, first_expand, second_expand, reduce_weight.T, first_reduce.T, second_reduce.T),
        (
            disco_filter,
            first_filter,
            second_filter,
            noise_mixing,
            first_mixing,
            second_mixing,
            channel_vectors,
            first_vectors,
            second_vectors,
            expand_bias[None],
            first_bias[None],
            second_bias[None],
        ),
    )
    input_gradient = join_call(sz, shifts, me.reshape(1), after_all(returned, norm))
    return (
        mean[0],
        input_gradient,
        norm[0],
        we,
        m_e,
        v_e,
        *rest[9:12],
        wr.T,
        m_r.T,
        v_r.T,
        *rest[6:9],
        *rest[0:3],
        *rest[3:6],
        c_e,
        c_r.T,
    )


def solution(mesh):
    members = mesh.shape["member"]
    lat = mesh.shape["lat"]
    split = Mesh(mesh.devices.reshape(members, lat // 2, 2), ("member", "stack", "core"))
    rows = ("stack", "core")
    whole = [P()] * 18
    in_specs = (
        P("member", None, rows, None),
        P("member", None, rows, None),
        P(None, rows, None),
        P(),
        P(None, rows),
        *whole,
    )
    out_specs = (P(), P("member", None, rows, None)) + (P(),) * 21
    return jax.shard_map(on_device, mesh=split, in_specs=in_specs, out_specs=out_specs, check_vma=False)
```

```python
import functools
import math

import jax
import jax.numpy as jnp
from jax import lax
from jax.experimental import pallas as pl
from jax.experimental.pallas import tpu as pltpu
from jax.sharding import Mesh, PartitionSpec as P

STEP = 10
BETA_ONE = 0.9
BETA_TWO = 0.95
ADAM_EPS = 1e-08
DECAY_RATE = 0.1
NORM_EPS = 1e-05
SMALL_RATE = 0.3
REACH = 8
f32 = jnp.float32
bf16 = jnp.bfloat16

NN = (((1,), (0,)), ((), ()))
NT = (((1,), (1,)), ((), ()))
TN = (((0,), (0,)), ((), ()))


def round_up(value, step):
    return -(-value // step) * step


def mm(a, b, dims=NN):
    return lax.dot_general(a, b, dims, preferred_element_type=f32)


class Sizes:
    def __init__(self, members, channels, hidden, noise, lon):
        self.m = members
        self.c = channels
        self.h = hidden
        self.k = noise
        self.lon = lon
        self.q = lon // members
        self.pr = round_up(self.q, 8)
        self.ext = round_up(self.pr + 2 * REACH, 8)
        self.pe = 2 * self.pr
        self.p = members * self.pe
        self.cp = round_up(channels + noise, 128)
        self.ct = self.cp // 128
        self.cr = round_up(channels, 16)
        self.hp = round_up(hidden, 128)
        self.mc = channels // 128 * 128
        self.mh = hidden // 256 * 256

    def piece_rows(self, members, stacks):
        each = self.mc // members
        return next(n for n in range(8, each + 1, 8) if each % n == 0 and n * stacks >= each)


class Rows:
    def __init__(self, sz):
        self.mixing = 9
        self.outbias = self.mixing + sz.k
        self.biasin = self.outbias + 1
        self.row_e = self.biasin + 2
        self.row_r = self.row_e + 2
        self.spare = sz.h - sz.mh
        self.col_e = self.row_r + 2
        self.col_r = self.col_e + self.spare
        self.extra = self.col_r + self.spare
        self.count = round_up(self.extra + 1, 32)
        self.x_mixing = 9
        self.x_outbias = self.x_mixing + sz.k
        self.x_biasin = self.x_outbias + 1
        self.x_row_e = self.x_biasin + self.spare
        self.x_row_r = self.x_row_e + self.spare
        self.x_loss = self.x_row_r + self.spare


def smem():
    return pl.BlockSpec(memory_space=pltpu.SMEM)


def vmem():
    return pl.BlockSpec(memory_space=pltpu.VMEM)


def tile_sum(values):
    tiles = [values[i : i + 8] for i in range(0, values.shape[0], 8)]
    while len(tiles) > 1:
        tiles = [a + b for a, b in zip(tiles[::2], tiles[1::2])] + tiles[len(tiles) // 2 * 2 :]
    return tiles[0]


def column_blocks(width, step):
    return [(i, min(step, width - i)) for i in range(0, width, step)]


def norm_rows(values, channels, lanes):
    inside = lanes < channels
    values = jnp.where(inside, values, 0.0)
    mean = jnp.sum(values, axis=1, keepdims=True) * (1.0 / channels)
    centred = jnp.where(inside, values - mean, 0.0)
    spread = jnp.sum(centred * centred, axis=1, keepdims=True) * (1.0 / channels)
    return centred, lax.rsqrt(spread + NORM_EPS)


def gelu_parts(v):
    size = jnp.abs(v)
    t = 1.0 / (1.0 + (0.3275911 * math.sqrt(0.5)) * size)
    bell = jnp.exp(-0.5 * v * v)
    poly = t * (
        0.5 * 0.254829592
        + t * (-0.5 * 0.284496736 + t * (0.5 * 1.421413741 + t * (-0.5 * 1.453152027 + t * (0.5 * 1.061405429))))
    )
    tail = poly * bell
    cdf = jnp.where(v >= 0.0, 1.0 - tail, tail)
    return v * cdf, cdf + v * bell * (1.0 / math.sqrt(2.0 * math.pi))


def cost(microseconds):
    return pl.CostEstimate(flops=int(microseconds * 5e7), bytes_accessed=0, transcendentals=0)


def transpose_into(sz, src, dst):
    def move(at, count):
        for ct in range(sz.ct):
            block = src[pl.ds(at, count), ct * 128 : (ct + 1) * 128].T
            size = min(128, sz.cr - ct * 128)
            if size > 0:
                dst[ct * 128 : ct * 128 + size, pl.ds(at, count)] = block[:size]

    def body(i, c):
        move(pl.multiple_of(i * 128, 128), 128)
        return c

    lax.fori_loop(0, sz.p // 128, body, 0)
    if sz.p % 128:
        move(sz.p // 128 * 128, sz.p % 128)


def weight_grad(sz, core, left_ref, right_ref, left_t_ref, mine_ref, other_ref, row_ref, col_ref):
    transpose_into(sz, left_ref, left_t_ref)
    half = sz.mh // 2
    for half_ref, which in ((other_ref, 1 - core), (mine_ref, core)):
        for at, width in column_blocks(half, 256):
            cols = pl.ds(pl.multiple_of(which * half + at, 128), width)
            block = mm(left_t_ref[...], right_ref[:, cols])
            row_ref[:, cols] = block[sz.mc :]
            half_ref[:, at : at + width] = block[: sz.mc].astype(bf16)
    rest = right_ref[:, sz.mh :]
    row_ref[:, sz.mh :] = mm(left_t_ref[sz.mc :, :], rest)
    col_ref[...] = mm(rest.astype(f32).T[0:16].astype(bf16), left_ref[...])


def split_kernel(sz, shifts, heights_ref, band_ref, me_ref, x_hbm, noise_hbm, *refs):
    places, (y_ref, s_ref, x_ref, noise_ref, out_ref, in_sems, out_sems) = refs[: sz.m], refs[sz.m :]
    loads = []
    for ct in range(sz.ct):
        channels = pl.ds(ct * 128, min(128, sz.c - ct * 128))
        loads.append(pltpu.make_async_copy(x_hbm.at[:, channels], x_ref.at[:, channels], in_sems.at[ct]))
    loads.append(pltpu.make_async_copy(noise_hbm, noise_ref, in_sems.at[sz.ct]))
    for load in loads:
        load.start()
    for ct in range(sz.ct):
        first = ct * 128
        loads[ct].wait()
        if ct < sz.ct - 1:
            spans = [(x_ref, first, 128, 0)]
        else:
            rest = sz.c - first
            loads[sz.ct].wait()
            s_ref[...] = jnp.zeros_like(s_ref)
            spans = [(x_ref, first, rest, 0), (noise_ref, 0, sz.k, rest)]
        for ref, at, count, to in spans:
            for lt, width in column_blocks(sz.lon, 128):
                block = ref[0, at : at + count, :, lt : lt + width].astype(f32)
                s_ref[lt // 128, 2 * to : 2 * (to + count), :width] = block.reshape(2 * count, width)
        for r in range(2):
            for lt, width in column_blocks(sz.lon, 128):
                block = s_ref[lt // 128, pl.ds(r, 128, stride=2), :].T
                y_ref[r, ct, REACH + lt : REACH + lt + width, :] = block[:width]
    for r in range(2):
        for ct in range(sz.ct):
            y_ref[r, ct, :REACH, :] = y_ref[r, ct, sz.lon : sz.lon + REACH, :]
            y_ref[r, ct, REACH + sz.lon :, :] = y_ref[r, ct, REACH : sz.ext - sz.q, :]
    stores = []
    for s in (*range(1, sz.m), 0):
        start = (me_ref[0] ^ shifts[s]) * sz.q
        for r, row in enumerate((0, heights_ref[band_ref[0]] - 1)):
            for ct in range(sz.ct):
                out_ref[s, r, :, ct * 128 : (ct + 1) * 128] = y_ref[row, ct, pl.ds(start, sz.ext), :].astype(bf16)
        stores.append(pltpu.make_async_copy(out_ref.at[s], places[s], out_sems.at[s]))
        stores[-1].start()
    for store in stores:
        store.wait()


def split_call(sz, shifts, heights, band, me, x, noise):
    outs = tuple(jax.ShapeDtypeStruct((2, sz.ext, sz.cp), bf16) for _ in range(sz.m))
    anywhere = pl.BlockSpec(memory_space=pltpu.HBM)
    return pl.pallas_call(
        functools.partial(split_kernel, sz, shifts),
        out_shape=outs,
        in_specs=[smem(), smem(), smem(), anywhere, anywhere],
        out_specs=tuple(anywhere for _ in outs),
        scratch_shapes=[
            pltpu.VMEM((2, sz.ct, sz.lon + sz.ext - sz.q, 128), f32),
            pltpu.VMEM((round_up(sz.lon, 128) // 128, 256, 128), f32),
            pltpu.VMEM(x.shape, bf16),
            pltpu.VMEM(noise.shape, bf16),
            pltpu.VMEM((sz.m, 2, sz.ext, sz.cp), bf16),
            pltpu.SemaphoreType.DMA((sz.ct + 1,)),
            pltpu.SemaphoreType.DMA((sz.m,)),
        ],
        compiler_params=pltpu.CompilerParams(vmem_limit_bytes=50 * 1024 * 1024),
        cost_estimate=cost(5),
        name="split",
    )(heights, band, me, x, noise)


def join_kernel(sz, shifts, me_ref, *refs):
    pieces, out_ref, y_ref, t_ref, s_ref = refs[: sz.m], *refs[sz.m :]
    inner = slice(REACH, REACH + sz.q)
    starts = [(me_ref[0] ^ shift) * sz.q for shift in shifts]
    for s in range(sz.m):
        for r in range(2):
            for ct in range(sz.ct):
                part = pieces[s][r, :, ct * 128 : (ct + 1) * 128].astype(f32)
                y_ref[r, ct, pl.ds(starts[s] + REACH, sz.q), :] = part[inner]
                s_ref[s, r, ct, :REACH] = part[:REACH]
                s_ref[s, r, ct, REACH:] = part[REACH + sz.q : 2 * REACH + sz.q]
    for s in range(sz.m):
        left = jnp.where(starts[s] == 0, sz.lon, starts[s])
        right = jnp.where(starts[s] == sz.lon - sz.q, REACH, starts[s] + REACH + sz.q)
        for r in range(2):
            for ct in range(sz.ct):
                y_ref[r, ct, pl.ds(left, REACH), :] += s_ref[s, r, ct, :REACH]
                y_ref[r, ct, pl.ds(right, REACH), :] += s_ref[s, r, ct, REACH:]
    for ct in range(sz.ct):
        for r in range(2):
            for lt in range(0, sz.lon, 128):
                block = y_ref[r, ct, REACH + lt : REACH + lt + 128, :].T
                t_ref[lt // 128, pl.ds(r, 128, stride=2), :] = block
        size = min(128, sz.c - ct * 128)
        for lt, width in column_blocks(sz.lon, 128):
            block = t_ref[lt // 128, : 2 * size, :width].reshape(size, 2, width)
            out_ref[0, ct * 128 : ct * 128 + size, :, lt : lt + width] = block.astype(bf16)


def join_call(sz, shifts, me, pieces):
    return pl.pallas_call(
        functools.partial(join_kernel, sz, shifts),
        out_shape=jax.ShapeDtypeStruct((1, sz.c, 2, sz.lon), bf16),
        in_specs=[smem()] + [vmem()] * sz.m,
        out_specs=vmem(),
        scratch_shapes=[
            pltpu.VMEM((2, sz.ct, REACH + max(round_up(sz.lon, 128), sz.lon + sz.ext - sz.q - REACH), 128), f32),
            pltpu.VMEM((round_up(sz.lon, 128) // 128, 256, 128), f32),
            pltpu.VMEM((sz.m, 2, sz.ct, 2 * REACH, 128), f32),
        ],
        compiler_params=pltpu.CompilerParams(vmem_limit_bytes=24 * 1024 * 1024),
        cost_estimate=cost(6),
        name="join",
    )(me, *pieces)


def norm_and_filter(sz, e, height_ref, taps_ref, x_ref, prev_ref, next_ref, gain_ref, filter_ref, normed_ref, n_ref, fil_ref):
    lanes = lax.broadcasted_iota(jnp.int32, (1, sz.cp), 1)
    below_first = jnp.where(height_ref[0] == 2, 2, 3)
    sources = ((0, 1, below_first), (1, 2, 3))

    def norm_store(values, row):
        centred, inv = norm_rows(values.astype(f32), sz.c, lanes)
        normed = (centred * inv * gain_ref[...]).astype(bf16)
        normed_ref[e, row] = normed
        normed = normed.astype(f32)
        for ct in range(sz.ct):
            n_ref[row, ct] = normed[:, ct * 128 : (ct + 1) * 128]

    norm_store(prev_ref[e], 0)
    norm_store(x_ref[e, 0], 1)
    norm_store(x_ref[e, 1], 2)
    norm_store(next_ref[e], 3)

    def filter_tile(ct, c):
        for r in range(2):
            acc = jnp.zeros((sz.pr, 128), f32)
            for a in range(3):
                for j in range(3):
                    tap = 3 * a + j
                    start = taps_ref[tap, r] + REACH
                    moved = n_ref[sources[r][a], ct, pl.ds(start, sz.pr), :]
                    acc = acc + filter_ref[ct, tap : tap + 1, :] * moved
            fil_ref[ct, r * sz.pr : (r + 1) * sz.pr, :] = acc
        return c

    lax.fori_loop(0, sz.ct, filter_tile, 0)


def feed_forward(sz, e, x_ref, fil_ref, expand_ref, bias_ref, reduce_ref, outbias_ref, noisemix_ref, store):
    own = jnp.concatenate([x_ref[e, r].astype(f32)[REACH : REACH + sz.pr] for r in range(2)], axis=0)
    noise = own[:, (sz.ct - 1) * 128 :].astype(bf16)
    mixed = mm(jnp.concatenate([noise, noise], axis=1), noisemix_ref[...])
    filtered = jnp.concatenate([fil_ref[ct] for ct in range(sz.ct)], axis=1)
    lanes = lax.broadcasted_iota(jnp.int32, (1, sz.cp), 1)
    mixed = jnp.where(lanes == sz.c, 1.0, filtered + mixed).astype(bf16)
    store("mixed", slice(0, sz.cp), mixed)
    acts = []
    for at, width in column_blocks(sz.hp, 256):
        pre = mm(mixed, expand_ref[:, at : at + width]) + bias_ref[:, at : at + width]
        act, slope = gelu_parts(pre)
        if at <= sz.h < at + width:
            units = at + lax.broadcasted_iota(jnp.int32, (1, width), 1)
            act = jnp.where(units == sz.h, 1.0, act)
        acts.append(act.astype(bf16))
        store("act", slice(at, at + width), acts[-1])
        store("slope", slice(at, at + width), slope.astype(bf16))
    act = jnp.concatenate(acts, axis=1)
    return own + (mm(act, reduce_ref[...], NT) + outbias_ref[...])


def own_kernel(
    sz,
    height_ref,
    taps_ref,
    x_ref,
    prev_ref,
    next_ref,
    expand_ref,
    bias_ref,
    reduce_ref,
    gain_ref,
    outbias_ref,
    filter_ref,
    noisemix_ref,
    normed_ref,
    mx_ref,
    act_ref,
    dg_ref,
    pred_ref,
    n_ref,
    fil_ref,
):
    norm_and_filter(sz, 0, height_ref, taps_ref, x_ref, prev_ref, next_ref, gain_ref, filter_ref, normed_ref, n_ref, fil_ref)
    places = {"mixed": mx_ref, "act": act_ref, "slope": dg_ref}

    def store(name, cols, values):
        places[name][:, cols] = values

    pred_ref[...] = feed_forward(
        sz, 0, x_ref, fil_ref, expand_ref, bias_ref, reduce_ref, outbias_ref, noisemix_ref, store
    )


def filter_scratch(sz):
    return [pltpu.VMEM((4, sz.ct, sz.ext, 128), f32), pltpu.VMEM((sz.ct, sz.pe, 128), f32)]


def own_call(sz, height, taps, x, prev, after, weights):
    shape = jax.ShapeDtypeStruct
    outs = (
        shape((sz.m, 4, sz.ext, sz.cp), bf16),
        shape((sz.pe, sz.cp), bf16),
        shape((sz.pe, sz.hp), bf16),
        shape((sz.pe, sz.hp), bf16),
        shape((sz.pe, sz.cp), f32),
    )
    return pl.pallas_call(
        functools.partial(own_kernel, sz),
        grid=(1,),
        out_shape=outs,
        in_specs=[smem(), smem()] + [vmem()] * 10,
        out_specs=(pl.BlockSpec((1, 4, sz.ext, sz.cp), lambda i: (0, 0, 0, 0)),) + (vmem(),) * 4,
        scratch_shapes=filter_scratch(sz),
        compiler_params=pltpu.CompilerParams(vmem_limit_bytes=50 * 1024 * 1024),
        cost_estimate=cost(8),
        name="own",
    )(height, taps, x, prev, after, *weights)


def main_kernel(
    sz,
    height_ref,
    core_ref,
    taps_ref,
    bias_ref,
    gain_ref,
    outbias_ref,
    filter_ref,
    noisemix_ref,
    x_hbm,
    prev_hbm,
    next_hbm,
    target_hbm,
    expand_hbm,
    reduce_hbm,
    normed_own_hbm,
    mx_hbm,
    act_hbm,
    dg_hbm,
    pred_hbm,
    mine_hbm,
    other_hbm,
    bg_hbm,
    pg_hbm,
    normed_hbm,
    small_ref,
    x_ref,
    prev_ref,
    next_ref,
    target_ref,
    expand_ref,
    reduce_ref,
    mine_ref,
    other_ref,
    bg_ref,
    pg_ref,
    n_ref,
    fil_ref,
    nb_ref,
    mx_ref,
    act_ref,
    dg_ref,
    pred_ref,
    tr_ref,
    row_e_ref,
    row_r_ref,
    col_e_ref,
    col_r_ref,
    loss_ref,
    in_sems,
    out_sems,
):
    first = pl.ds(0, sz.pe)
    others = pl.ds(1, sz.m - 1)
    early = [
        pltpu.make_async_copy(x_hbm.at[others], x_ref, in_sems.at[0]),
        pltpu.make_async_copy(prev_hbm, prev_ref, in_sems.at[1]),
        pltpu.make_async_copy(next_hbm, next_ref, in_sems.at[2]),
    ]
    expand_load = pltpu.make_async_copy(expand_hbm, expand_ref, in_sems.at[3])
    reduce_load = pltpu.make_async_copy(reduce_hbm, reduce_ref, in_sems.at[4])
    loads = [
        pltpu.make_async_copy(mx_hbm, mx_ref.at[first], in_sems.at[5]),
        pltpu.make_async_copy(act_hbm, act_ref.at[first], in_sems.at[6]),
        pltpu.make_async_copy(dg_hbm, dg_ref.at[first], in_sems.at[7]),
        pltpu.make_async_copy(pred_hbm, pred_ref.at[0], in_sems.at[8]),
        pltpu.make_async_copy(target_hbm, target_ref, in_sems.at[9]),
    ]
    for load in (*early, expand_load, reduce_load, *loads):
        load.start()
    for load in early:
        load.wait()

    def forward(e, carry):
        norm_and_filter(
            sz, e, height_ref, taps_ref, x_ref, prev_ref, next_ref, gain_ref, filter_ref, nb_ref, n_ref, fil_ref
        )

        @pl.when(e == 0)
        def _():
            expand_load.wait()
            reduce_load.wait()

        rows = pl.ds(pl.multiple_of((e + 1) * sz.pe, 16), sz.pe)
        places = {"mixed": mx_ref, "act": act_ref, "slope": dg_ref}

        def store(name, cols, values):
            places[name][rows, cols] = values

        pred_ref[e + 1] = feed_forward(
            sz, e, x_ref, fil_ref, expand_ref, bias_ref, reduce_ref, outbias_ref, noisemix_ref, store
        )
        return carry

    lax.fori_loop(0, sz.m - 1, forward, 0)
    save = pltpu.make_async_copy(nb_ref, normed_hbm.at[pl.ds(1, sz.m - 1)], out_sems.at[0])
    save.start()
    for load in loads:
        load.wait()

    height = height_ref[0]
    lanes = lax.broadcasted_iota(jnp.int32, (1, sz.cp), 1)
    inside = (lanes < sz.c).astype(f32)
    loss_ref[...] = jnp.zeros_like(loss_ref)
    step = 16
    inv_m = 1.0 / sz.m
    inv_mm = inv_m * inv_m

    def score(i, carry):
        at = pl.multiple_of(i * step, step)
        pixel = at + lax.broadcasted_iota(jnp.int32, (step, 1), 0)
        row = (pixel >= sz.pr).astype(jnp.int32)
        use = (pixel - row * sz.pr < sz.q) & (row < height)
        mask_rows = use.astype(f32)
        for ct in range(sz.ct):
            cols = slice(ct * 128, (ct + 1) * 128)
            mask = mask_rows * inside[:, cols]
            preds = [pred_ref[e, pl.ds(at, step), cols] for e in range(sz.m)]
            truth = target_ref[pl.ds(at, step), cols].astype(f32)
            slopes = []
            own_sum = 0.0
            for p in preds:
                d = p - truth
                q = d * d + 1.0
                r = lax.rsqrt(q)
                own_sum = own_sum + q * r
                slopes.append(d * r * inv_m)
            pair_sum = 0.0
            pairs = [0.0] * sz.m
            for a in range(sz.m):
                for b in range(a + 1, sz.m):
                    d = preds[a] - preds[b]
                    q = d * d + 1.0
                    r = lax.rsqrt(q)
                    pair_sum = pair_sum + q * r
                    s = d * r
                    pairs[a] = pairs[a] + s
                    pairs[b] = pairs[b] - s
            value = own_sum * inv_m - (pair_sum + 0.5 * sz.m) * inv_mm
            value = mask * value
            loss_ref[:, cols] += value[0:8] + value[8:16]
            for e in range(sz.m):
                g = (mask * (slopes[e] - pairs[e] * inv_mm)).astype(bf16)
                where = pl.ds(pl.multiple_of(e * sz.pe + at, 16), step)
                bg_ref[where, cols] = g
        return carry

    lax.fori_loop(0, sz.pe // step, score, 0)
    core = core_ref[0]
    saves = [save]

    def write(here, there, which):
        saves.append(pltpu.make_async_copy(here, there, out_sems.at[which]))
        saves[-1].start()

    write(bg_ref, bg_hbm, 1)
    weight_grad(sz, core, bg_ref, act_ref, tr_ref, mine_ref.at[1], other_ref.at[1], row_r_ref, col_r_ref)
    write(mine_ref.at[1], mine_hbm.at[1], 2)
    write(other_ref.at[1], other_hbm.at[1], 3)


    def backward(e, carry):
        rows = pl.ds(pl.multiple_of(e * sz.pe, 16), sz.pe)
        bg = bg_ref[rows, :]
        for at, width in column_blocks(sz.hp, 256):
            grad = mm(bg, reduce_ref[:, at : at + width])
            pre = (grad * dg_ref[rows, at : at + width].astype(f32)).astype(bf16)
            pg_ref[rows, at : at + width] = pre
        return carry

    lax.fori_loop(0, sz.m, backward, 0)
    write(pg_ref, pg_hbm, 4)
    weight_grad(sz, core, mx_ref, pg_ref, tr_ref, mine_ref.at[0], other_ref.at[0], row_e_ref, col_e_ref)
    write(other_ref.at[0], other_hbm.at[0], 5)
    write(mine_ref.at[0], mine_hbm.at[0], 6)
    at = Rows(sz)
    small_ref[...] = jnp.zeros_like(small_ref)
    lane = lax.broadcasted_iota(jnp.int32, (1, sz.mc), 1)
    half = sz.mh // 2

    def column_sum(ref):
        return jnp.sum(ref[...], axis=0, keepdims=True)

    def long_row(row, place, values, extra):
        small_ref[row : row + 1, :] = values[:, :half]
        small_ref[row + 1 : row + 2, :] = values[:, half : sz.mh]
        for i in range(at.spare):
            extra = jnp.where(lane == place + i, values[:, sz.mh + i : sz.mh + i + 1], extra)
        return extra

    extra = jnp.zeros((1, sz.mc), f32)
    outbias_grad = col_r_ref[at.spare : at.spare + 1, :]
    small_ref[at.outbias : at.outbias + 1, :] = outbias_grad[:, : sz.mc]
    extra = jnp.where(lane == at.x_outbias, outbias_grad[:, sz.mc : sz.mc + 1], extra)
    extra = long_row(at.biasin, at.x_biasin, row_e_ref[sz.c - sz.mc : sz.c - sz.mc + 1, :], extra)
    extra = long_row(at.row_e, at.x_row_e, row_e_ref[0:1, :], extra)
    extra = long_row(at.row_r, at.x_row_r, row_r_ref[0:1, :], extra)
    small_ref[at.col_e : at.col_e + at.spare, :] = col_e_ref[: at.spare, : sz.mc]
    small_ref[at.col_r : at.col_r + at.spare, :] = col_r_ref[: at.spare, : sz.mc]
    extra = jnp.where(lane == at.x_loss, jnp.sum(column_sum(loss_ref), axis=1, keepdims=True), extra)
    small_ref[at.extra : at.extra + 1, :] = extra
    for save in saves:
        save.wait()


def main_call(sz, height, core, taps, x, prev, after, target, weights, state):
    shape = jax.ShapeDtypeStruct
    half = shape((2, sz.mc, sz.mh // 2), bf16)
    outs = (
        half,
        half,
        shape((sz.p, sz.cp), bf16),
        shape((sz.p, sz.hp), bf16),
        shape((sz.m, 4, sz.ext, sz.cp), bf16),
        shape((Rows(sz).count, sz.mc), f32),
    )
    anywhere = pl.BlockSpec(memory_space=pl.ANY)
    expand, bias, reduce, gain, outbias, filt, noisemix = weights
    return pl.pallas_call(
        functools.partial(main_kernel, sz),
        out_shape=outs,
        in_specs=[smem()] * 3 + [vmem()] * 5 + [anywhere] * 11,
        out_specs=(anywhere,) * 5 + (vmem(),),
        input_output_aliases={14: 4},
        scratch_shapes=[
            pltpu.VMEM((sz.m - 1, 2, sz.ext, sz.cp), bf16),
            pltpu.VMEM((sz.m - 1, sz.ext, sz.cp), bf16),
            pltpu.VMEM((sz.m - 1, sz.ext, sz.cp), bf16),
            pltpu.VMEM((sz.pe, sz.cp), bf16),
            pltpu.VMEM((sz.cp, sz.hp), bf16),
            pltpu.VMEM((sz.cp, sz.hp), bf16),
            pltpu.VMEM((2, sz.mc, sz.mh // 2), bf16),
            pltpu.VMEM((2, sz.mc, sz.mh // 2), bf16),
            pltpu.VMEM((sz.p, sz.cp), bf16),
            pltpu.VMEM((sz.p, sz.hp), bf16),
            *filter_scratch(sz),
            pltpu.VMEM((sz.m - 1, 4, sz.ext, sz.cp), bf16),
            pltpu.VMEM((sz.p, sz.cp), bf16),
            pltpu.VMEM((sz.p, sz.hp), bf16),
            pltpu.VMEM((sz.p, sz.hp), bf16),
            pltpu.VMEM((sz.m, sz.pe, sz.cp), f32),
            pltpu.VMEM((sz.cr, sz.p), bf16),
            pltpu.VMEM((sz.cr - sz.mc, sz.hp), f32),
            pltpu.VMEM((sz.cr - sz.mc, sz.hp), f32),
            pltpu.VMEM((16, sz.cp), f32),
            pltpu.VMEM((16, sz.cp), f32),
            pltpu.VMEM((8, sz.cp), f32),
            pltpu.SemaphoreType.DMA((10,)),
            pltpu.SemaphoreType.DMA((7,)),
        ],
        compiler_params=pltpu.CompilerParams(vmem_limit_bytes=50 * 1024 * 1024),
        cost_estimate=cost(40),
        name="main",
    )(height, core, taps, bias, gain, outbias, filt, noisemix, x, prev, after, target, expand, reduce, *state)


def share_kernel(size, me_ref, mine_ref, got_ref, *outs):
    for s, out_ref in enumerate(outs):
        rows = pl.ds(pl.multiple_of((me_ref[0] ^ s) * size, 16), size)
        for kind in range(2):
            total = mine_ref[kind, rows, :].astype(f32) + got_ref[kind, rows, :].astype(f32)
            out_ref[kind] = total.astype(bf16)


def share_call(me, mine, got, count):
    kinds, rows, width = mine.shape
    size = rows // count
    outs = tuple(jax.ShapeDtypeStruct((kinds, size, width), bf16) for _ in range(count))
    return pl.pallas_call(
        functools.partial(share_kernel, size),
        out_shape=outs,
        in_specs=[smem(), vmem(), vmem()],
        out_specs=tuple(vmem() for _ in outs),
        compiler_params=pltpu.CompilerParams(vmem_limit_bytes=16 * 1024 * 1024),
        cost_estimate=cost(2),
        name="share",
    )(me, pltpu.with_memory_space_constraint(mine, pltpu.HBM), got)


def unmix_kernel(
    sz,
    base,
    count,
    height_ref,
    taps_ref,
    filter_ref,
    small_in_ref,
    pg_hbm,
    x_hbm,
    normed_hbm,
    expand_hbm,
    gn_own_hbm,
    gn_prev_hbm,
    gn_next_hbm,
    small_ref,
    pg_ref,
    x_ref,
    normed_ref,
    expand_ref,
    own_ref,
    edge_ref,
    filter_grad_ref,
    mixing_grad_ref,
    n_ref,
    gn_ref,
    gm_ref,
    in_sems,
    out_sems,
):
    below_first = jnp.where(height_ref[0] == 2, 2, 3)
    sources = ((0, 1, below_first), (1, 2, 3))
    last = sz.ct - 1
    weights = pltpu.make_async_copy(expand_hbm, expand_ref, in_sems.at[0])
    weights.start()
    loads = []
    for e in range(count):
        rows = pl.ds((base + e) * sz.pe, sz.pe)
        channels = pl.ds(last * 128, 128)
        loads.append(
            (
                pltpu.make_async_copy(pg_hbm.at[rows], pg_ref.at[e], in_sems.at[3 * e + 1]),
                pltpu.make_async_copy(x_hbm.at[base + e, :, :, channels], x_ref.at[e], in_sems.at[3 * e + 2]),
                pltpu.make_async_copy(normed_hbm.at[base + e], normed_ref.at[e], in_sems.at[3 * e + 3]),
            )
        )
    for load in loads[0]:
        load.start()
    filter_grad_ref[...] = jnp.zeros_like(filter_grad_ref)
    mixing_grad_ref[...] = jnp.zeros_like(mixing_grad_ref)
    pad = 2 * REACH
    for r in range(2):
        for ct in range(sz.ct):
            gm_ref[r, ct, :pad, :] = jnp.zeros((pad, 128), f32)
            gm_ref[r, ct, pad + sz.pr :, :] = jnp.zeros((sz.ext + REACH - sz.pr, 128), f32)
    weights.wait()
    stores = []
    for e in range(count):
        loads[e][0].wait()
        if e + 1 < count:
            for load in loads[e + 1]:
                load.start()
        gm = mm(pg_ref[e], expand_ref[...], NT)
        for r in range(2):
            for ct in range(sz.ct):
                gm_ref[r, ct, pad : pad + sz.pr, :] = gm[r * sz.pr : (r + 1) * sz.pr, ct * 128 : (ct + 1) * 128]
        for load in loads[e][1:]:
            load.wait()
        for row in range(4):
            normed = normed_ref[e, row].astype(f32)
            for ct in range(sz.ct):
                n_ref[row, ct] = normed[:, ct * 128 : (ct + 1) * 128]
        noise = jnp.concatenate([x_ref[e, r].astype(f32)[REACH : REACH + sz.pr] for r in range(2)], axis=0)
        mixing_grad_ref[...] += mm(noise.T[0:16].astype(bf16), gm.astype(bf16))

        def unfilter_tile(ct, c):
            def gathered(*readers):
                acc = jnp.zeros((sz.ext, 128), f32)
                for r, a in readers:
                    for tap in range(3 * a, 3 * a + 3):
                        start = REACH - taps_ref[tap, r]
                        acc = acc + filter_ref[ct, tap : tap + 1, :] * gm_ref[r, ct, pl.ds(start, sz.ext), :]
                return acc

            gn_ref[0, ct] = gathered((0, 0))
            gn_ref[1, ct] = gathered((0, 1), (1, 0))
            gn_ref[2, ct] = gathered((1, 1))
            gn_ref[3, ct] = gathered((1, 2))
            gn_ref[below_first, ct] += gathered((0, 2))
            for r in range(2):
                g = gm_ref[r, ct, pad : pad + sz.pr, :]
                for a in range(3):
                    for tap in range(3 * a, 3 * a + 3):
                        read = n_ref[sources[r][a], ct, pl.ds(taps_ref[tap, r] + REACH, sz.pr), :]
                        filter_grad_ref[ct, tap] += tile_sum(g * read)
            return c

        lax.fori_loop(0, sz.ct, unfilter_tile, 0)
        for ct in range(sz.ct):
            cols = slice(ct * 128, (ct + 1) * 128)
            edge_ref[e, 0, :, cols] = gn_ref[0, ct].astype(bf16)
            edge_ref[e, 1, :, cols] = gn_ref[3, ct].astype(bf16)
            own_ref[e, 0, :, cols] = gn_ref[1, ct].astype(bf16)
            own_ref[e, 1, :, cols] = gn_ref[2, ct].astype(bf16)
        stores += [
            pltpu.make_async_copy(own_ref.at[e], gn_own_hbm.at[e], out_sems.at[3 * e]),
            pltpu.make_async_copy(edge_ref.at[e, 0], gn_prev_hbm.at[e], out_sems.at[3 * e + 1]),
            pltpu.make_async_copy(edge_ref.at[e, 1], gn_next_hbm.at[e], out_sems.at[3 * e + 2]),
        ]
        for store in stores[-3:]:
            store.start()

    at = Rows(sz)
    lane = lax.broadcasted_iota(jnp.int32, (1, sz.mc), 1)
    small_ref[...] = small_in_ref[...]
    extra = small_in_ref[at.extra : at.extra + 1, :]
    first = sz.c - last * 128
    for tap in range(9):
        for ct in range(last):
            row = jnp.sum(filter_grad_ref[ct, tap], axis=0, keepdims=True)
            small_ref[tap : tap + 1, ct * 128 : (ct + 1) * 128] += row
        row = jnp.sum(filter_grad_ref[last, tap], axis=0, keepdims=True)
        extra = extra + jnp.where(lane == tap, row[:, 0:1], 0.0)
    mixing = mixing_grad_ref[first : first + sz.k, :]
    small_ref[at.mixing : at.mixing + sz.k, :] += mixing[:, : sz.mc]
    for i in range(sz.k):
        extra = extra + jnp.where(lane == at.x_mixing + i, mixing[i : i + 1, sz.mc : sz.mc + 1], 0.0)
    small_ref[at.extra : at.extra + 1, :] = extra
    for store in stores:
        store.wait()


def unmix_call(sz, base, count, height, taps, pg, x, normed, expand, filt, small):
    shape = jax.ShapeDtypeStruct
    outs = (
        shape((count, 2, sz.ext, sz.cp), bf16),
        shape((count, sz.ext, sz.cp), bf16),
        shape((count, sz.ext, sz.cp), bf16),
        shape(small.shape, f32),
    )
    anywhere = pl.BlockSpec(memory_space=pltpu.HBM)
    return pl.pallas_call(
        functools.partial(unmix_kernel, sz, base, count),
        out_shape=outs,
        in_specs=[smem(), smem(), vmem(), vmem()] + [anywhere] * 4,
        out_specs=(anywhere,) * 3 + (vmem(),),
        scratch_shapes=[
            pltpu.VMEM((count, sz.pe, sz.hp), bf16),
            pltpu.VMEM((count, 2, sz.ext, 128), bf16),
            pltpu.VMEM((count, 4, sz.ext, sz.cp), bf16),
            pltpu.VMEM((sz.cp, sz.hp), bf16),
            pltpu.VMEM((count, 2, sz.ext, sz.cp), bf16),
            pltpu.VMEM((count, 2, sz.ext, sz.cp), bf16),
            pltpu.VMEM((sz.ct, 9, 8, 128), f32),
            pltpu.VMEM((16, sz.cp), f32),
            pltpu.VMEM((4, sz.ct, sz.ext, 128), f32),
            pltpu.VMEM((4, sz.ct, sz.ext, 128), f32),
            pltpu.VMEM((2, sz.ct, sz.ext + 3 * REACH, 128), f32),
            pltpu.SemaphoreType.DMA((3 * count + 1,)),
            pltpu.SemaphoreType.DMA((3 * count,)),
        ],
        compiler_params=pltpu.CompilerParams(vmem_limit_bytes=28 * 1024 * 1024),
        cost_estimate=cost(5 * count),
        name="unmix",
    )(height, taps, filt, small, *(pltpu.with_memory_space_constraint(v, pltpu.HBM) for v in (pg, x, normed, expand)))


def norm_back_kernel(sz, height_ref, x_ref, gn_ref, up_ref, down_ref, bg_ref, gain_ref, out_ref):
    height = height_ref[0]
    lanes = lax.broadcasted_iota(jnp.int32, (1, sz.cp), 1)
    from_up = up_ref[0].astype(f32)
    from_down = down_ref[0].astype(f32)
    direct = bg_ref[...].astype(f32)
    for r in range(2):
        centred, inv = norm_rows(x_ref[0, r].astype(f32), sz.c, lanes)
        xhat = centred * inv
        g = gn_ref[0, r].astype(f32) + jnp.where(height == r + 1, from_down, 0.0)
        if r == 0:
            g = g + from_up
        q = g * gain_ref[...]
        mean_q = jnp.sum(q, axis=1, keepdims=True) * (1.0 / sz.c)
        mean_qx = jnp.sum(q * xhat, axis=1, keepdims=True) * (1.0 / sz.c)
        result = (q - mean_q - xhat * mean_qx) * inv
        part = result[REACH : REACH + sz.pr] + direct[r * sz.pr : (r + 1) * sz.pr]
        pieces = [result[:REACH], part, result[REACH + sz.pr :]]
        out_ref[0, r] = jnp.concatenate(pieces, axis=0).astype(bf16)


def norm_back_call(sz, base, count, height, x, gn, up, down, bg, gain):
    return pl.pallas_call(
        functools.partial(norm_back_kernel, sz),
        grid=(count,),
        out_shape=jax.ShapeDtypeStruct((count, 2, sz.ext, sz.cp), bf16),
        in_specs=[
            smem(),
            pl.BlockSpec((1, 2, sz.ext, sz.cp), lambda i: (i + base, 0, 0, 0)),
            pl.BlockSpec((1, 2, sz.ext, sz.cp), lambda i: (i, 0, 0, 0)),
            pl.BlockSpec((1, sz.ext, sz.cp), lambda i: (i, 0, 0)),
            pl.BlockSpec((1, sz.ext, sz.cp), lambda i: (i, 0, 0)),
            pl.BlockSpec((sz.pe, sz.cp), lambda i: (i + base, 0)),
            pl.BlockSpec((1, sz.cp), lambda i: (0, 0)),
        ],
        out_specs=pl.BlockSpec((1, 2, sz.ext, sz.cp), lambda i: (i, 0, 0, 0)),
        compiler_params=pltpu.CompilerParams(vmem_limit_bytes=14 * 1024 * 1024),
        cost_estimate=cost(2 * count),
        name="norm_back",
    )(height, x, gn, up, down, bg, gain)


def adam_kernel(sz, limit, pixels, members, stacks, place_ref, heights_ref, *refs):
    mine_ref, got_ref, small_mine_ref, small_got_ref = refs[:4]
    ins, small_ins, (norm_ref, mean_ref) = refs[4:10], refs[10:22], refs[22:24]
    outs, small_outs = refs[24:32], refs[32:44]
    factor_ref, small_ref, column_ref, cols_ref, gain_ref = refs[44:]
    at = Rows(sz)
    step = pl.program_id(0)
    core, member, stack = place_ref[0], place_ref[1], place_ref[2]
    half = sz.mh // 2
    each = sz.mc // members
    rows = sz.piece_rows(members, stacks)

    def wide(row, count, place):
        return jnp.concatenate([small_ref[row : row + count, :], column_ref[place : place + count, 0:1]], axis=1)

    def long(row, place):
        extra = small_ref[at.extra : at.extra + 1, place : place + at.spare]
        return jnp.concatenate([small_ref[row : row + 1, :], small_ref[row + 1 : row + 2, :], extra], axis=1)

    @pl.when(step == 0)
    def _():
        part = at.count // 2
        for which, ref in ((core, small_mine_ref), (1 - core, small_got_ref)):
            where = pl.ds(pl.multiple_of(which * part, part), part)
            values = ref[...].astype(f32)
            small_ref[where, :] = values[:part] + values[part:]
        extra = small_ref[at.extra : at.extra + 1, 0:128]
        column_ref[...] = jnp.broadcast_to(extra, (8, 128)).T
        total = jnp.zeros((8, half), f32)
        for ref in (mine_ref, got_ref):

            def body(i, acc):
                values = ref[i].astype(f32)
                values = values * values
                for j in range(0, rows, 8):
                    acc = acc + values[j : j + 8]
                return acc

            total = lax.fori_loop(0, 2 * members * stacks, body, total)
        count = jnp.sum(total)
        filter_grad = wide(0, 9, 0)
        gain_row = jnp.sum(small_ins[0][...] * filter_grad, axis=0, keepdims=True) / small_ins[6][0:1, :]
        gain_ref[...] = gain_row
        cols = small_ref[at.col_e : at.extra, :]
        for values in (
            filter_grad,
            wide(at.mixing, sz.k, at.x_mixing),
            gain_row,
            wide(at.outbias, 1, at.x_outbias),
            long(at.biasin, at.x_biasin),
            long(at.row_e, at.x_row_e),
            long(at.row_r, at.x_row_r),
            cols,
        ):
            count = count + jnp.sum(values * values)
        norm = jnp.sqrt(jnp.full((8, 128), count, f32))
        factor_ref[...] = jnp.minimum(1.0, limit / (norm + 1e-06))
        live = heights_ref[0]
        for i in range(1, heights_ref.shape[0]):
            live = live + heights_ref[i]
        loss = column_ref[at.x_loss : at.x_loss + 1, 0:1]
        mean = loss / (jnp.full((8, 128), pixels, f32) * live.astype(f32))
        norm_ref[0] = norm[0, 0]
        mean_ref[0] = mean[0, 0]
        cols_ref[...] = jnp.concatenate([cols, jnp.zeros((8 - 2 * at.spare, sz.mc), f32)], axis=0).T

    factor = factor_ref[0:1, 0:1]

    def adam(w, g, m, v, rate):
        g = factor * g
        m_new = BETA_ONE * m + (1.0 - BETA_ONE) * g
        v_new = BETA_TWO * v + (1.0 - BETA_TWO) * g * g
        v_hat = v_new * (1.0 / (1.0 - BETA_TWO**STEP))
        root = v_hat * lax.rsqrt(v_hat) + ADAM_EPS
        inverse = pl.reciprocal(root, approx=True)
        inverse = inverse * (2.0 - root * inverse)
        change = m_new * (rate / (1.0 - BETA_ONE**STEP)) * inverse
        return w * (1.0 - rate * DECAY_RATE) - change, m_new, v_new

    kinds = ((0, at.row_e, at.x_row_e, sz.c**-0.5), (1, at.row_r, at.x_row_r, sz.h**-0.5))

    @pl.when(step < sz.mc // ROWS)
    def _():
        first_core = core == 0
        for i in range(ROWS // rows):
            first = step * ROWS + i * rows
            t = member ^ (first // each)
            s = stack ^ ((first % each) // rows)
            where = pl.ds(pl.multiple_of(first, 8), rows)
            to = slice(i * rows, (i + 1) * rows)
            for kind, _, _, rate in kinds:
                slot = (t * stacks + s) * 2 + kind
                mine = mine_ref[slot].astype(f32)
                got = got_ref[slot].astype(f32)
                low = jnp.where(first_core, mine, got)
                high = jnp.where(first_core, got, mine)
                cols = cols_ref[where, kind * at.spare : (kind + 1) * at.spare]
                g = jnp.concatenate([low, high, cols], axis=1)
                w_ref, m_ref, v_ref = ins[3 * kind : 3 * kind + 3]
                w_out, m_out, v_out, c_out = outs[4 * kind : 4 * kind + 4]
                w, m, v = adam(w_ref[where, :], g, m_ref[where, :], v_ref[where, :], rate)
                w_out[to, :] = w
                m_out[to, :] = m
                v_out[to, :] = v
            if (i + 1) * rows % 16 == 0:
                both = slice((i + 1) * rows // 16 * 16 - max(16, rows * 2), (i + 1) * rows)
                for kind in range(2):
                    outs[4 * kind + 3][both, :] = outs[4 * kind][both, :].astype(bf16)

    @pl.when(step == sz.mc // ROWS)
    def _():
        last = slice(sz.mc, sz.c)
        for kind, row, place, rate in kinds:
            w_ref, m_ref, v_ref = ins[3 * kind : 3 * kind + 3]
            w_out, m_out, v_out, c_out = outs[4 * kind : 4 * kind + 4]
            w, m, v = adam(w_ref[last, :], long(row, place), m_ref[last, :], v_ref[last, :], rate)
            w_out[0:1, :] = w
            m_out[0:1, :] = m
            v_out[0:1, :] = v
            c_out[0:16, :] = jnp.broadcast_to(w, (16, sz.h)).astype(bf16)

    @pl.when(step == 0)
    def _():
        grads = (
            wide(0, 9, 0),
            wide(at.mixing, sz.k, at.x_mixing),
            jnp.concatenate([gain_ref[...], wide(at.outbias, 1, at.x_outbias)], axis=0),
            long(at.biasin, at.x_biasin),
        )
        for i, g in enumerate(grads):
            new = adam(small_ins[3 * i][...], g, small_ins[3 * i + 1][...], small_ins[3 * i + 2][...], SMALL_RATE)
            for ref, values in zip(small_outs[3 * i : 3 * i + 3], new):
                ref[...] = values.reshape(ref.shape)


ROWS = 80


def adam_call(sz, limit, pixels, members, stacks, place, heights, grads, weights, small_weights):
    shape = jax.ShapeDtypeStruct
    full = shape((sz.c, sz.h), f32)
    low = shape((sz.c, sz.h), bf16)
    outs = (shape((1,), f32),) * 2 + (full, full, full, low) * 2 + tuple(shape(v.shape if v.shape[0] > 1 else v.shape[1:], f32) for v in small_weights)
    block = pl.BlockSpec((ROWS, sz.h), lambda i: (i, 0))
    steps = sz.mc // ROWS + 1
    return pl.pallas_call(
        functools.partial(adam_kernel, sz, limit, pixels, members, stacks),
        grid=(steps,),
        out_shape=outs,
        in_specs=[smem()] * 2 + [vmem()] * (4 + 6) + [vmem()] * 12,
        out_specs=(smem(),) * 2 + (block,) * 8 + (vmem(),) * 12,
        scratch_shapes=[
            pltpu.VMEM((8, 128), f32),
            pltpu.VMEM((Rows(sz).count, sz.mc), f32),
            pltpu.VMEM((128, 8), f32),
            pltpu.VMEM((sz.mc, 8), f32),
            pltpu.VMEM((1, sz.c), f32),
        ],
        compiler_params=pltpu.CompilerParams(vmem_limit_bytes=24 * 1024 * 1024),
        cost_estimate=cost(16),
        name="adam",
    )(place, heights, *grads, *weights, *small_weights)


def exchange(pieces, axis, count, shifts):
    return [
        piece if s == 0 else lax.ppermute(piece, axis, [(i, i ^ s) for i in range(count)])
        for piece, s in zip(pieces, shifts)
    ]


def scatter_over(values, axis, count, size):
    me = lax.axis_index(axis)
    values = jnp.pad(values, ((0, 0), (0, count * size - values.shape[1]), (0, 0)))
    pieces = [lax.dynamic_slice_in_dim(values, (me ^ s) * size, size, axis=1) for s in range(count)]
    return exchange(pieces, axis, count, range(count))


def added(parts):
    return sum(part.astype(f32) for part in parts).astype(bf16)


def two_parts(values):
    coarse = lax.reduce_precision(values, exponent_bits=8, mantissa_bits=7)
    return coarse.astype(bf16), (values - coarse).astype(bf16)


def after_all(values, *others):
    return lax.optimization_barrier((values, others))[0]


def pad_to(values, shape):
    return jnp.pad(values, [(0, n - m) for n, m in zip(shape, values.shape)])


def on_device(
    fields,
    noise_fields,
    target_fields,
    band_heights,
    tap_offsets,
    expand_weight,
    expand_bias,
    reduce_weight,
    channel_vectors,
    disco_filter,
    noise_mixing,
    first_expand,
    second_expand,
    first_bias,
    second_bias,
    first_reduce,
    second_reduce,
    first_vectors,
    second_vectors,
    first_filter,
    second_filter,
    first_mixing,
    second_mixing,
):
    members = lax.axis_size("member")
    stacks = lax.axis_size("stack")
    lat_count = 2 * stacks
    lat = ("stack", "core")
    channels, hidden = expand_weight.shape
    lon = fields.shape[3]
    sz = Sizes(members, channels, hidden, noise_fields.shape[1], lon)
    me = lax.axis_index("member")
    core = lax.axis_index("core")
    band = lax.axis_index("stack") * 2 + core
    height = lax.dynamic_slice_in_dim(band_heights, band, 1)

    shifts = [0, members - 1, *range(1, members - 1)]
    pieces = split_call(sz, shifts, band_heights, band.reshape(1), me.reshape(1), fields, noise_fields)
    arrived = exchange(pieces, "member", members, shifts)
    upward = [(i, i + 1) for i in range(lat_count - 1)]
    downward = [(i + 1, i) for i in range(lat_count - 1)]

    def edges(rows):
        bottom = jnp.stack([x[1] for x in rows])
        top = jnp.stack([x[0] for x in rows])
        return lax.ppermute(bottom, lat, upward), lax.ppermute(top, lat, downward)

    truth = pad_to(target_fields, (channels, 2, lon + sz.pr - sz.q))
    truth = lax.dynamic_slice_in_dim(truth, me * sz.q, sz.pr, axis=2)
    truth = pad_to(jnp.transpose(truth, (1, 2, 0)), (2, sz.pr, sz.cp)).reshape(sz.pe, sz.cp)

    expand_low = pad_to(after_all(expand_weight, pieces).astype(bf16), (sz.cp, sz.hp))
    reduce_low = pad_to(reduce_weight.T.astype(bf16), (sz.cp, sz.hp))
    bias = pad_to(expand_bias[None], (1, sz.hp))
    gain = pad_to(channel_vectors[0:1], (1, sz.cp))
    outbias = pad_to(channel_vectors[1:2], (1, sz.cp))
    filt = jnp.transpose(pad_to(disco_filter, (16, sz.cp)).reshape(16, sz.ct, 128), (1, 0, 2))
    spot = channels - (sz.ct - 1) * 128
    coarse, fine = two_parts(noise_mixing)
    noisemix = jnp.zeros((256, sz.cp), bf16)
    noisemix = noisemix.at[spot : spot + sz.k, :channels].set(coarse)
    noisemix = noisemix.at[128 + spot : 128 + spot + sz.k, :channels].set(fine)

    weights = (expand_low, bias, reduce_low, gain, outbias, filt, noisemix)
    core_id = core.reshape(1)
    own_edges = edges(after_all(arrived[:1], expand_low))
    state = own_call(sz, height, tap_offsets, arrived[0][None], *own_edges, weights)
    others = after_all(arrived[1:], state)
    other_edges = edges(others)
    x = jnp.stack([arrived[0], *others])
    mine, other, bg, pg, normed, small = main_call(
        sz, height, core_id, tap_offsets, x, *other_edges, truth, weights, state
    )

    swap = [(0, 1), (1, 0)]
    pieces = share_call(me.reshape(1), mine, lax.ppermute(other, "core", swap), members)
    cut = members // 2

    def unmix_raw(base, count, pg, small):
        gn, gn_prev, gn_next, small = unmix_call(
            sz, base, count, height, tap_offsets, pg, x, normed, expand_low, filt, small
        )
        return (gn, gn_prev, gn_next), small

    def edges_back(raw):
        gn, gn_prev, gn_next = raw
        return gn, lax.ppermute(gn_next, lat, upward), lax.ppermute(gn_prev, lat, downward)

    def unmix(base, count, pg, small):
        raw, small = unmix_raw(base, count, pg, small)
        return edges_back(raw), small, raw[1]

    arriving = exchange(pieces, "member", members, range(members))
    near, small, done = unmix(0, cut, after_all(pg, pieces), small)
    arriving, done = after_all((arriving, done))
    arriving = scatter_over(added(arriving), "stack", stacks, sz.piece_rows(members, stacks))
    far_raw, small = unmix_raw(cut, members - cut, after_all(pg, done), small)

    def packed(main, small):
        return jnp.concatenate([main, *two_parts(small)], axis=0)

    def unpacked(messages):
        cut = messages[0].shape[0] - at.count
        half = at.count // 2
        parts = [m[cut:].astype(f32) for m in messages]
        return jnp.concatenate([m[:cut] for m in messages], axis=0), sum(p[:half] + p[half:] for p in parts)

    at = Rows(sz)
    arriving, far_raw, near, small = after_all((arriving, far_raw, near, small))
    small = small.reshape(2, -1, sz.mc)
    other_small = lax.dynamic_index_in_dim(small, 1 - core, 0, keepdims=False)
    small = lax.dynamic_index_in_dim(small, core, 0, keepdims=False) + lax.ppermute(other_small, "core", swap)
    near_grads = norm_back_call(sz, 0, cut, height, x, *near, bg, gain)
    small, part = after_all((small, added(arriving)))
    message = packed(part.reshape(-1, sz.mh // 2), small)
    gathered = exchange([message] * stacks, "stack", stacks, range(stacks))
    returned = exchange([near_grads[s] for s in range(cut)], "member", members, shifts[:cut])

    gathered, far_raw, returned = after_all((gathered, far_raw, returned))
    message = packed(*unpacked(gathered))
    gathered = exchange([message] * members, "member", members, range(members))
    far = edges_back(far_raw)

    far_grads = norm_back_call(sz, cut, members - cut, height, x, *far, bg, gain)
    far_pieces = [far_grads[s] for s in range(members - cut)]

    gathered, far_pieces = after_all((gathered, far_pieces))
    mine, small = unpacked(gathered)
    small = packed(mine[:0], small)
    got = lax.ppermute(mine, "core", swap)
    got_small = lax.ppermute(small, "core", swap)
    returned = returned + exchange(far_pieces, "member", members, shifts[cut:])
    pieces = [v.reshape(-1, sz.piece_rows(members, stacks), sz.mh // 2) for v in (mine, got)]

    limit = 0.02 * math.sqrt(hidden * channels * lat_count * 2 * lon / members)
    norm, mean, we, m_e, v_e, c_e, wr, m_r, v_r, c_r, *rest = adam_call(
        sz,
        limit,
        channels * lon,
        members,
        stacks,
        jnp.stack([core, me, lax.axis_index("stack")]),
        band_heights,
        (*pieces, small, got_small),
        (expand_weight, first_expand, second_expand, reduce_weight.T, first_reduce.T, second_reduce.T),
        (
            disco_filter,
            first_filter,
            second_filter,
            noise_mixing,
            first_mixing,
            second_mixing,
            channel_vectors,
            first_vectors,
            second_vectors,
            expand_bias[None],
            first_bias[None],
            second_bias[None],
        ),
    )
    input_gradient = join_call(sz, shifts, me.reshape(1), after_all(returned, norm))
    return (
        mean[0],
        input_gradient,
        norm[0],
        we,
        m_e,
        v_e,
        *rest[9:12],
        wr.T,
        m_r.T,
        v_r.T,
        *rest[6:9],
        *rest[0:3],
        *rest[3:6],
        c_e,
        c_r.T,
    )


def solution(mesh):
    members = mesh.shape["member"]
    lat = mesh.shape["lat"]
    split = Mesh(mesh.devices.reshape(members, lat // 2, 2), ("member", "stack", "core"))
    rows = ("stack", "core")
    whole = [P()] * 18
    in_specs = (
        P("member", None, rows, None),
        P("member", None, rows, None),
        P(None, rows, None),
        P(),
        P(None, rows),
        *whole,
    )
    out_specs = (P(), P("member", None, rows, None)) + (P(),) * 21
    return jax.shard_map(on_device, mesh=split, in_specs=in_specs, out_specs=out_specs, check_vma=False)
```
